512 devices in a mesh: gz: 8 (over z), xy: 64 (over y, x, core).
Axes of the slice: x: 4, y: 8, z: 8, core: 2. Of those that a mesh axis runs over, the one named last changes fastest.
Arguments:
- right_side: float32 [256, 512, 128], P('gz', 'xy'), may hold values from -12 to 12
- labels: int32 [256, 512, 128], P('gz', 'xy'), may hold values from 0 to 1, as said below
Outputs:
- pressure: float32 [256, 512, 128], P('gz', 'xy')
- remain: float32 [256, 512, 128], P('gz', 'xy')
The draws below stay inside these ranges and needn't reach their ends.
Inputs may be any that keep to these rules, and one draw needn't show every extreme that they name: `labels`: 1 marks a gas cell inside a bubble, 0 a liquid cell.
All inputs are finite; a program needn't handle non-finite values.
Results may differ from the reference program's by a relative error of at most 0.0003.
Values sent between devices are 32-bit elements; how exact they have to be, the bound alone decides.
No kernel may reach another device: no remote copies, remote signals or barrier semaphores. Data moves between devices by JAX's collectives and lax.ppermute only.
A program may use at most 64 MiB of HBM per device.

```python
import jax
import jax.numpy as jnp
from jax import lax

LEVELS = 3
SWEEPS = 2
COARSE_SWEEPS = 12
NZ = 256
NY = 512
NX = 128


def draw_right_side(key, part):
    key = jax.random.fold_in(key, 11)
    rough = jax.random.normal(key, (NZ, NY, NX), jnp.float32)
    return jnp.clip(3.0 * rough, -12.0, 12.0)


def draw_labels(key, part):
    key = jax.random.fold_in(key, 5)
    first, second, third, fourth = jax.random.split(key, 4)
    blocks_z, blocks_y, blocks_x = (NZ // 16, NY // 16, NX // 16)
    table_shape = (blocks_z, blocks_y, blocks_x)
    centre_z = jnp.pad(jax.random.randint(first, table_shape, 0, 16), 1)
    centre_y = jnp.pad(jax.random.randint(second, table_shape, 0, 16), 1)
    centre_x = jnp.pad(jax.random.randint(third, table_shape, 0, 16), 1)
    radius = jnp.pad(jax.random.randint(fourth, table_shape, 3, 11), 1)
    cell_shape = (1, 16, 1, 16, 1, 16)
    offset_z = lax.broadcasted_iota(jnp.int32, cell_shape, 1)
    offset_y = lax.broadcasted_iota(jnp.int32, cell_shape, 3)
    offset_x = lax.broadcasted_iota(jnp.int32, cell_shape, 5)
    gas = jnp.zeros((blocks_z, 16, blocks_y, 16, blocks_x, 16), jnp.int32)
    for shift_z in (-1, 0, 1):
        for shift_y in (-1, 0, 1):
            for shift_x in (-1, 0, 1):
                window = (slice(1 + shift_z, 1 + shift_z + blocks_z), slice(1 + shift_y, 1 + shift_y + blocks_y), slice(1 + shift_x, 1 + shift_x + blocks_x))
                spot_z = (centre_z[window] + 16 * shift_z)[:, None, :, None, :, None]
                spot_y = (centre_y[window] + 16 * shift_y)[:, None, :, None, :, None]
                spot_x = (centre_x[window] + 16 * shift_x)[:, None, :, None, :, None]
                reach = radius[window][:, None, :, None, :, None]
                distance = (offset_z - spot_z) ** 2 + (offset_y - spot_y) ** 2 + (offset_x - spot_x) ** 2
                inside = (distance < reach * reach).astype(jnp.int32)
                gas = jnp.maximum(gas, inside)
    return gas.reshape(NZ, NY, NX)


def setup_inputs(seed: int = 0) -> dict:
    keys = jax.random.split(jax.random.key(seed), 3)
    right_side = draw_right_side(jax.random.fold_in(keys[2], 71), 0)
    labels = draw_labels(jax.random.fold_in(keys[2], 71), 0)
    return dict(right_side=right_side, labels=labels)


gas_density = 0.001


def density_of(labels):
    return jnp.where(labels == 1, gas_density, 1.0).astype(jnp.float32)


def coarsen(values):
    extent_z, extent_y, extent_x = values.shape
    blocks = values.reshape(extent_z // 2, 2, extent_y // 2, 2, extent_x // 2, 2)
    return jnp.mean(blocks, axis=(1, 3, 5))


def prolong(values):
    extent_z, extent_y, extent_x = values.shape
    spread = jnp.broadcast_to(values[:, None, :, None, :, None], (extent_z, 2, extent_y, 2, extent_x, 2))
    return spread.reshape(2 * extent_z, 2 * extent_y, 2 * extent_x)


def coefficients(density, rimmed):
    lower_z = 2.0 / (density + rimmed[:-2, 1:-1, 1:-1])
    upper_z = 2.0 / (density + rimmed[2:, 1:-1, 1:-1])
    lower_y = 2.0 / (density + rimmed[1:-1, :-2, 1:-1])
    upper_y = 2.0 / (density + rimmed[1:-1, 2:, 1:-1])
    lower_x = 2.0 / (density + rimmed[1:-1, 1:-1, :-2])
    upper_x = 2.0 / (density + rimmed[1:-1, 1:-1, 2:])
    diagonal = lower_z + upper_z + lower_y + upper_y + lower_x + upper_x
    return (lower_z, upper_z, lower_y, upper_y, lower_x, upper_x), diagonal


def neighbours(faces, rimmed):
    lower_z, upper_z, lower_y, upper_y, lower_x, upper_x = faces
    return (lower_z * rimmed[:-2, 1:-1, 1:-1] + upper_z * rimmed[2:, 1:-1, 1:-1]
            + lower_y * rimmed[1:-1, :-2, 1:-1] + upper_y * rimmed[1:-1, 2:, 1:-1]
            + lower_x * rimmed[1:-1, 1:-1, :-2] + upper_x * rimmed[1:-1, 1:-1, 2:])


def checker(shape):
    summed = (lax.broadcasted_iota(jnp.int32, shape, 0) + lax.broadcasted_iota(jnp.int32, shape, 1)
              + lax.broadcasted_iota(jnp.int32, shape, 2))
    return summed % 2


def plain_rims(values):
    return jnp.pad(values, 1)


def smooth(pressure, source, faces, diagonal, factor, colours, rimmer):
    for colour in (0, 1):
        gathered = neighbours(faces, rimmer(pressure))
        updated = (factor * source + gathered) / diagonal
        pressure = jnp.where(colours == colour, updated, pressure)
    return pressure


def residual_of(pressure, source, faces, diagonal, inverse, rimmer):
    return source - (diagonal * pressure - neighbours(faces, rimmer(pressure))) * inverse


def reference(right_side, labels):
    density = density_of(labels)
    saved = []
    source = right_side
    for level_index in range(LEVELS):
        faces, diagonal = coefficients(density, jnp.pad(density, 1))
        colours = checker(density.shape)
        factor = 4.0 ** level_index
        pressure = jnp.zeros_like(source)
        for repeat in range(SWEEPS):
            pressure = smooth(pressure, source, faces, diagonal, factor, colours, plain_rims)
        saved.append((faces, diagonal, colours, factor, pressure, source))
        leftover = residual_of(pressure, source, faces, diagonal, 1.0 / factor, plain_rims)
        source = coarsen(leftover)
        density = coarsen(density)
    faces, diagonal = coefficients(density, jnp.pad(density, 1))
    colours = checker(density.shape)
    factor = 4.0 ** LEVELS

    def coarse_turn(counter, current):
        return smooth(current, source, faces, diagonal, factor, colours, plain_rims)

    pressure = lax.fori_loop(0, COARSE_SWEEPS, coarse_turn, jnp.zeros_like(source))
    for level_index in reversed(range(LEVELS)):
        faces, diagonal, colours, factor, below, source = saved[level_index]
        pressure = below + prolong(pressure)
        for repeat in range(SWEEPS):
            pressure = smooth(pressure, source, faces, diagonal, factor, colours, plain_rims)
    faces, diagonal, colours, factor, below, source = saved[0]
    remain = residual_of(pressure, right_side, faces, diagonal, 1.0, plain_rims)
    return pressure, remain
```

```python
from functools import partial

import jax
import jax.numpy as jnp
from jax import lax
from jax.experimental import pallas as pl
from jax.experimental.pallas import tpu as pltpu
from jax.sharding import PartitionSpec as P

gas_density = 0.001
least = 1e-4
F32 = jnp.float32


def dot(a, b):
    return lax.dot_general(
        a, b, (((1,), (0,)), ((), ())), precision=lax.Precision.HIGHEST, preferred_element_type=F32
    )


def halving(offset, weight, width=128):
    row = lax.broadcasted_iota(jnp.int32, (128, 128), 0)
    column = lax.broadcasted_iota(jnp.int32, (128, 128), 1)
    return jnp.where((row // 2 + offset == column) & (row < width), weight, 0.0).astype(F32)


def doubling(width):
    row = lax.broadcasted_iota(jnp.int32, (128, 128), 0)
    column = lax.broadcasted_iota(jnp.int32, (128, 128), 1)
    return jnp.where((column // 2 == row) & (row < width), 1.0, 0.0).astype(F32)


def iota(shape, axis):
    return lax.broadcasted_iota(jnp.int32, shape, axis)


def low(a, axis):
    return pltpu.roll(a, 1, axis)


def high(a, axis):
    return pltpu.roll(a, a.shape[axis] - 1, axis)


class Level:
    def __init__(self, rows, shift, depth, full, by, bz, bx, inv, diag, source, value):
        self.rows, self.shift, self.depth, self.full = rows, shift, depth, full
        self.by, self.bz, self.bx, self.inv, self.diag = by, bz, bx, inv, diag
        self.source, self.value = source, value

    def coefficients(self, density, lo, hi, block):
        n = (hi - lo) // block
        assert n * block == hi - lo

        def step(i, _):
            y = lo + i * block
            d = density[pl.ds(y, block)]
            lower_y = 2.0 / jnp.maximum(d + density[pl.ds(y - 1, block)], least)
            upper_y = 2.0 / jnp.maximum(d + density[pl.ds(y + 1, block)], least)
            lower_z = 2.0 / jnp.maximum(d + low(d, 1), least)
            upper_z = high(lower_z, 1)
            side = low(d, 2)
            if self.full:
                lane = iota(d.shape, 2)
                side = jnp.where(lane == 0, 0.0, side)
            lower_x = 2.0 / jnp.maximum(d + side, least)
            upper_x = high(lower_x, 2)
            if self.full:
                upper_x = jnp.where(lane == 127, 2.0 / jnp.maximum(d, least), upper_x)
            total = lower_z + upper_z + lower_y + upper_y + lower_x + upper_x
            if self.full:
                lower_x = jnp.where(lane == 0, 0.0, lower_x)
            self.by[pl.ds(y, block)] = lower_y
            self.by[pl.ds(y + 1, block)] = upper_y
            self.bz[pl.ds(y, block)] = lower_z
            self.bx[pl.ds(y, block)] = lower_x
            self.inv[pl.ds(y, block)] = jnp.where(d > 0.0, 1.0 / total, 0.0)
            if self.diag is not None:
                self.diag[pl.ds(y, block)] = total
            return 0

        lax.fori_loop(0, n, step, 0)

    def gathered(self, y, block):
        v = self.value[pl.ds(y, block)]
        bz, bx = self.bz[pl.ds(y, block)], self.bx[pl.ds(y, block)]
        total = self.by[pl.ds(y, block)] * self.value[pl.ds(y - 1, block)]
        total += self.by[pl.ds(y + 1, block)] * self.value[pl.ds(y + 1, block)]
        total += bz * low(v, 1) + high(bz * v, 1)
        total += bx * low(v, 2) + high(bx * v, 2)
        return v, total

    def parity(self, block):
        shape = (block, self.depth, 128)
        return (iota(shape, 0) + iota(shape, 1) + iota(shape, 2) + self.shift) & 1

    def first(self, factor, lo, hi, block):
        parity = self.parity(block)
        n = (hi - lo) // block
        assert n * block == hi - lo

        def step(i, _):
            y = lo + i * block
            new = factor * self.source[pl.ds(y, block)] * self.inv[pl.ds(y, block)]
            self.value[pl.ds(y, block)] = jnp.where(parity == (y & 1), new, 0.0)
            return 0

        lax.fori_loop(0, n, step, 0)

    def half(self, colour, factor, lo, hi, block):
        parity = self.parity(block)
        n = (hi - lo) // block
        assert n * block == hi - lo

        def step(i, _):
            y = lo + i * block
            v, total = self.gathered(y, block)
            new = (factor * self.source[pl.ds(y, block)] + total) * self.inv[pl.ds(y, block)]
            self.value[pl.ds(y, block)] = jnp.where(parity == ((y + colour) & 1), new, v)
            return 0

        lax.fori_loop(0, n, step, 0)

    def residual(self, factor, y, block):
        v, total = self.gathered(y, block)
        return self.source[pl.ds(y, block)] - (self.diag[pl.ds(y, block)] * v - total) * (1.0 / factor)


def finest_down(s_ref, d_ref, before_ref, after_ref, message_ref, low_ref, high_ref,
                by, bz, bx, inv, diag, source, value, density, plane):
    zeros = jnp.zeros((5, 8, 128), F32)
    for ref in (source, density):
        for rows in (pl.ds(0, 5), pl.ds(13, 5)):
            ref[rows, 0:8] = zeros
            ref[rows, 56:64] = zeros
    source[0:5, 8:56] = before_ref[0:5]
    source[13:18, 8:56] = after_ref[0:5]
    density[0:5, 8:56] = before_ref[5:10]
    density[13:18, 8:56] = after_ref[5:10]
    source[5:13] = s_ref[...]
    density[5:13] = d_ref[...]
    value[0] = jnp.zeros((64, 128), F32)
    value[17] = jnp.zeros((64, 128), F32)
    level = Level(18, 5, 64, True, by, bz, bx, inv, diag, source, value)
    level.coefficients(density, 1, 17, 1)
    level.first(1.0, 1, 17, 1)
    level.half(1, 1.0, 2, 16, 1)
    level.half(0, 1.0, 3, 15, 1)
    level.half(1, 1.0, 4, 14, 1)
    to_low, to_high = halving(0, 0.125), halving(64, 0.125)
    for row in range(6):
        y = 3 + 2 * row
        plane[...] = density[y, 16:48] + density[y + 1, 16:48]
        pooled = plane[pl.ds(0, 16, stride=2)] + plane[pl.ds(1, 16, stride=2)]
        out = dot(pooled, to_high)
        if 0 < row < 5:
            left = level.residual(1.0, y, 2)
            plane[...] = left[0, 16:48] + left[1, 16:48]
            pooled = plane[pl.ds(0, 16, stride=2)] + plane[pl.ds(1, 16, stride=2)]
            out = out + dot(pooled, to_low)
        message_ref[row] = out
    low_ref[...] = value[5:10, 8:56]
    high_ref[...] = value[8:13, 8:56]


def middle_down(window_ref, far_before_ref, far_after_ref, coarse_ref, halo_ref,
                by, bz, bx, inv, source, value,
                diag, density, plane, by2, bz2, bx2, inv2, diag2, source2, value2, density2):
    lane = iota((1, 48, 128), 2)

    zeros = jnp.zeros((8, 128), F32)
    for i in range(9):
        for row, ref in ((i, far_before_ref), (21 + i, far_after_ref)):
            block = ref[i]
            source[row, 8:40] = block
            density[row, 8:40] = jnp.where(lane[0, :32] < 64, pltpu.roll(block, 64, 1), 0.0)
            for rows in (pl.ds(0, 8), pl.ds(40, 8)):
                source[row, rows] = zeros
                density[row, rows] = zeros
    for i in range(12):
        block = window_ref[i]
        source[9 + i] = block
        density[9 + i] = jnp.where(lane[0] < 64, pltpu.roll(block, 64, 1), 0.0)
    value[0] = jnp.zeros((48, 128), F32)
    value[29] = jnp.zeros((48, 128), F32)
    level = Level(30, 13, 48, False, by, bz, bx, inv, diag, source, value)
    level.coefficients(density, 1, 29, 1)
    level.first(4.0, 1, 29, 1)
    level.half(1, 4.0, 2, 28, 1)
    level.half(0, 4.0, 3, 27, 1)
    level.half(1, 4.0, 4, 26, 1)

    pool = halving(0, 0.125, 64)
    for row in range(12):
        y = 3 + 2 * row
        plane[...] = density[y] + density[y + 1]
        density2[row] = dot(plane[pl.ds(0, 24, stride=2)] + plane[pl.ds(1, 24, stride=2)], pool)
        if 0 < row < 11:
            left = level.residual(4.0, y, 2)
            plane[...] = left[0] + left[1]
            source2[row] = dot(plane[pl.ds(0, 24, stride=2)] + plane[pl.ds(1, 24, stride=2)], pool)
    value2[0] = jnp.zeros((24, 128), F32)
    value2[11] = jnp.zeros((24, 128), F32)
    below = Level(12, 5, 24, False, by2, bz2, bx2, inv2, diag2, source2, value2)
    below.coefficients(density2, 1, 11, 2)
    below.first(16.0, 1, 11, 2)
    below.half(1, 16.0, 2, 10, 2)
    below.half(0, 16.0, 3, 9, 2)
    below.half(1, 16.0, 4, 8, 2)
    left = below.residual(16.0, 5, 2)
    pool = halving(0, 0.125, 32)
    plane[0:24] = left[0] + left[1]
    upper = plane[pl.ds(8, 4, stride=2)] + plane[pl.ds(9, 4, stride=2)]
    plane[0:24] = density2[5] + density2[6]
    lower = plane[pl.ds(8, 4, stride=2)] + plane[pl.ds(9, 4, stride=2)]
    pooled = dot(jnp.concatenate([upper, lower], axis=0), pool)
    total = pooled[0:1]
    for i in range(1, 8):
        total = total + pltpu.roll(pooled[i : i + 1], 16 * i, 1)
    coarse_ref[...] = total
    for i in range(2):
        halo_ref[i] = (
            source2[5 + i, 8:16]
            + pltpu.roll(value2[5 + i, 8:16], 32, 1)
            + pltpu.roll(density2[5 + i, 8:16], 64, 1)
        )


def coarsest(planes, gathered_ref, density, source, by, bz, bx, inv, value):
    devices = gathered_ref.shape[0] // (planes // 4)
    shape = (8, 8, 128)
    row, lane = iota((8, 128), 0), iota((8, 128), 1)
    edge = jnp.zeros((8, 128), F32)
    for ref in (density, value):
        ref[0] = edge
        ref[planes + 1] = edge

    def spread(g, _):
        blocks = [gathered_ref[pl.ds(pl.multiple_of(g * devices + 8 * h, 8), 8)] for h in range(devices // 8)]
        for part, ref in enumerate((source, density)):
            for z in range(4):
                out = jnp.zeros((8, 128), F32)
                for h, block in enumerate(blocks):
                    moved = pltpu.roll(block, (16 * (h - z) - 64 * part) % 128, 1)
                    out = jnp.where(lane // 16 == h, moved, out)
                ref[1 + 4 * g + z] = out
        return 0

    lax.fori_loop(0, planes // 4, spread, 0)
    row, lane = iota(shape, 1), iota(shape, 2)
    first_y = (row == 0) & (lane < 16)
    last_y = (row == 7) & (lane >= 112)
    first_x = lane % 16 == 0
    last_x = lane % 16 == 15

    def low_y(a):
        turned = low(a, 1)
        return jnp.where(row == 0, pltpu.roll(turned, 16, 2), turned)

    def high_y(a):
        turned = high(a, 1)
        return jnp.where(row == 7, pltpu.roll(turned, 112, 2), turned)

    for start in range(1, planes + 1, 8):
        d = density[start : start + 8]
        lower_z = 2.0 / jnp.maximum(d + density[start - 1 : start + 7], least)
        upper_z = 2.0 / jnp.maximum(d + density[start + 1 : start + 9], least)
        lower_y = 2.0 / jnp.maximum(d + jnp.where(first_y, 0.0, low_y(d)), least)
        upper_y = 2.0 / jnp.maximum(d + jnp.where(last_y, 0.0, high_y(d)), least)
        lower_x = 2.0 / jnp.maximum(d + jnp.where(first_x, 0.0, low(d, 2)), least)
        upper_x = 2.0 / jnp.maximum(d + jnp.where(last_x, 0.0, high(d, 2)), least)
        total = lower_z + upper_z + lower_y + upper_y + lower_x + upper_x
        inverse = jnp.where(d > 0.0, 1.0 / total, 0.0)
        inv[start : start + 8] = inverse
        bz[start : start + 8] = lower_z
        bz[start + 1 : start + 9] = upper_z
        by[start : start + 8] = jnp.where(first_y, 0.0, lower_y)
        bx[start : start + 8] = jnp.where(first_x, 0.0, lower_x)
        source[start : start + 8] = 64.0 * source[start : start + 8]
        value[start : start + 8] = jnp.zeros(shape, F32)
    parity = (iota(shape, 0) + row + lane) & 1

    def sweep(_, carry):
        for colour in (0, 1):
            for start in range(1, planes + 1, 8):
                v = value[start : start + 8]
                cy, cx = by[start : start + 8], bx[start : start + 8]
                total = bz[start : start + 8] * value[start - 1 : start + 7]
                total += bz[start + 1 : start + 9] * value[start + 1 : start + 9]
                total += cy * low_y(v) + high_y(cy * v)
                total += cx * low(v, 2) + high(cx * v, 2)
                new = (source[start : start + 8] + total) * inv[start : start + 8]
                value[start : start + 8] = jnp.where(parity == colour, new, v)
        return carry

    lax.fori_loop(0, 12, sweep, 0)


def way_up(planes, place_ref, gathered_ref, halo_ref,
           by1, bz1, bx1, inv1, source1, below1,
           by0, bz0, bx0, inv0, diag0, source0, below0, before_ref, after_ref,
           pressure_ref, remain_ref,
           density3, source3, by3, bz3, bx3, inv3, value3,
           wide, density2, source2, by2, bz2, bx2, inv2, value2, value1, value0, plane):
    devices = gathered_ref.shape[0] // (planes // 4)
    coarsest(planes, gathered_ref, density3, source3, by3, bz3, bx3, inv3, value3)
    at_z, at_y = place_ref[0], place_ref[1]

    lane = iota((24, 128), 1)
    def halo(i):
        y = 2 * at_y + i - 8
        return jnp.where((y >= 0) & (y < 2 * devices), halo_ref[i], 0.0)

    for i in range(18):
        block = halo(i)
        source2[i] = jnp.where(lane < 32, block, 0.0)
        density2[i] = jnp.where(lane < 32, pltpu.roll(block, 64, 1), 0.0)
    level = Level(18, 8, 24, False, by2, bz2, bx2, inv2, None, source2, value2)
    level.coefficients(density2, 1, 17, 2)
    wide[0:4] = jnp.zeros((4, 8, 128), F32)
    wide[planes + 4 : planes + 8] = jnp.zeros((4, 8, 128), F32)
    wide[4 : planes + 4] = value3[1 : planes + 1]
    near = wide[pl.ds(4 * at_z, 12)]
    row, lane3 = iota((8, 128), 0), iota((8, 128), 1)
    double = doubling(16)
    for i in range(9):
        y = at_y + i - 4
        inside = (y >= 0) & (y < devices)
        y = jnp.clip(y, 0, devices - 1)
        picked = jnp.sum(jnp.where(row == y % 8, near, 0.0), axis=1)
        picked = pltpu.roll(picked, (128 - 16 * (y // 8)) % 128, 1)
        picked = jnp.where(inside & (iota((12, 128), 1) < 16), picked, 0.0)
        picked = dot(jnp.concatenate([picked, jnp.zeros((4, 128), F32)], axis=0), double)[0:12]
        plane[pl.ds(0, 12, stride=2)] = picked
        plane[pl.ds(1, 12, stride=2)] = picked
        for j in range(2):
            below = pltpu.roll(halo(2 * i + j), 96, 1)
            value2[2 * i + j] = jnp.where(lane < 32, below, 0.0) + plane[0:24]
    level.half(0, 16.0, 1, 17, 2)
    level.half(1, 16.0, 2, 16, 2)
    level.half(0, 16.0, 3, 15, 2)
    level.half(1, 16.0, 4, 14, 2)

    level = Level(30, 13, 48, False, by1, bz1, bx1, inv1, None, source1, value1)
    double = doubling(32)
    for i in range(10):
        picked = dot(value2[4 + i], double)
        plane[pl.ds(0, 24, stride=2)] = picked
        plane[pl.ds(1, 24, stride=2)] = picked
        for j in range(2):
            value1[5 + 2 * i + j] = below1[5 + 2 * i + j] + plane[0:48]
    level.half(0, 4.0, 7, 23, 2)
    level.half(1, 4.0, 8, 22, 2)
    level.half(0, 4.0, 9, 21, 2)
    level.half(1, 4.0, 10, 20, 2)

    level = Level(18, 5, 64, True, by0, bz0, bx0, inv0, diag0, source0, value0)
    double = doubling(64)
    for i in range(10):
        picked = dot(value1[10 + i, 8:40], double)
        plane[pl.ds(0, 32, stride=2)] = picked
        plane[pl.ds(1, 32, stride=2)] = picked
        for j in range(2):
            y = 2 * i + j - 1
            if 0 <= y < 5:
                value0[y] = plane[...]
                value0[y, 8:56] = value0[y, 8:56] + before_ref[y]
            elif 5 <= y < 13:
                value0[y] = below0[y] + plane[...]
            elif 13 <= y < 18:
                value0[y] = plane[...]
                value0[y, 8:56] = value0[y, 8:56] + after_ref[y - 13]
    level.half(0, 1.0, 1, 17, 1)
    level.half(1, 1.0, 2, 16, 1)
    level.half(0, 1.0, 3, 15, 1)
    level.half(1, 1.0, 4, 14, 1)
    for y in range(8):
        pressure_ref[y] = value0[5 + y, 16:48]
        remain_ref[y] = level.residual(1.0, 5 + y, 1)[0, 16:48]


def pair(array_up, array_down, axis, distance, ring=False):
    devices = lax.axis_size(axis)
    up = [(i, (i + distance) % devices) for i in range(devices if ring else devices - distance)]
    down = [(j, i) for i, j in up]
    return lax.ppermute(array_up, axis, up), lax.ppermute(array_down, axis, down)


def shape(*sizes):
    return jax.ShapeDtypeStruct(sizes, F32)


def vmem(*sizes):
    return pltpu.VMEM(sizes, F32)


def params():
    return pltpu.CompilerParams(vmem_limit_bytes=48 * 1024 * 1024)


def body(right_side, labels):
    gz, xy = lax.axis_size("gz"), lax.axis_size("xy")
    density = jnp.where(labels == 1, gas_density, 1.0).astype(F32)
    before, after = pair(
        jnp.concatenate([right_side[-8:], density[-9:]], axis=0),
        jnp.concatenate([right_side[:8], density[:9]], axis=0),
        "gz",
        1,
    )
    zeros = jnp.zeros((8, 8, 128), F32)
    wide_source = jnp.concatenate([zeros, before[:8], right_side, after[:8], zeros], axis=0)
    wide_density = jnp.concatenate([zeros[:7], before[8:], density, after[8:], zeros[:7]], axis=0)
    wide_source = jnp.swapaxes(wide_source, 0, 1)
    wide_density = jnp.swapaxes(wide_density, 0, 1)
    before, after = pair(
        jnp.concatenate([wide_source[3:, 8:56], wide_density[3:, 8:56]], axis=0),
        jnp.concatenate([wide_source[:5, 8:56], wide_density[:5, 8:56]], axis=0),
        "xy",
        1,
    )
    window0 = [shape(18, 64, 128)] * 7
    message, first_rows, last_rows, *level0 = pl.pallas_call(
        finest_down,
        out_shape=[shape(6, 16, 128), shape(5, 48, 128), shape(5, 48, 128)] + window0,
        scratch_shapes=[vmem(18, 64, 128), vmem(32, 128)],
        compiler_params=params(),
    )(wide_source, wide_density, before, after)

    before, after = pair(message, message, "gz", 1)
    window = jnp.concatenate([before, message, after], axis=1)
    before, after = pair(
        jnp.concatenate([window, last_rows], axis=0),
        jnp.concatenate([window, first_rows], axis=0),
        "xy",
        1,
    )
    value_before, value_after = before[6:], after[6:]
    before, after = before[:6], after[:6]
    near = jnp.concatenate([before[1:5], window[1:5], after[1:5]], axis=0)
    far_before, far_after = pair(
        jnp.concatenate([before[0:5], window[1:5]], axis=0)[:, 8:40],
        jnp.concatenate([window[1:5], after[1:6]], axis=0)[:, 8:40],
        "xy",
        2,
    )
    window1 = [shape(30, 48, 128)] * 6
    window2 = [vmem(12, 24, 128)] * 8
    coarse, halo, *level1 = pl.pallas_call(
        middle_down,
        out_shape=[shape(1, 128), shape(2, 8, 128)] + window1,
        scratch_shapes=[vmem(30, 48, 128), vmem(30, 48, 128), vmem(48, 128)] + window2,
        compiler_params=params(),
    )(near, far_before, far_after)

    everywhere = lax.all_to_all(
        jnp.broadcast_to(coarse[None], (gz * xy, 1, 128)), ("gz", "xy"), 0, 0, tiled=True
    ).reshape(gz * xy, 128)
    before, after = pair(halo, halo, "gz", 1)
    halo = jnp.concatenate([before, halo, after], axis=1)
    before, after = pair(halo, halo, "xy", 1, ring=True)
    halo = jnp.concatenate([before, halo, after], axis=0)
    before, after = pair(halo, halo, "xy", 3, ring=True)
    halo = jnp.concatenate([before, halo, after], axis=0)
    place = jnp.stack([lax.axis_index("gz"), lax.axis_index("xy")]).astype(jnp.int32)
    planes = 4 * gz
    pressure, remain = pl.pallas_call(
        partial(way_up, planes),
        out_shape=[shape(8, 32, 128)] * 2,
        in_specs=[pl.BlockSpec(memory_space=pltpu.SMEM)] + [pl.BlockSpec(memory_space=pltpu.VMEM)] * 17,
        scratch_shapes=[vmem(planes + 2, 8, 128)] * 7
        + [vmem(planes + 8, 8, 128)]
        + [vmem(18, 24, 128)] * 7
        + [vmem(30, 48, 128), vmem(18, 64, 128), vmem(64, 128)],
        compiler_params=params(),
    )(place, everywhere, halo, *level1, *level0, value_before, value_after)
    return jnp.swapaxes(pressure, 0, 1), jnp.swapaxes(remain, 0, 1)


def solution(mesh):
    return jax.shard_map(
        body,
        mesh=mesh,
        in_specs=(P("gz", "xy", None), P("gz", "xy", None)),
        out_specs=(P("gz", "xy", None), P("gz", "xy", None)),
        check_vma=False,
    )
```

```python
from functools import partial

import jax
import jax.numpy as jnp
from jax import lax
from jax.experimental import pallas as pl
from jax.experimental.pallas import tpu as pltpu
from jax.sharding import PartitionSpec as P

gas_density = 0.001
least = 1e-4
F32 = jnp.float32
GROUP = 4


def dot(a, b):
    return lax.dot_general(
        a, b, (((1,), (0,)), ((), ())), precision=lax.Precision.HIGHEST, preferred_element_type=F32
    )


def halving(offset, weight, width=128):
    row = lax.broadcasted_iota(jnp.int32, (128, 128), 0)
    column = lax.broadcasted_iota(jnp.int32, (128, 128), 1)
    return jnp.where((row // 2 + offset == column) & (row < width), weight, 0.0).astype(F32)


def doubling(width):
    row = lax.broadcasted_iota(jnp.int32, (128, 128), 0)
    column = lax.broadcasted_iota(jnp.int32, (128, 128), 1)
    return jnp.where((column // 2 == row) & (row < width), 1.0, 0.0).astype(F32)


def iota(shape, axis):
    return lax.broadcasted_iota(jnp.int32, shape, axis)


def low(a, axis):
    return pltpu.roll(a, 1, axis)


def high(a, axis):
    return pltpu.roll(a, a.shape[axis] - 1, axis)


class Level:
    def __init__(self, rows, shift, depth, full, by, bz, bx, inv, diag, source, value):
        self.rows, self.shift, self.depth, self.full = rows, shift, depth, full
        self.by, self.bz, self.bx, self.inv, self.diag = by, bz, bx, inv, diag
        self.source, self.value = source, value

    def coefficients(self, density, lo, hi, block):
        n = (hi - lo) // block
        assert n * block == hi - lo

        def step(i, _):
            y = lo + i * block
            d = density[pl.ds(y, block)]
            lower_y = 2.0 / jnp.maximum(d + density[pl.ds(y - 1, block)], least)
            upper_y = 2.0 / jnp.maximum(d + density[pl.ds(y + 1, block)], least)
            lower_z = 2.0 / jnp.maximum(d + low(d, 1), least)
            upper_z = high(lower_z, 1)
            side = low(d, 2)
            if self.full:
                lane = iota(d.shape, 2)
                side = jnp.where(lane == 0, 0.0, side)
            lower_x = 2.0 / jnp.maximum(d + side, least)
            upper_x = high(lower_x, 2)
            if self.full:
                upper_x = jnp.where(lane == 127, 2.0 / jnp.maximum(d, least), upper_x)
            total = lower_z + upper_z + lower_y + upper_y + lower_x + upper_x
            if self.full:
                lower_x = jnp.where(lane == 0, 0.0, lower_x)
            self.by[pl.ds(y, block)] = lower_y
            self.by[pl.ds(y + 1, block)] = upper_y
            self.bz[pl.ds(y, block)] = lower_z
            self.bx[pl.ds(y, block)] = lower_x
            self.inv[pl.ds(y, block)] = jnp.where(d > 0.0, 1.0 / total, 0.0)
            if self.diag is not None:
                self.diag[pl.ds(y, block)] = total
            return 0

        lax.fori_loop(0, n, step, 0)

    def gathered(self, y, block):
        v = self.value[pl.ds(y, block)]
        bz, bx = self.bz[pl.ds(y, block)], self.bx[pl.ds(y, block)]
        total = self.by[pl.ds(y, block)] * self.value[pl.ds(y - 1, block)]
        total += self.by[pl.ds(y + 1, block)] * self.value[pl.ds(y + 1, block)]
        total += bz * low(v, 1) + high(bz * v, 1)
        total += bx * low(v, 2) + high(bx * v, 2)
        return v, total

    def parity(self, block):
        shape = (block, self.depth, 128)
        return (iota(shape, 0) + iota(shape, 1) + iota(shape, 2) + self.shift) & 1

    def first(self, factor, lo, hi, block):
        parity = self.parity(block)
        n = (hi - lo) // block
        assert n * block == hi - lo

        def step(i, _):
            y = lo + i * block
            new = factor * self.source[pl.ds(y, block)] * self.inv[pl.ds(y, block)]
            self.value[pl.ds(y, block)] = jnp.where(parity == (y & 1), new, 0.0)
            return 0

        lax.fori_loop(0, n, step, 0)

    def half(self, colour, factor, lo, hi, block):
        parity = self.parity(block)
        n = (hi - lo) // block
        assert n * block == hi - lo

        def step(i, _):
            y = lo + i * block
            v, total = self.gathered(y, block)
            new = (factor * self.source[pl.ds(y, block)] + total) * self.inv[pl.ds(y, block)]
            self.value[pl.ds(y, block)] = jnp.where(parity == ((y + colour) & 1), new, v)
            return 0

        lax.fori_loop(0, n, step, 0)

    def residual(self, factor, y, block):
        v, total = self.gathered(y, block)
        return self.source[pl.ds(y, block)] - (self.diag[pl.ds(y, block)] * v - total) * (1.0 / factor)


def finest_window(s_ref, d_ref, before_ref, after_ref, source, density):
    zeros = jnp.zeros((5, 8, 128), F32)
    for ref in (source, density):
        for rows in (pl.ds(0, 5), pl.ds(13, 5)):
            ref[rows, 0:8] = zeros
            ref[rows, 56:64] = zeros
    source[0:5, 8:56] = before_ref[0:5]
    source[13:18, 8:56] = after_ref[0:5]
    density[0:5, 8:56] = before_ref[5:10]
    density[13:18, 8:56] = after_ref[5:10]
    source[5:13] = s_ref[...]
    density[5:13] = d_ref[...]


def finest_down(s_ref, d_ref, before_ref, after_ref, message_ref, low_ref, high_ref, below_ref,
                by, bz, bx, inv, diag, source, value, density, plane):
    finest_window(s_ref, d_ref, before_ref, after_ref, source, density)
    value[0] = jnp.zeros((64, 128), F32)
    value[17] = jnp.zeros((64, 128), F32)
    level = Level(18, 5, 64, True, by, bz, bx, inv, diag, source, value)
    level.coefficients(density, 1, 17, 2)
    level.first(1.0, 1, 17, 2)
    level.half(1, 1.0, 2, 16, 2)
    level.half(0, 1.0, 3, 15, 2)
    level.half(1, 1.0, 4, 14, 2)
    to_low, to_high = halving(0, 0.125), halving(64, 0.125)
    pooled = []
    for row in range(4):
        y = 5 + 2 * row
        left = level.residual(1.0, y, 2)
        plane[row] = left[0, 16:48] + left[1, 16:48]
        plane[4 + row] = density[y, 16:48] + density[y + 1, 16:48]
    for row in range(8):
        pooled.append(plane[row, pl.ds(0, 16, stride=2)] + plane[row, pl.ds(1, 16, stride=2)])
    out = dot(jnp.concatenate(pooled[:4], axis=0), to_low) + dot(jnp.concatenate(pooled[4:], axis=0), to_high)
    message_ref[...] = out.reshape(4, 16, 128)
    low_ref[...] = value[5:10, 8:56]
    high_ref[...] = value[8:13, 8:56]
    below_ref[...] = value[5:13]


def middle_down(place_ref, window_ref, before_ref, after_ref, coarse_ref, halo_ref, kept_ref, below_ref,
                by, bz, bx, inv, source, value, diag, density, plane,
                by2, bz2, bx2, inv2, diag2, source2, value2, density2):
    for start, rows, ref in ((0, 13, before_ref), (13, 16, window_ref), (29, 13, after_ref)):
        block = ref[...]
        source[start : start + rows] = block
        density[start : start + rows] = jnp.where(iota(block.shape, 2) < 64, pltpu.roll(block, 64, 2), 0.0)
    value[0] = jnp.zeros((48, 128), F32)
    value[41] = jnp.zeros((48, 128), F32)
    level = Level(42, 13, 48, False, by, bz, bx, inv, diag, source, value)
    level.coefficients(density, 1, 41, 2)
    level.first(4.0, 1, 41, 2)
    level.half(1, 4.0, 2, 40, 2)
    level.half(0, 4.0, 3, 39, 2)
    level.half(1, 4.0, 4, 38, 2)
    mine = pl.ds(5 + 4 * place_ref[2], 20)
    kept_ref[...] = source[mine]
    below_ref[...] = value[mine]

    pool = halving(0, 0.125, 64)

    def pooling(row, _):
        y = 3 + 2 * row
        plane[0] = density[y] + density[y + 1]
        density2[row] = dot(plane[0, pl.ds(0, 24, stride=2)] + plane[0, pl.ds(1, 24, stride=2)], pool)

        @pl.when((row > 0) & (row < 17))
        def _():
            left = level.residual(4.0, y, 2)
            plane[1] = left[0] + left[1]
            source2[row] = dot(plane[1, pl.ds(0, 24, stride=2)] + plane[1, pl.ds(1, 24, stride=2)], pool)

        return 0

    lax.fori_loop(0, 18, pooling, 0)
    value2[0] = jnp.zeros((24, 128), F32)
    value2[17] = jnp.zeros((24, 128), F32)
    below = Level(18, 5, 24, False, by2, bz2, bx2, inv2, diag2, source2, value2)
    below.coefficients(density2, 1, 17, 4)
    below.first(16.0, 1, 17, 4)
    below.half(1, 16.0, 2, 16, 7)
    below.half(0, 16.0, 3, 15, 6)
    below.half(1, 16.0, 4, 14, 5)
    pool = halving(0, 0.125, 32)
    rows = []
    for row in range(4):
        y = 5 + 2 * row
        left = below.residual(16.0, y, 2)
        plane[row, 0:24] = left[0] + left[1]
        plane[4 + row, 0:24] = density2[y] + density2[y + 1]
    for row in range(4):
        for part in (row, 4 + row):
            rows.append(plane[part, pl.ds(8, 4, stride=2)] + plane[part, pl.ds(9, 4, stride=2)])
    pooled = dot(jnp.concatenate(rows, axis=0), pool)
    for row in range(4):
        total = pooled[8 * row : 8 * row + 1]
        for i in range(1, 8):
            total = total + pltpu.roll(pooled[8 * row + i : 8 * row + i + 1], 16 * i, 1)
        coarse_ref[row : row + 1] = total
    halo_ref[...] = (
        source2[5:13, 8:16] + pltpu.roll(value2[5:13, 8:16], 32, 2) + pltpu.roll(density2[5:13, 8:16], 64, 2)
    )


def coarsest(planes, gathered_ref, density, source, by, bz, bx, inv, value):
    devices = gathered_ref.shape[0] // (planes // 4)
    shape = (8, 8, 128)
    row, lane = iota((8, 128), 0), iota((8, 128), 1)
    edge = jnp.zeros((8, 128), F32)
    for ref in (density, value):
        ref[0] = edge
        ref[planes + 1] = edge

    def spread(g, _):
        blocks = [gathered_ref[pl.ds(pl.multiple_of(g * devices + 8 * h, 8), 8)] for h in range(devices // 8)]
        for part, ref in enumerate((source, density)):
            for z in range(4):
                out = jnp.zeros((8, 128), F32)
                for h, block in enumerate(blocks):
                    moved = pltpu.roll(block, (16 * (h - z) - 64 * part) % 128, 1)
                    out = jnp.where(lane // 16 == h, moved, out)
                ref[1 + 4 * g + z] = out
        return 0

    lax.fori_loop(0, planes // 4, spread, 0)
    row, lane = iota(shape, 1), iota(shape, 2)
    first_y = (row == 0) & (lane < 16)
    last_y = (row == 7) & (lane >= 112)
    first_x = lane % 16 == 0
    last_x = lane % 16 == 15

    def low_y(a):
        turned = low(a, 1)
        return jnp.where(row == 0, pltpu.roll(turned, 16, 2), turned)

    def high_y(a):
        turned = high(a, 1)
        return jnp.where(row == 7, pltpu.roll(turned, 112, 2), turned)

    for start in range(1, planes + 1, 8):
        d = density[start : start + 8]
        lower_z = 2.0 / jnp.maximum(d + density[start - 1 : start + 7], least)
        upper_z = 2.0 / jnp.maximum(d + density[start + 1 : start + 9], least)
        lower_y = 2.0 / jnp.maximum(d + jnp.where(first_y, 0.0, low_y(d)), least)
        upper_y = 2.0 / jnp.maximum(d + jnp.where(last_y, 0.0, high_y(d)), least)
        lower_x = 2.0 / jnp.maximum(d + jnp.where(first_x, 0.0, low(d, 2)), least)
        upper_x = 2.0 / jnp.maximum(d + jnp.where(last_x, 0.0, high(d, 2)), least)
        total = lower_z + upper_z + lower_y + upper_y + lower_x + upper_x
        inverse = jnp.where(d > 0.0, 1.0 / total, 0.0)
        inv[start : start + 8] = inverse
        bz[start : start + 8] = lower_z
        bz[start + 1 : start + 9] = upper_z
        by[start : start + 8] = jnp.where(first_y, 0.0, lower_y)
        bx[start : start + 8] = jnp.where(first_x, 0.0, lower_x)
        source[start : start + 8] = 64.0 * source[start : start + 8]
        value[start : start + 8] = jnp.zeros(shape, F32)
    parity = (iota(shape, 0) + row + lane) & 1

    def sweep(_, carry):
        for colour in (0, 1):
            for start in range(1, planes + 1, 8):
                v = value[start : start + 8]
                cy, cx = by[start : start + 8], bx[start : start + 8]
                total = bz[start : start + 8] * value[start - 1 : start + 7]
                total += bz[start + 1 : start + 9] * value[start + 1 : start + 9]
                total += cy * low_y(v) + high_y(cy * v)
                total += cx * low(v, 2) + high(cx * v, 2)
                new = (source[start : start + 8] + total) * inv[start : start + 8]
                value[start : start + 8] = jnp.where(parity == colour, new, v)
        return carry

    lax.fori_loop(0, 12, sweep, 0)


def way_up(planes, place_ref, gathered_ref, halo_ref, kept_ref, below1,
           s_ref, d_ref, rim_before_ref, rim_after_ref, below0, before_ref, after_ref,
           pressure_ref, remain_ref,
           density3, source3, by3, bz3, bx3, inv3, value3, wide,
           density2, source2, by2, bz2, bx2, inv2, value2,
           density1, source1, by1, bz1, bx1, inv1, value1,
           density0, source0, by0, bz0, bx0, inv0, diag0, value0, plane):
    devices = gathered_ref.shape[0] // (planes // 4)
    at_z, at_y, at_group = place_ref[0], place_ref[1], place_ref[2]
    coarsest(planes, gathered_ref, density3, source3, by3, bz3, bx3, inv3, value3)

    block = halo_ref[pl.ds(2 * at_group, 18)]
    lane = iota(block.shape, 2)
    source2[...] = jnp.where(lane < 32, block, 0.0)
    density2[...] = jnp.where(lane < 32, pltpu.roll(block, 64, 2), 0.0)
    value2[...] = jnp.where(lane < 32, pltpu.roll(block, 96, 2), 0.0)
    level = Level(18, 8, 24, False, by2, bz2, bx2, inv2, None, source2, value2)
    level.coefficients(density2, 1, 17, 4)
    wide[0:4] = jnp.zeros((4, 8, 128), F32)
    wide[planes + 4 : planes + 8] = jnp.zeros((4, 8, 128), F32)
    wide[4 : planes + 4] = value3[1 : planes + 1]
    near = wide[pl.ds(4 * at_z, 12)]
    row = iota((8, 128), 0)
    picked = []
    for i in range(9):
        y = at_y + i - 4
        inside = (y >= 0) & (y < devices)
        y = jnp.clip(y, 0, devices - 1)
        rows = jnp.sum(jnp.where(row == y % 8, near, 0.0), axis=1)
        rows = pltpu.roll(rows, (128 - 16 * (y // 8)) % 128, 1)
        picked.append(jnp.where(inside & (iota((12, 128), 1) < 16), rows, 0.0))
        picked.append(jnp.zeros((4, 128), F32))
    spread = dot(jnp.concatenate(picked, axis=0), doubling(16))
    for i in range(9):
        plane[i, pl.ds(0, 12, stride=2)] = spread[16 * i : 16 * i + 12]
        plane[i, pl.ds(1, 12, stride=2)] = spread[16 * i : 16 * i + 12]
    for i in range(9):
        for j in range(2):
            value2[2 * i + j] = value2[2 * i + j] + plane[i, 0:24]
    level.half(0, 16.0, 1, 17, 4)
    level.half(1, 16.0, 2, 16, 7)
    level.half(0, 16.0, 3, 15, 6)
    level.half(1, 16.0, 4, 14, 5)

    source1[...] = kept_ref[...]
    lane = iota((20, 48, 128), 2)
    density1[...] = jnp.where(lane < 64, pltpu.roll(kept_ref[...], 64, 2), 0.0)
    level = Level(20, 8, 48, False, by1, bz1, bx1, inv1, None, source1, value1)
    level.coefficients(density1, 2, 18, 2)
    spread = dot(value2[4:14].reshape(240, 128), doubling(32))
    for i in range(10):
        plane[i, pl.ds(0, 24, stride=2)] = spread[24 * i : 24 * i + 24]
        plane[i, pl.ds(1, 24, stride=2)] = spread[24 * i : 24 * i + 24]
    for i in range(10):
        for j in range(2):
            value1[2 * i + j] = below1[2 * i + j] + plane[i, 0:48]
    level.half(0, 4.0, 2, 18, 2)
    level.half(1, 4.0, 3, 17, 2)
    level.half(0, 4.0, 4, 16, 2)
    level.half(1, 4.0, 5, 15, 2)

    finest_window(s_ref, d_ref, rim_before_ref, rim_after_ref, source0, density0)
    level = Level(18, 5, 64, True, by0, bz0, bx0, inv0, diag0, source0, value0)
    level.coefficients(density0, 1, 17, 2)
    spread = dot(value1[5:15, 8:40].reshape(320, 128), doubling(64))
    for i in range(10):
        plane[i, pl.ds(0, 32, stride=2)] = spread[32 * i : 32 * i + 32]
        plane[i, pl.ds(1, 32, stride=2)] = spread[32 * i : 32 * i + 32]
    for i in range(10):
        for j in range(2):
            y = 2 * i + j - 1
            if 5 <= y < 13:
                value0[y] = below0[y - 5] + plane[i]
            elif 0 <= y < 18:
                value0[y] = plane[i]
    value0[0:5, 8:56] = value0[0:5, 8:56] + before_ref[...]
    value0[13:18, 8:56] = value0[13:18, 8:56] + after_ref[...]
    level.half(0, 1.0, 1, 17, 2)
    level.half(1, 1.0, 2, 16, 2)
    level.half(0, 1.0, 3, 15, 2)
    level.half(1, 1.0, 4, 14, 2)
    pressure_ref[...] = jnp.swapaxes(value0[5:13, 16:48], 0, 1)
    for i in range(0, 8, 2):
        plane[i : i + 2] = level.residual(1.0, 5 + i, 2)
    remain_ref[...] = jnp.swapaxes(plane[0:8, 16:48], 0, 1)


def pair(array_up, array_down, axis, distance, ring=False):
    devices = lax.axis_size(axis)
    up = [(i, (i + distance) % devices) for i in range(devices if ring else devices - distance)]
    down = [(j, i) for i, j in up]
    return lax.ppermute(array_up, axis, up), lax.ppermute(array_down, axis, down)


def shape(*sizes):
    return jax.ShapeDtypeStruct(sizes, F32)


def vmem(*sizes):
    return pltpu.VMEM(sizes, F32)


def params():
    return pltpu.CompilerParams(vmem_limit_bytes=48 * 1024 * 1024)


def body(right_side, labels):
    gz, xy = lax.axis_size("gz"), lax.axis_size("xy")
    density = jnp.where(labels == 1, gas_density, 1.0).astype(F32)
    before, after = pair(
        jnp.concatenate([right_side[-8:], density[-9:]], axis=0),
        jnp.concatenate([right_side[:8], density[:9]], axis=0),
        "gz",
        1,
    )
    zeros = jnp.zeros((8, 8, 128), F32)
    wide_source = jnp.concatenate([zeros, before[:8], right_side, after[:8], zeros], axis=0)
    wide_density = jnp.concatenate([zeros[:7], before[8:], density, after[8:], zeros[:7]], axis=0)
    wide_source = jnp.swapaxes(wide_source, 0, 1)
    wide_density = jnp.swapaxes(wide_density, 0, 1)
    before, after = pair(
        jnp.concatenate([wide_source[3:, 8:56], wide_density[3:, 8:56]], axis=0),
        jnp.concatenate([wide_source[:5, 8:56], wide_density[:5, 8:56]], axis=0),
        "xy",
        1,
    )
    finest = (wide_source, wide_density, before, after)
    message, first_rows, last_rows, below0 = pl.pallas_call(
        finest_down,
        out_shape=[shape(4, 16, 128), shape(5, 48, 128), shape(5, 48, 128), shape(8, 64, 128)],
        scratch_shapes=[vmem(18, 64, 128)] * 8 + [vmem(8, 32, 128)],
        compiler_params=params(),
    )(*finest)

    groups = [[GROUP * i + j for j in range(GROUP)] for i in range(xy // GROUP)]
    window = lax.all_to_all(
        jnp.broadcast_to(message[None], (GROUP, 4, 16, 128)), "xy", 0, 0, axis_index_groups=groups, tiled=True
    ).reshape(4 * GROUP, 16, 128)
    before, after = pair(window, window, "gz", 1)
    window = jnp.concatenate([before, window, after], axis=1)
    before, after = pair(window[-13:], window[:13], "xy", GROUP)
    place = jnp.stack([lax.axis_index("gz"), lax.axis_index("xy"), lax.axis_index("xy") % GROUP]).astype(jnp.int32)
    smem, block = pl.BlockSpec(memory_space=pltpu.SMEM), pl.BlockSpec(memory_space=pltpu.VMEM)
    coarse, halo, kept, below1 = pl.pallas_call(
        middle_down,
        out_shape=[shape(4, 128), shape(8, 8, 128), shape(20, 48, 128), shape(20, 48, 128)],
        in_specs=[smem] + [block] * 3,
        scratch_shapes=[vmem(42, 48, 128)] * 8 + [vmem(8, 48, 128)] + [vmem(18, 24, 128)] * 8,
        compiler_params=params(),
    )(place, window, before, after)

    peers = [[xy * z + GROUP * i + j for z in range(gz) for i in range(xy // GROUP)] for j in range(GROUP)]
    everywhere = lax.all_to_all(
        jnp.broadcast_to(coarse[None], (gz * xy // GROUP, 4, 128)),
        ("gz", "xy"), 0, 0, axis_index_groups=peers, tiled=True,
    ).reshape(gz * xy, 128)
    before, after = pair(halo, halo, "gz", 1)
    halo = jnp.concatenate([before, halo, after], axis=1)
    before, after = pair(halo, halo, "xy", GROUP)
    halo = jnp.concatenate([before, halo, after], axis=0)
    value_before, value_after = pair(last_rows, first_rows, "xy", 1)
    planes = 4 * gz
    return pl.pallas_call(
        partial(way_up, planes),
        out_shape=[shape(32, 8, 128)] * 2,
        in_specs=[smem] + [block] * 11,
        scratch_shapes=[vmem(planes + 2, 8, 128)] * 7
        + [vmem(planes + 8, 8, 128)]
        + [vmem(18, 24, 128)] * 7
        + [vmem(20, 48, 128)] * 7
        + [vmem(18, 64, 128)] * 8
        + [vmem(10, 64, 128)],
        compiler_params=params(),
    )(place, everywhere, halo, kept, below1, *finest, below0, value_before, value_after)


def solution(mesh):
    return jax.shard_map(
        body,
        mesh=mesh,
        in_specs=(P("gz", "xy", None), P("gz", "xy", None)),
        out_specs=(P("gz", "xy", None), P("gz", "xy", None)),
        check_vma=False,
    )
```

```python
from functools import partial

import jax
import jax.numpy as jnp
from jax import lax
from jax.experimental import pallas as pl
from jax.experimental.pallas import tpu as pltpu
from jax.sharding import PartitionSpec as P

gas_density = 0.001
least = 1e-4
F32 = jnp.float32
GROUP = 4


def dot(a, b):
    return lax.dot_general(
        a, b, (((1,), (0,)), ((), ())), precision=lax.Precision.HIGHEST, preferred_element_type=F32
    )


def iota(shape, axis):
    return lax.broadcasted_iota(jnp.int32, shape, axis)


def halving(offset, weight, width=128):
    row, column = iota((128, 128), 0), iota((128, 128), 1)
    return jnp.where((row // 2 + offset == column) & (row < width), weight, 0.0).astype(F32)


def doubling(width, first=0, period=128):
    row, column = iota((128, 128), 0), iota((128, 128), 1)
    hit = ((column % period) // 2 + first == row) & (row < first + width)
    return jnp.where(hit, 1.0, 0.0).astype(F32)


def inverse(a):
    r = pl.reciprocal(a, approx=True)
    r = r * (2.0 - a * r)
    return r * (2.0 - a * r)


def blocks(lo, count, block, step):
    assert count % block == 0
    if count == block:
        step(lo)
    else:

        def turn(i, _):
            step(lo + i * block)
            return 0

        lax.fori_loop(0, count // block, turn, 0)


LOWER, UPPER, LEFT, RIGHT, OUT, INNER, INVERSE, DIAGONAL, SOURCE = 0, 2, 4, 6, 8, 10, 11, 13, 15
KEPT = 17


class Level:
    def __init__(self, density, keep, value, width, cross=0, ends=False):
        self.density, self.keep, self.value = density, keep, value
        self.depth, self.width, self.cross, self.ends = value.shape[2], width, cross, ends
        self.row, self.lane = iota((1, 8, 128), 1), iota((1, 8, 128), 2)
        self.odd = (self.row + self.lane) % 2 == 1

    def choose(self, mask, a, b):
        if not isinstance(a, float):
            shape, a = a.shape, a.reshape(-1, 8, 128)
        if not isinstance(b, float):
            shape, b = b.shape, b.reshape(-1, 8, 128)
        return jnp.where(mask, a, b).reshape(shape)

    def low(self, a):
        turned = pltpu.roll(a, 1, 1)
        if self.cross:
            head = turned[:, :8]
            head = jnp.where(self.row == 0, pltpu.roll(head, self.cross, 2), head)
            turned = head if self.depth == 8 else jnp.concatenate([head, turned[:, 8:]], axis=1)
        return turned

    def high(self, a):
        turned = pltpu.roll(a, self.depth - 1, 1)
        if self.cross:
            tail = turned[:, -8:]
            tail = jnp.where(self.row == 7, pltpu.roll(tail, 128 - self.cross, 2), tail)
            turned = tail if self.depth == 8 else jnp.concatenate([turned[:, :-8], tail], axis=1)
        return turned

    def coefficients(self, source, factor, lo, count, block):
        first_x, last_x = self.lane % max(self.width, 1) == 0, self.lane % max(self.width, 1) == self.width - 1
        if self.ends:
            first, last = (self.row == 0) & (self.lane < self.width), (self.row == 7) & (self.lane >= 128 - self.width)

        def coupling(a, b):
            return 2.0 * inverse(jnp.maximum(a + b, least))

        def both(place, at, even, odd):
            self.keep[place, at] = self.choose(self.odd, odd, even)
            self.keep[place + 1, at] = self.choose(self.odd, even, odd)

        def step(j):
            at = pl.ds(j, block)
            shape = (block, 2, self.depth, 128)
            rows = self.density[pl.ds(2 * j, 2 * block)].reshape(shape)
            before = self.density[pl.ds(2 * j - 1, 2 * block)].reshape(shape)[:, 0]
            after = self.density[pl.ds(2 * j + 1, 2 * block)].reshape(shape)[:, 1]
            inner = coupling(rows[:, 0], rows[:, 1])
            out = (coupling(rows[:, 0], before), coupling(rows[:, 1], after))
            parts = []
            for k in range(2):
                d = rows[:, k]
                if self.width or self.ends:
                    edge = 2.0 * inverse(jnp.maximum(d, least))
                lower = coupling(d, self.low(d))
                upper = self.high(lower)
                if self.ends:
                    lower, upper = self.choose(first, edge, lower), self.choose(last, edge, upper)
                left = coupling(d, pltpu.roll(d, 1, 2))
                right = pltpu.roll(left, 127, 2)
                if self.width:
                    left, right = self.choose(first_x, edge, left), self.choose(last_x, edge, right)
                total = lower + upper + (out[0] + inner if k == 0 else inner + out[1]) + left + right
                if self.ends:
                    lower, upper = self.choose(first, 0.0, lower), self.choose(last, 0.0, upper)
                if self.width:
                    left, right = self.choose(first_x, 0.0, left), self.choose(last_x, 0.0, right)
                parts.append((lower, upper, left, right, jnp.where(d > 0.0, inverse(total), 0.0), total))
            for place, even, odd in zip((LOWER, UPPER, LEFT, RIGHT, INVERSE, DIAGONAL), *parts):
                both(place, at, even, odd)
            both(OUT, at, out[0], out[1])
            self.keep[INNER, at] = inner
            if source is not None:
                rows = factor * source[pl.ds(2 * j, 2 * block)].reshape(shape)
                both(SOURCE, at, rows[:, 0], rows[:, 1])

        blocks(lo, count, block, step)

    def gathered(self, colour, j, block):
        at, keep = pl.ds(j, block), self.keep
        other = self.value.at[1 - colour]
        w = other[at]
        mask = self.odd if colour else jnp.logical_not(self.odd)
        side = self.choose(mask, other[pl.ds(j - 1, block)], other[pl.ds(j + 1, block)])
        total = keep[INNER, at] * w + keep[OUT + colour, at] * side
        total += keep[LOWER + colour, at] * self.low(w) + keep[UPPER + colour, at] * self.high(w)
        total += keep[LEFT + colour, at] * pltpu.roll(w, 1, 2) + keep[RIGHT + colour, at] * pltpu.roll(w, 127, 2)
        return total

    def first(self, lo, count, block):
        def step(j):
            at = pl.ds(j, block)
            self.value[0, at] = self.keep[SOURCE, at] * self.keep[INVERSE, at]

        blocks(lo, count, block, step)

    def half(self, colour, lo, count, block):
        def step(j):
            at = pl.ds(j, block)
            total = self.keep[SOURCE + colour, at] + self.gathered(colour, j, block)
            self.value[colour, at] = total * self.keep[INVERSE + colour, at]

        blocks(lo, count, block, step)

    def residual(self, factor, j, block):
        at, out = pl.ds(j, block), []
        for colour in (0, 1):
            total = self.keep[DIAGONAL + colour, at] * self.value[colour, at] - self.gathered(colour, j, block)
            out.append((self.keep[SOURCE + colour, at] - total) * (1.0 / factor))
        return out

    def rows(self, red, black):
        return self.choose(self.odd, black, red), self.choose(self.odd, red, black)

    def clear_red(self, pairs):
        for j in pairs:
            self.value[0, j] = jnp.zeros((self.depth, 128), F32)

    def clear(self, pairs):
        for j in pairs:
            self.value[:, j] = jnp.zeros((2, self.depth, 128), F32)


def finest_window(s_ref, d_ref, before_ref, after_ref, source, density):
    for ref in (source, density):
        for rows in (pl.ds(0, 6), pl.ds(14, 6)):
            ref[rows] = jnp.zeros((6, 64, 128), F32)
    source[1:6, 8:56] = before_ref[0:5]
    source[14:19, 8:56] = after_ref[0:5]
    density[1:6, 8:56] = before_ref[5:10]
    density[14:19, 8:56] = after_ref[5:10]
    source[6:14] = s_ref[...]
    density[6:14] = d_ref[...]


def finest_down(s_ref, d_ref, before_ref, after_ref, message_ref, low_ref, high_ref, below_ref,
                source, density, keep, value, plane):
    finest_window(s_ref, d_ref, before_ref, after_ref, source, density)
    level = Level(density, keep, value, 128)
    level.clear((0, 9))
    value[1, 1] = jnp.zeros((64, 128), F32)
    value[1, 8] = jnp.zeros((64, 128), F32)
    level.coefficients(source, 1.0, 1, 8, 1)
    level.first(1, 8, 2)
    level.half(1, 1, 8, 2)
    level.half(0, 2, 6, 2)
    level.half(1, 2, 6, 2)

    def pooling(j):
        red, black = level.residual(1.0, 3 + j, 1)
        plane[pl.ds(j, 1)] = (red + black)[:, 16:48]
        plane[pl.ds(4 + j, 1)] = (density[pl.ds(6 + 2 * j, 1)] + density[pl.ds(7 + 2 * j, 1)])[:, 16:48]

    blocks(0, 4, 1, pooling)
    pooled = plane[:, pl.ds(0, 16, stride=2)] + plane[:, pl.ds(1, 16, stride=2)]
    out = dot(pooled[:4].reshape(64, 128), halving(0, 0.125)) + dot(pooled[4:].reshape(64, 128), halving(64, 0.125))
    message_ref[...] = out.reshape(4, 16, 128)
    low_ref[...] = value[1, 3:6, 8:56]
    high_ref[...] = value[1, 4:7, 8:56]
    below_ref[...] = value[1, 3:7]


def folded(ref, rows, source, density, start):
    block = ref[rows]
    near, far = block[:, :24], block[:, 24:]
    left = iota(near.shape, 2) < 64
    source[start] = jnp.where(left, near, pltpu.roll(far, 64, 2))
    density[start] = jnp.where(left, pltpu.roll(near, 64, 2), far)


def middle_down(place_ref, window_ref, before_ref, after_ref, coarse_ref, halo_ref, kept_ref, below_ref,
                window, source, density, keep, value, plane, source2, density2, keep2, value2):
    window[1:43, 16:32] = window_ref[...]
    for ref, near, far in ((before_ref, 0, 8), (after_ref, 32, 32)):
        window[9:35, near : near + 16] = ref[0:416].reshape(26, 16, 128)
        for start, rows in ((1, 416), (35, 480)):
            window[start : start + 8, far : far + 8] = ref[rows : rows + 64].reshape(8, 8, 128)
            clear = 0 if near == 0 else 40
            window[start : start + 8, clear : clear + 8] = jnp.zeros((8, 8, 128), F32)
    for row in (0, 43):
        window[row] = jnp.zeros((48, 128), F32)
    blocks(0, 44, 4, lambda r: folded(window, pl.ds(r, 4), source, density, pl.ds(r, 4)))
    level = Level(density, keep, value, 64, 64)
    level.clear((0, 21))
    for j in (1, 20):
        value[1, j] = jnp.zeros((24, 128), F32)
    level.coefficients(source, 4.0, 1, 20, 2)
    level.first(1, 20, 5)
    level.half(1, 1, 20, 5)
    level.half(0, 2, 18, 6)
    level.half(1, 2, 18, 6)
    kept_ref[...] = window[pl.ds(6 + 4 * place_ref[2], 20)]
    below_ref[...] = value[1, pl.ds(3 + 2 * place_ref[2], 10)]

    def pooling(j):
        red, black = level.residual(4.0, 3 + j, 4)
        plane[pl.ds(j, 4), 0:24] = red + black

    blocks(0, 16, 4, pooling)
    rows = density[4:40].reshape(18, 2, 24, 128)
    plane[16:34, 0:24] = rows[:, 0] + rows[:, 1]
    pooled = plane[:, pl.ds(0, 16, stride=2)] + plane[:, pl.ds(1, 16, stride=2)]
    pooled = dot(pooled.reshape(34 * 16, 128), halving(0, 0.125)).reshape(34, 16, 128)
    lane = iota((34, 16, 128), 2)
    near, far = jnp.where(lane < 32, pooled, 0.0), jnp.where(lane < 32, pltpu.roll(pooled, 96, 2), 0.0)
    for ref, start, parts in ((source2, 2, slice(0, 16)), (density2, 1, slice(16, 34))):
        ref[start : start + parts.stop - parts.start, 0:12] = near[parts, 0:12]
        ref[start : start + parts.stop - parts.start, 12:24] = far[parts, 0:12]
    for row in (0, 19):
        density2[row] = jnp.zeros((24, 128), F32)
    below = Level(density2, keep2, value2, 0)
    below.clear((0, 9))
    for j in (1, 8):
        value2[1, j] = jnp.zeros((24, 128), F32)
    below.coefficients(source2, 16.0, 1, 8, 2)
    below.first(1, 8, 8)
    below.half(1, 1, 8, 4)
    below.half(0, 2, 6, 6)
    below.half(1, 2, 6, 6)
    red, black = below.residual(16.0, 3, 4)
    plane[0:4, 0:24] = red + black
    rows = density2[6:14].reshape(4, 2, 24, 128)
    plane[4:8, 0:24] = rows[:, 0] + rows[:, 1]
    rows = []
    for row in range(4):
        for part in (row, 4 + row):
            rows.append(plane[part, pl.ds(8, 4, stride=2)] + plane[part, pl.ds(9, 4, stride=2)])
    pooled = dot(jnp.concatenate(rows, axis=0), halving(0, 0.125, 32))
    for row in range(4):
        total = pooled[8 * row : 8 * row + 1]
        for i in range(1, 8):
            total = total + pltpu.roll(pooled[8 * row + i : 8 * row + i + 1], 16 * i, 1)
        coarse_ref[row : row + 1] = total
    for j in range(4):
        for k in range(2):
            row = 6 + 2 * j + k
            total = source2[row, 8:16] + pltpu.roll(density2[row, 8:16], 64, 1)
            if k == 0:
                total = total + pltpu.roll(value2[1, 3 + j, 8:16], 32, 1)
            halo_ref[2 * j + k] = total


def coarsest(planes, place_ref, gathered_ref, near_ref, source, density, keep, value, wide):
    groups = gathered_ref.shape[0]
    lane = iota((8, 128), 1)
    for row in (0, 1, planes + 2, planes + 3):
        density[row] = jnp.zeros((8, 128), F32)

    def spread(g, _):
        tiles = [
            jnp.concatenate([gathered_ref[2 * h, g], gathered_ref[2 * h + 1, g]], axis=0) for h in range(groups // 2)
        ]
        for part, ref in enumerate((source, density)):
            for z in range(4):
                out = jnp.zeros((8, 128), F32)
                for h, block in enumerate(tiles):
                    moved = pltpu.roll(block, (16 * (h - z) - 64 * part) % 128, 1)
                    out = jnp.where(lane // 16 == h, moved, out)
                ref[2 + 4 * g + z] = out
        return 0

    lax.fori_loop(0, planes // 4, spread, 0)
    level = Level(density, keep, value, 16, 16, ends=True)
    pairs = planes // 2
    value[...] = jnp.zeros(value.shape, F32)
    level.coefficients(source, 64.0, 1, pairs, 4)

    def sweep(_, carry):
        level.half(0, 1, pairs, pairs)
        level.half(1, 1, pairs, pairs)
        return carry

    lax.fori_loop(0, 12, sweep, 0)
    wide[0:4] = jnp.zeros((4, 8, 128), F32)
    wide[planes + 4 : planes + 8] = jnp.zeros((4, 8, 128), F32)
    even, odd = level.rows(value[0, 1 : pairs + 1], value[1, 1 : pairs + 1])
    for j in range(pairs):
        wide[4 + 2 * j] = even[j]
        wide[5 + 2 * j] = odd[j]
    near_ref[...] = wide[pl.ds(4 * place_ref[0], 12)]


def way_up(devices, place_ref, near_ref, halo_ref, kept_ref, below1_ref,
           s_ref, d_ref, rim_before_ref, rim_after_ref, below0_ref, before_ref, after_ref,
           pressure_ref, remain_ref,
           source2, density2, keep2, value2, source1, density1, keep1, value1,
           source0, density0, keep0, value0, plane):
    at_y, at_group = place_ref[1], place_ref[2]

    block = halo_ref[pl.ds(2 * at_group, 18)]
    lane = iota(block.shape, 2)
    source2[2:20] = block
    for rows in (slice(0, 2), slice(20, 22)):
        density2[rows] = jnp.zeros((2, 24, 128), F32)
    density2[2:20] = jnp.where(lane < 32, pltpu.roll(block, 64, 2), 0.0)
    level = Level(density2, keep2, value2, 0)
    level.clear((0, 10))
    level.coefficients(source2, 16.0, 1, 9, 3)
    row = iota((8, 128), 0)
    near = near_ref[...]
    picked = []
    for i in range(9):
        y = at_y + i - 4
        inside = (y >= 0) & (y < devices)
        y = jnp.clip(y, 0, devices - 1)
        rows = jnp.sum(jnp.where(row == y % 8, near, 0.0), axis=1)
        rows = pltpu.roll(rows, (128 - 16 * (y // 8)) % 128, 1)
        picked.append(jnp.where(inside & (iota((12, 128), 1) < 16), rows, 0.0))
        picked.append(jnp.zeros((4, 128), F32))
    spread = dot(jnp.concatenate(picked, axis=0), doubling(16)).reshape(9, 16, 128)
    plane[0:9, pl.ds(0, 12, stride=2)] = spread[:, 0:12]
    plane[0:9, pl.ds(1, 12, stride=2)] = spread[:, 0:12]
    below = jnp.where(lane < 32, pltpu.roll(block, 96, 2), 0.0).reshape(9, 2, 24, 128)[:, 0]
    value2[1, 1:10] = below + plane[0:9, 0:24]
    level.half(0, 1, 9, 3)
    level.half(1, 2, 7, 7)
    level.half(0, 2, 7, 7)
    level.half(1, 3, 5, 5)
    even, odd = level.rows(value2[0, 3:8], value2[1, 3:8])

    blocks(0, 20, 4, lambda r: folded(kept_ref, pl.ds(r, 4), source1, density1, pl.ds(r, 4)))
    level = Level(density1, keep1, value1, 64, 64)
    level.coefficients(source1, 4.0, 1, 8, 2)
    rows = jnp.stack([even, odd], axis=1).reshape(240, 128)
    spread = dot(rows, doubling(32, 0, 64)).reshape(10, 24, 128)
    plane[0:10, pl.ds(0, 24, stride=2)] = spread
    plane[0:10, pl.ds(1, 24, stride=2)] = spread
    left = iota((10, 24, 128), 2) < 64
    value1[1] = below1_ref[...] + jnp.where(left, plane[0:10, 0:24], plane[0:10, 24:48])
    level.clear_red((0, 9))
    level.half(0, 1, 8, 4)
    level.half(1, 1, 8, 4)
    level.half(0, 2, 6, 6)
    level.half(1, 2, 6, 6)
    even, odd = level.rows(value1[0, 2:8], value1[1, 2:8])
    rows = jnp.stack([even, odd], axis=1).reshape(12, 24, 128)[1:11]

    finest_window(s_ref, d_ref, rim_before_ref, rim_after_ref, source0, density0)
    level = Level(density0, keep0, value0, 128)
    level.coefficients(source0, 1.0, 1, 8, 1)
    near = dot(rows[:, 8:24].reshape(160, 128), doubling(64)).reshape(10, 16, 128)
    far = dot(rows[:, 0:16].reshape(160, 128), doubling(64, 64)).reshape(10, 16, 128)
    for start, part in ((0, near), (32, far)):
        plane[0:10, pl.ds(start, 16, stride=2)] = part
        plane[0:10, pl.ds(start + 1, 16, stride=2)] = part
    value0[1] = plane[...]
    value0[1, 0:3, 8:56] = value0[1, 0:3, 8:56] + before_ref[...]
    value0[1, 3:7] = value0[1, 3:7] + below0_ref[...]
    value0[1, 7:10, 8:56] = value0[1, 7:10, 8:56] + after_ref[...]
    level.clear_red((0, 9))
    level.half(0, 1, 8, 2)
    level.half(1, 1, 8, 2)
    level.half(0, 2, 6, 2)
    level.half(1, 2, 6, 2)
    even, odd = level.rows(value0[0, 3:7, 16:48], value0[1, 3:7, 16:48])
    pressure_ref[...] = jnp.swapaxes(jnp.stack([even, odd], axis=1).reshape(8, 32, 128), 0, 1)

    def remaining(j):
        red, black = level.residual(1.0, 3 + j, 1)
        even, odd = level.rows(red, black)
        plane[pl.ds(2 * j, 1)] = even
        plane[pl.ds(2 * j + 1, 1)] = odd

    blocks(0, 4, 1, remaining)
    remain_ref[...] = jnp.swapaxes(plane[0:8, 16:48], 0, 1)


def pair(array_up, array_down, axis, distance, ring=False):
    devices = lax.axis_size(axis)
    up = [(i, (i + distance) % devices) for i in range(devices if ring else devices - distance)]
    down = [(j, i) for i, j in up]
    return lax.ppermute(array_up, axis, up), lax.ppermute(array_down, axis, down)


def shape(*sizes):
    return jax.ShapeDtypeStruct(sizes, F32)


def vmem(*sizes):
    return pltpu.VMEM(sizes, F32)


def params():
    return pltpu.CompilerParams(vmem_limit_bytes=48 * 1024 * 1024)


def body(right_side, labels):
    gz, xy = lax.axis_size("gz"), lax.axis_size("xy")
    density = jnp.where(labels == 1, gas_density, 1.0).astype(F32)
    before, after = pair(
        jnp.concatenate([right_side[-8:], density[-9:]], axis=0),
        jnp.concatenate([right_side[:8], density[:9]], axis=0),
        "gz",
        1,
    )
    zeros = jnp.zeros((8, 8, 128), F32)
    wide_source = jnp.concatenate([zeros, before[:8], right_side, after[:8], zeros], axis=0)
    wide_density = jnp.concatenate([zeros[:7], before[8:], density, after[8:], zeros[:7]], axis=0)
    wide_source = jnp.swapaxes(wide_source, 0, 1)
    wide_density = jnp.swapaxes(wide_density, 0, 1)
    before, after = pair(
        jnp.concatenate([wide_source[3:, 8:56], wide_density[3:, 8:56]], axis=0),
        jnp.concatenate([wide_source[:5, 8:56], wide_density[:5, 8:56]], axis=0),
        "xy",
        1,
    )
    finest = (wide_source, wide_density, before, after)
    message, first_rows, last_rows, below0 = pl.pallas_call(
        finest_down,
        out_shape=[shape(4, 16, 128), shape(3, 48, 128), shape(3, 48, 128), shape(4, 64, 128)],
        scratch_shapes=[vmem(20, 64, 128)] * 2 + [vmem(KEPT, 10, 64, 128), vmem(2, 10, 64, 128), vmem(8, 32, 128)],
        compiler_params=params(),
    )(*finest)

    teams = [[GROUP * i + j for j in range(GROUP)] for i in range(xy // GROUP)]
    window = lax.all_to_all(
        jnp.broadcast_to(message[None], (GROUP, 4, 16, 128)), "xy", 0, 0, axis_index_groups=teams, tiled=True
    ).reshape(4 * GROUP, 16, 128)
    before, after = pair(window[-13:], window[:13], "xy", GROUP)
    window = jnp.concatenate([before, window, after], axis=0)

    def faces(near):
        parts = (window[8:34], window[:8, near], window[34:, near])
        return jnp.concatenate([part.reshape(-1, 128) for part in parts], axis=0)

    before, after = pair(faces(slice(8, 16)), faces(slice(0, 8)), "gz", 1)
    place = jnp.stack([lax.axis_index("gz"), lax.axis_index("xy"), lax.axis_index("xy") % GROUP]).astype(jnp.int32)
    smem, block = pl.BlockSpec(memory_space=pltpu.SMEM), pl.BlockSpec(memory_space=pltpu.VMEM)
    coarse, halo, kept, below1 = pl.pallas_call(
        middle_down,
        out_shape=[shape(4, 128), shape(8, 8, 128), shape(20, 48, 128), shape(10, 24, 128)],
        in_specs=[smem] + [block] * 3,
        scratch_shapes=[vmem(44, 48, 128)]
        + [vmem(44, 24, 128)] * 2
        + [vmem(KEPT, 22, 24, 128), vmem(2, 22, 24, 128), vmem(34, 32, 128)]
        + [vmem(20, 24, 128)] * 2
        + [vmem(KEPT, 10, 24, 128), vmem(2, 10, 24, 128)],
        compiler_params=params(),
    )(place, window, before, after)

    column = lax.all_to_all(
        jnp.broadcast_to(jnp.concatenate([coarse, halo.reshape(64, 128)], axis=0)[None], (gz, 68, 128)),
        "gz", 0, 0, tiled=True,
    )
    peers = [[GROUP * i + j for i in range(xy // GROUP)] for j in range(GROUP)]
    everywhere = lax.all_to_all(
        jnp.broadcast_to(column[None, :, :4], (xy // GROUP, gz, 4, 128)), "xy", 0, 0, axis_index_groups=peers, tiled=True
    )
    halo = jnp.pad(column[:, 4:], ((1, 1), (0, 0), (0, 0)))
    halo = lax.dynamic_slice(halo, (lax.axis_index("gz"), 0, 0), (3, 64, 128)).reshape(3, 8, 8, 128)
    halo = jnp.swapaxes(halo, 0, 1).reshape(8, 24, 128)
    before, after = pair(halo, halo, "xy", GROUP)
    halo = jnp.concatenate([before, halo, after], axis=0)
    value_before, value_after = pair(last_rows, first_rows, "xy", 1)
    planes = 4 * gz
    near = pl.pallas_call(
        partial(coarsest, planes),
        out_shape=shape(12, 8, 128),
        in_specs=[smem, block],
        scratch_shapes=[vmem(planes + 4, 8, 128)] * 2
        + [vmem(KEPT, planes // 2 + 2, 8, 128), vmem(2, planes // 2 + 2, 8, 128), vmem(planes + 8, 8, 128)],
        compiler_params=params(),
        cost_estimate=pl.CostEstimate(flops=100_000_000, bytes_accessed=16_000_000, transcendentals=0),
    )(place, everywhere)
    return pl.pallas_call(
        partial(way_up, xy),
        out_shape=[shape(32, 8, 128)] * 2,
        in_specs=[smem] + [block] * 11,
        scratch_shapes=[vmem(22, 24, 128)] * 2
        + [vmem(KEPT, 11, 24, 128), vmem(2, 11, 24, 128)]
        + [vmem(20, 24, 128)] * 2
        + [vmem(KEPT, 10, 24, 128), vmem(2, 10, 24, 128)]
        + [vmem(20, 64, 128)] * 2
        + [vmem(KEPT, 10, 64, 128), vmem(2, 10, 64, 128), vmem(10, 64, 128)],
        compiler_params=params(),
    )(place, near, halo, kept, below1, *finest, below0, value_before, value_after)


def solution(mesh):
    return jax.shard_map(
        body,
        mesh=mesh,
        in_specs=(P("gz", "xy", None), P("gz", "xy", None)),
        out_specs=(P("gz", "xy", None), P("gz", "xy", None)),
        check_vma=False,
    )
```

```python
from functools import partial

import jax
import jax.numpy as jnp
from jax import lax
from jax.experimental import pallas as pl
from jax.experimental.pallas import tpu as pltpu
from jax.sharding import PartitionSpec as P

gas_density = 0.001
least = 1e-4
F32 = jnp.float32
GROUP = 4


def dot(a, b):
    return lax.dot_general(
        a, b, (((1,), (0,)), ((), ())), precision=lax.Precision.HIGHEST, preferred_element_type=F32
    )


def iota(shape, axis):
    return lax.broadcasted_iota(jnp.int32, shape, axis)


def halving(offset, weight, width=128):
    row, column = iota((128, 128), 0), iota((128, 128), 1)
    return jnp.where((row // 2 + offset == column) & (row < width), weight, 0.0).astype(F32)


def doubling(width, first=0, period=128):
    row, column = iota((128, 128), 0), iota((128, 128), 1)
    hit = ((column % period) // 2 + first == row) & (row < first + width)
    return jnp.where(hit, 1.0, 0.0).astype(F32)


def inverse(a):
    r = pl.reciprocal(a, approx=True)
    r = r * (2.0 - a * r)
    return r * (2.0 - a * r)


def blocks(lo, count, block, step):
    assert count % block == 0
    if count == block:
        step(lo)
    else:

        def turn(i, _):
            step(lo + i * block)
            return 0

        lax.fori_loop(0, count // block, turn, 0)


LOWER, UPPER, LEFT, RIGHT, OUT, INNER, INVERSE, DIAGONAL, SOURCE = 0, 2, 4, 6, 8, 10, 11, 13, 15
KEPT = 17


class Level:
    def __init__(self, density, keep, value, width, cross=0, ends=False):
        self.density, self.keep, self.value = density, keep, value
        self.depth, self.width, self.cross, self.ends = value.shape[2], width, cross, ends
        self.row, self.lane = iota((1, 8, 128), 1), iota((1, 8, 128), 2)
        self.odd = (self.row + self.lane) % 2 == 1

    def choose(self, mask, a, b):
        if not isinstance(a, float):
            shape, a = a.shape, a.reshape(-1, 8, 128)
        if not isinstance(b, float):
            shape, b = b.shape, b.reshape(-1, 8, 128)
        return jnp.where(mask, a, b).reshape(shape)

    def low(self, a):
        turned = pltpu.roll(a, 1, 1)
        if self.cross:
            head = turned[:, :8]
            head = jnp.where(self.row == 0, pltpu.roll(head, self.cross, 2), head)
            turned = head if self.depth == 8 else jnp.concatenate([head, turned[:, 8:]], axis=1)
        return turned

    def high(self, a):
        turned = pltpu.roll(a, self.depth - 1, 1)
        if self.cross:
            tail = turned[:, -8:]
            tail = jnp.where(self.row == 7, pltpu.roll(tail, 128 - self.cross, 2), tail)
            turned = tail if self.depth == 8 else jnp.concatenate([turned[:, :-8], tail], axis=1)
        return turned

    def coefficients(self, source, factor, lo, count, block):
        first_x, last_x = self.lane % max(self.width, 1) == 0, self.lane % max(self.width, 1) == self.width - 1
        if self.ends:
            first, last = (self.row == 0) & (self.lane < self.width), (self.row == 7) & (self.lane >= 128 - self.width)

        def coupling(a, b):
            return 2.0 * inverse(jnp.maximum(a + b, least))

        def both(place, at, even, odd):
            self.keep[place, at] = self.choose(self.odd, odd, even)
            self.keep[place + 1, at] = self.choose(self.odd, even, odd)

        def step(j):
            at = pl.ds(j, block)
            shape = (block, 2, self.depth, 128)
            rows = self.density[pl.ds(2 * j, 2 * block)].reshape(shape)
            before = self.density[pl.ds(2 * j - 1, 2 * block)].reshape(shape)[:, 0]
            after = self.density[pl.ds(2 * j + 1, 2 * block)].reshape(shape)[:, 1]
            inner = coupling(rows[:, 0], rows[:, 1])
            out = (coupling(rows[:, 0], before), coupling(rows[:, 1], after))
            parts = []
            for k in range(2):
                d = rows[:, k]
                if self.width or self.ends:
                    edge = 2.0 * inverse(jnp.maximum(d, least))
                lower = coupling(d, self.low(d))
                upper = self.high(lower)
                if self.ends:
                    lower, upper = self.choose(first, edge, lower), self.choose(last, edge, upper)
                left = coupling(d, pltpu.roll(d, 1, 2))
                right = pltpu.roll(left, 127, 2)
                if self.width:
                    left, right = self.choose(first_x, edge, left), self.choose(last_x, edge, right)
                total = lower + upper + (out[0] + inner if k == 0 else inner + out[1]) + left + right
                if self.ends:
                    lower, upper = self.choose(first, 0.0, lower), self.choose(last, 0.0, upper)
                if self.width:
                    left, right = self.choose(first_x, 0.0, left), self.choose(last_x, 0.0, right)
                parts.append((lower, upper, left, right, jnp.where(d > 0.0, inverse(total), 0.0), total))
            for place, even, odd in zip((LOWER, UPPER, LEFT, RIGHT, INVERSE, DIAGONAL), *parts):
                both(place, at, even, odd)
            both(OUT, at, out[0], out[1])
            self.keep[INNER, at] = inner
            if source is not None:
                rows = factor * source[pl.ds(2 * j, 2 * block)].reshape(shape)
                both(SOURCE, at, rows[:, 0], rows[:, 1])

        blocks(lo, count, block, step)

    def gathered(self, colour, j, block):
        at, keep = pl.ds(j, block), self.keep
        other = self.value.at[1 - colour]
        w = other[at]
        mask = self.odd if colour else jnp.logical_not(self.odd)
        side = self.choose(mask, other[pl.ds(j - 1, block)], other[pl.ds(j + 1, block)])
        total = keep[INNER, at] * w + keep[OUT + colour, at] * side
        total += keep[LOWER + colour, at] * self.low(w) + keep[UPPER + colour, at] * self.high(w)
        total += keep[LEFT + colour, at] * pltpu.roll(w, 1, 2) + keep[RIGHT + colour, at] * pltpu.roll(w, 127, 2)
        return total

    def first(self, lo, count, block):
        def step(j):
            at = pl.ds(j, block)
            self.value[0, at] = self.keep[SOURCE, at] * self.keep[INVERSE, at]

        blocks(lo, count, block, step)

    def half(self, colour, lo, count, block):
        def step(j):
            at = pl.ds(j, block)
            total = self.keep[SOURCE + colour, at] + self.gathered(colour, j, block)
            self.value[colour, at] = total * self.keep[INVERSE + colour, at]

        blocks(lo, count, block, step)

    def residual(self, factor, j, block):
        at, out = pl.ds(j, block), []
        for colour in (0, 1):
            total = self.keep[DIAGONAL + colour, at] * self.value[colour, at] - self.gathered(colour, j, block)
            out.append((self.keep[SOURCE + colour, at] - total) * (1.0 / factor))
        return out

    def rows(self, red, black):
        return self.choose(self.odd, black, red), self.choose(self.odd, red, black)

    def clear_red(self, pairs):
        for j in pairs:
            self.value[0, j] = jnp.zeros((self.depth, 128), F32)

    def clear(self, pairs):
        for j in pairs:
            self.value[:, j] = jnp.zeros((2, self.depth, 128), F32)


def finest_window(s_ref, d_ref, before_ref, after_ref, source, density):
    for ref in (source, density):
        for rows in (pl.ds(0, 6), pl.ds(14, 6)):
            ref[rows] = jnp.zeros((6, 64, 128), F32)
    source[1:6, 8:56] = before_ref[0:5]
    source[14:19, 8:56] = after_ref[0:5]
    density[1:6, 8:56] = before_ref[5:10]
    density[14:19, 8:56] = after_ref[5:10]
    source[6:14] = s_ref[...]
    density[6:14] = d_ref[...]


def finest_down(place_ref, s_ref, d_ref, before_ref, after_ref, chunk_ref, low_ref, high_ref, below_ref,
                source, density, keep, value, plane):
    finest_window(s_ref, d_ref, before_ref, after_ref, source, density)
    level = Level(density, keep, value, 128)
    level.clear((0, 9))
    value[1, 1] = jnp.zeros((64, 128), F32)
    value[1, 8] = jnp.zeros((64, 128), F32)
    level.coefficients(source, 1.0, 1, 8, 1)
    level.first(1, 8, 2)
    level.half(1, 1, 8, 2)
    level.half(0, 2, 6, 2)
    level.half(1, 2, 6, 2)

    def pooling(j):
        red, black = level.residual(1.0, 3 + j, 1)
        plane[pl.ds(j, 1)] = (red + black)[:, 16:48]
        plane[pl.ds(4 + j, 1)] = (density[pl.ds(6 + 2 * j, 1)] + density[pl.ds(7 + 2 * j, 1)])[:, 16:48]

    blocks(0, 4, 1, pooling)
    pooled = plane[:, pl.ds(0, 16, stride=2)] + plane[:, pl.ds(1, 16, stride=2)]
    out = dot(pooled[:4].reshape(64, 128), halving(0, 0.125)) + dot(pooled[4:].reshape(64, 128), halving(64, 0.125))
    low_ref[...] = value[1, 3:6, 8:56].reshape(144, 128)
    high_ref[...] = value[1, 4:7, 8:56].reshape(144, 128)
    for peer in range(GROUP):
        chunk_ref[peer, 0:64] = out
        chunk_ref[peer, 64:208] = jnp.where(peer > place_ref[2], high_ref[...], low_ref[...])
    below_ref[...] = value[1, 3:7]


def folded(ref, rows, source, density, start):
    block = ref[rows]
    near, far = block[:, :24], block[:, 24:]
    left = iota(near.shape, 2) < 64
    source[start] = jnp.where(left, near, pltpu.roll(far, 64, 2))
    density[start] = jnp.where(left, pltpu.roll(near, 64, 2), far)


def middle_down(place_ref, window_ref, before_ref, after_ref, chunk_ref, kept_ref, below_ref,
                window, source, density, keep, value, plane, source2, density2, keep2, value2):
    window[1:43, 16:32] = window_ref[...]
    for ref, near, far in ((before_ref, 0, 8), (after_ref, 32, 32)):
        window[9:35, near : near + 16] = ref[0:416].reshape(26, 16, 128)
        for start, rows in ((1, 416), (35, 480)):
            window[start : start + 8, far : far + 8] = ref[rows : rows + 64].reshape(8, 8, 128)
            clear = 0 if near == 0 else 40
            window[start : start + 8, clear : clear + 8] = jnp.zeros((8, 8, 128), F32)
    for row in (0, 43):
        window[row] = jnp.zeros((48, 128), F32)
    blocks(0, 44, 4, lambda r: folded(window, pl.ds(r, 4), source, density, pl.ds(r, 4)))
    level = Level(density, keep, value, 64, 64)
    level.clear((0, 21))
    for j in (1, 20):
        value[1, j] = jnp.zeros((24, 128), F32)
    level.coefficients(source, 4.0, 1, 20, 2)
    level.first(1, 20, 5)
    level.half(1, 1, 20, 5)
    level.half(0, 2, 18, 6)
    level.half(1, 2, 18, 6)
    kept_ref[...] = window[pl.ds(6 + 4 * place_ref[2], 20)]
    below_ref[...] = value[1, pl.ds(3 + 2 * place_ref[2], 10)]

    def pooling(j):
        red, black = level.residual(4.0, 3 + j, 4)
        plane[pl.ds(j, 4), 0:24] = red + black

    blocks(0, 16, 4, pooling)
    rows = density[4:40].reshape(18, 2, 24, 128)
    plane[16:34, 0:24] = rows[:, 0] + rows[:, 1]
    pooled = plane[:, pl.ds(0, 16, stride=2)] + plane[:, pl.ds(1, 16, stride=2)]
    pooled = dot(pooled.reshape(34 * 16, 128), halving(0, 0.125)).reshape(34, 16, 128)
    lane = iota((34, 16, 128), 2)
    near, far = jnp.where(lane < 32, pooled, 0.0), jnp.where(lane < 32, pltpu.roll(pooled, 96, 2), 0.0)
    for ref, start, parts in ((source2, 2, slice(0, 16)), (density2, 1, slice(16, 34))):
        ref[start : start + parts.stop - parts.start, 0:12] = near[parts, 0:12]
        ref[start : start + parts.stop - parts.start, 12:24] = far[parts, 0:12]
    for row in (0, 19):
        density2[row] = jnp.zeros((24, 128), F32)
    below = Level(density2, keep2, value2, 0)
    below.clear((0, 9))
    for j in (1, 8):
        value2[1, j] = jnp.zeros((24, 128), F32)
    below.coefficients(source2, 16.0, 1, 8, 2)
    below.first(1, 8, 8)
    below.half(1, 1, 8, 4)
    below.half(0, 2, 6, 6)
    below.half(1, 2, 6, 6)
    red, black = below.residual(16.0, 3, 4)
    plane[0:4, 0:24] = red + black
    rows = density2[6:14].reshape(4, 2, 24, 128)
    plane[4:8, 0:24] = rows[:, 0] + rows[:, 1]
    rows = []
    for row in range(4):
        for part in (row, 4 + row):
            rows.append(plane[part, pl.ds(8, 4, stride=2)] + plane[part, pl.ds(9, 4, stride=2)])
    pooled = dot(jnp.concatenate(rows, axis=0), halving(0, 0.125, 32))
    for row in range(4):
        total = pooled[8 * row : 8 * row + 1]
        for i in range(1, 8):
            total = total + pltpu.roll(pooled[8 * row + i : 8 * row + i + 1], 16 * i, 1)
        chunk_ref[0, 64 + row : 65 + row] = total
    for j in range(4):
        for k in range(2):
            row = 6 + 2 * j + k
            total = source2[row, 8:16] + pltpu.roll(density2[row, 8:16], 64, 1)
            if k == 0:
                total = total + pltpu.roll(value2[1, 3 + j, 8:16], 32, 1)
            chunk_ref[0, 8 * (2 * j + k) : 8 * (2 * j + k) + 8] = total
    chunk_ref[0, 68:72] = jnp.zeros((4, 128), F32)
    for peer in range(1, chunk_ref.shape[0]):
        chunk_ref[peer] = chunk_ref[0]


def coarsest(planes, place_ref, gathered_ref, near_ref, source, density, keep, value, wide):
    groups = gathered_ref.shape[0]
    lane = iota((8, 128), 1)
    for row in (0, 1, planes + 2, planes + 3):
        density[row] = jnp.zeros((8, 128), F32)

    def spread(g, _):
        tiles = [
            jnp.concatenate([gathered_ref[2 * h, g], gathered_ref[2 * h + 1, g]], axis=0) for h in range(groups // 2)
        ]
        for part, ref in enumerate((source, density)):
            for z in range(4):
                out = jnp.zeros((8, 128), F32)
                for h, block in enumerate(tiles):
                    moved = pltpu.roll(block, (16 * (h - z) - 64 * part) % 128, 1)
                    out = jnp.where(lane // 16 == h, moved, out)
                ref[2 + 4 * g + z] = out
        return 0

    lax.fori_loop(0, planes // 4, spread, 0)
    level = Level(density, keep, value, 16, 16, ends=True)
    pairs = planes // 2
    value[...] = jnp.zeros(value.shape, F32)
    level.coefficients(source, 64.0, 1, pairs, 4)

    def sweep(_, carry):
        level.half(0, 1, pairs, pairs)
        level.half(1, 1, pairs, pairs)
        return carry

    lax.fori_loop(0, 12, sweep, 0)
    wide[0:4] = jnp.zeros((4, 8, 128), F32)
    wide[planes + 4 : planes + 8] = jnp.zeros((4, 8, 128), F32)
    even, odd = level.rows(value[0, 1 : pairs + 1], value[1, 1 : pairs + 1])
    for j in range(pairs):
        wide[4 + 2 * j] = even[j]
        wide[5 + 2 * j] = odd[j]
    near_ref[...] = wide[pl.ds(4 * place_ref[0], 12)]


def way_up(devices, place_ref, near_ref, halo_ref, kept_ref, below1_ref,
           s_ref, d_ref, rim_before_ref, rim_after_ref, below0_ref, before_ref, after_ref,
           pressure_ref, remain_ref,
           source2, density2, keep2, value2, source1, density1, keep1, value1,
           source0, density0, keep0, value0, plane):
    at_y, at_group = place_ref[1], place_ref[2]

    block = halo_ref[pl.ds(2 * at_group, 18)]
    lane = iota(block.shape, 2)
    source2[2:20] = block
    for rows in (slice(0, 2), slice(20, 22)):
        density2[rows] = jnp.zeros((2, 24, 128), F32)
    density2[2:20] = jnp.where(lane < 32, pltpu.roll(block, 64, 2), 0.0)
    level = Level(density2, keep2, value2, 0)
    level.clear((0, 10))
    level.coefficients(source2, 16.0, 1, 9, 3)
    row = iota((8, 128), 0)
    near = near_ref[...]
    picked = []
    for i in range(9):
        y = at_y + i - 4
        inside = (y >= 0) & (y < devices)
        y = jnp.clip(y, 0, devices - 1)
        rows = jnp.sum(jnp.where(row == y % 8, near, 0.0), axis=1)
        rows = pltpu.roll(rows, (128 - 16 * (y // 8)) % 128, 1)
        picked.append(jnp.where(inside & (iota((12, 128), 1) < 16), rows, 0.0))
        picked.append(jnp.zeros((4, 128), F32))
    spread = dot(jnp.concatenate(picked, axis=0), doubling(16)).reshape(9, 16, 128)
    plane[0:9, pl.ds(0, 12, stride=2)] = spread[:, 0:12]
    plane[0:9, pl.ds(1, 12, stride=2)] = spread[:, 0:12]
    below = jnp.where(lane < 32, pltpu.roll(block, 96, 2), 0.0).reshape(9, 2, 24, 128)[:, 0]
    value2[1, 1:10] = below + plane[0:9, 0:24]
    level.half(0, 1, 9, 3)
    level.half(1, 2, 7, 7)
    level.half(0, 2, 7, 7)
    level.half(1, 3, 5, 5)
    even, odd = level.rows(value2[0, 3:8], value2[1, 3:8])

    blocks(0, 20, 4, lambda r: folded(kept_ref, pl.ds(r, 4), source1, density1, pl.ds(r, 4)))
    level = Level(density1, keep1, value1, 64, 64)
    level.coefficients(source1, 4.0, 1, 8, 2)
    rows = jnp.stack([even, odd], axis=1).reshape(240, 128)
    spread = dot(rows, doubling(32, 0, 64)).reshape(10, 24, 128)
    plane[0:10, pl.ds(0, 24, stride=2)] = spread
    plane[0:10, pl.ds(1, 24, stride=2)] = spread
    left = iota((10, 24, 128), 2) < 64
    value1[1] = below1_ref[...] + jnp.where(left, plane[0:10, 0:24], plane[0:10, 24:48])
    level.clear_red((0, 9))
    level.half(0, 1, 8, 4)
    level.half(1, 1, 8, 4)
    level.half(0, 2, 6, 6)
    level.half(1, 2, 6, 6)
    even, odd = level.rows(value1[0, 2:8], value1[1, 2:8])
    rows = jnp.stack([even, odd], axis=1).reshape(12, 24, 128)[1:11]

    finest_window(s_ref, d_ref, rim_before_ref, rim_after_ref, source0, density0)
    level = Level(density0, keep0, value0, 128)
    level.coefficients(source0, 1.0, 1, 8, 1)
    near = dot(rows[:, 8:24].reshape(160, 128), doubling(64)).reshape(10, 16, 128)
    far = dot(rows[:, 0:16].reshape(160, 128), doubling(64, 64)).reshape(10, 16, 128)
    for start, part in ((0, near), (32, far)):
        plane[0:10, pl.ds(start, 16, stride=2)] = part
        plane[0:10, pl.ds(start + 1, 16, stride=2)] = part
    value0[1] = plane[...]
    value0[1, 0:3, 8:56] = value0[1, 0:3, 8:56] + before_ref[...]
    value0[1, 3:7] = value0[1, 3:7] + below0_ref[...]
    value0[1, 7:10, 8:56] = value0[1, 7:10, 8:56] + after_ref[...]
    level.clear_red((0, 9))
    level.half(0, 1, 8, 2)
    level.half(1, 1, 8, 2)
    level.half(0, 2, 6, 2)
    level.half(1, 2, 6, 2)
    even, odd = level.rows(value0[0, 3:7, 16:48], value0[1, 3:7, 16:48])
    pressure_ref[...] = jnp.swapaxes(jnp.stack([even, odd], axis=1).reshape(8, 32, 128), 0, 1)

    def remaining(j):
        red, black = level.residual(1.0, 3 + j, 1)
        even, odd = level.rows(red, black)
        plane[pl.ds(2 * j, 1)] = even
        plane[pl.ds(2 * j + 1, 1)] = odd

    blocks(0, 4, 1, remaining)
    remain_ref[...] = jnp.swapaxes(plane[0:8, 16:48], 0, 1)


def pair(array_up, array_down, axis, group=1):
    groups = lax.axis_size(axis) // group
    up = [(i * group + j, (i + 2) * group - 1 - j) for i in range(groups - 1) for j in range(group)]
    down = [(j, i) for i, j in up]
    return lax.ppermute(array_up, axis, up), lax.ppermute(array_down, axis, down)


def shape(*sizes):
    return jax.ShapeDtypeStruct(sizes, F32)


def vmem(*sizes):
    return pltpu.VMEM(sizes, F32)


def params():
    return pltpu.CompilerParams(vmem_limit_bytes=24 * 1024 * 1024)


def body(right_side, labels):
    gz, xy = lax.axis_size("gz"), lax.axis_size("xy")
    density = jnp.where(labels == 1, gas_density, 1.0).astype(F32)
    before, after = pair(
        jnp.concatenate([right_side[-8:], density[-9:]], axis=0),
        jnp.concatenate([right_side[:8], density[:9]], axis=0),
        "gz",
    )
    zeros = jnp.zeros((8, 8, 128), F32)
    wide_source = jnp.concatenate([zeros, before[:8], right_side, after[:8], zeros], axis=0)
    wide_density = jnp.concatenate([zeros[:7], before[8:], density, after[8:], zeros[:7]], axis=0)
    wide_source = jnp.swapaxes(wide_source, 0, 1)
    wide_density = jnp.swapaxes(wide_density, 0, 1)
    before, after = pair(
        jnp.concatenate([wide_source[3:, 8:56], wide_density[3:, 8:56]], axis=0),
        jnp.concatenate([wide_source[:5, 8:56], wide_density[:5, 8:56]], axis=0),
        "xy",
    )
    finest = (wide_source, wide_density, before, after)
    at_group = lax.axis_index("xy") % GROUP
    place = jnp.stack([lax.axis_index("gz"), lax.axis_index("xy"), at_group]).astype(jnp.int32)
    smem, block = pl.BlockSpec(memory_space=pltpu.SMEM), pl.BlockSpec(memory_space=pltpu.VMEM)
    chunks, first_rows, last_rows, below0 = pl.pallas_call(
        finest_down,
        out_shape=[shape(GROUP, 208, 128), shape(144, 128), shape(144, 128), shape(4, 64, 128)],
        in_specs=[smem] + [block] * 4,
        scratch_shapes=[vmem(20, 64, 128)] * 2 + [vmem(KEPT, 10, 64, 128), vmem(2, 10, 64, 128), vmem(8, 32, 128)],
        compiler_params=params(),
    )(place, *finest)

    teams = [[GROUP * i + j for j in range(GROUP)] for i in range(xy // GROUP)]
    chunks = lax.all_to_all(chunks, "xy", 0, 0, axis_index_groups=teams, tiled=True)
    window = chunks[:, :64].reshape(4 * GROUP * 16, 128)
    before, after = pair(
        jnp.concatenate([window[-208:], last_rows], axis=0),
        jnp.concatenate([window[:208], first_rows], axis=0),
        "xy",
        GROUP,
    )
    rims = jnp.concatenate([before[None, 208:], chunks[:, 64:], after[None, 208:]], axis=0)
    value_before = lax.dynamic_index_in_dim(rims, at_group, 0, keepdims=False).reshape(3, 48, 128)
    value_after = lax.dynamic_index_in_dim(rims, at_group + 2, 0, keepdims=False).reshape(3, 48, 128)
    window = jnp.concatenate([before[:208], window, after[:208]], axis=0).reshape(-1, 16, 128)

    def faces(near):
        parts = (window[8:34], window[:8, near], window[34:, near])
        return jnp.concatenate([part.reshape(-1, 128) for part in parts], axis=0)

    before, after = pair(faces(slice(8, 16)), faces(slice(0, 8)), "gz")
    chunks, kept, below1 = pl.pallas_call(
        middle_down,
        out_shape=[shape(gz, 72, 128), shape(20, 48, 128), shape(10, 24, 128)],
        in_specs=[smem] + [block] * 3,
        scratch_shapes=[vmem(44, 48, 128)]
        + [vmem(44, 24, 128)] * 2
        + [vmem(KEPT, 22, 24, 128), vmem(2, 22, 24, 128), vmem(34, 32, 128)]
        + [vmem(20, 24, 128)] * 2
        + [vmem(KEPT, 10, 24, 128), vmem(2, 10, 24, 128)],
        compiler_params=params(),
    )(place, window, before, after)

    column = lax.all_to_all(chunks, "gz", 0, 0, tiled=True)
    peers = [[GROUP * i + j for i in range(xy // GROUP)] for j in range(GROUP)]
    everywhere = lax.all_to_all(
        jnp.broadcast_to(column[None, :, 64:68], (xy // GROUP, gz, 4, 128)), "xy", 0, 0, axis_index_groups=peers, tiled=True
    )
    halo = jnp.pad(column[:, :64], ((1, 1), (0, 0), (0, 0)))
    halo = lax.dynamic_slice(halo, (lax.axis_index("gz"), 0, 0), (3, 64, 128)).reshape(3, 8, 8, 128)
    halo = jnp.swapaxes(halo, 0, 1).reshape(8, 24, 128)
    before, after = pair(halo, halo, "xy", GROUP)
    halo = jnp.concatenate([before, halo, after], axis=0)
    planes = 4 * gz
    near = pl.pallas_call(
        partial(coarsest, planes),
        out_shape=shape(12, 8, 128),
        in_specs=[smem, block],
        scratch_shapes=[vmem(planes + 4, 8, 128)] * 2
        + [vmem(KEPT, planes // 2 + 2, 8, 128), vmem(2, planes // 2 + 2, 8, 128), vmem(planes + 8, 8, 128)],
        compiler_params=params(),
        cost_estimate=pl.CostEstimate(flops=100_000_000, bytes_accessed=16_000_000, transcendentals=0),
    )(place, everywhere)
    return pl.pallas_call(
        partial(way_up, xy),
        out_shape=[shape(32, 8, 128)] * 2,
        in_specs=[smem] + [block] * 11,
        scratch_shapes=[vmem(22, 24, 128)] * 2
        + [vmem(KEPT, 11, 24, 128), vmem(2, 11, 24, 128)]
        + [vmem(20, 24, 128)] * 2
        + [vmem(KEPT, 10, 24, 128), vmem(2, 10, 24, 128)]
        + [vmem(20, 64, 128)] * 2
        + [vmem(KEPT, 10, 64, 128), vmem(2, 10, 64, 128), vmem(10, 64, 128)],
        compiler_params=params(),
    )(place, near, halo, kept, below1, *finest, below0, value_before, value_after)


def solution(mesh):
    return jax.shard_map(
        body,
        mesh=mesh,
        in_specs=(P("gz", "xy", None), P("gz", "xy", None)),
        out_specs=(P("gz", "xy", None), P("gz", "xy", None)),
        check_vma=False,
    )
```

```python
from functools import partial

import jax
import jax.numpy as jnp
from jax import lax
from jax.experimental import pallas as pl
from jax.experimental.pallas import tpu as pltpu
from jax.sharding import PartitionSpec as P

gas_density = 0.001
least = 1e-4
F32 = jnp.float32
GROUP = 4


def dot(a, b):
    return lax.dot_general(
        a, b, (((1,), (0,)), ((), ())), precision=lax.Precision.HIGHEST, preferred_element_type=F32
    )


def iota(shape, axis):
    return lax.broadcasted_iota(jnp.int32, shape, axis)


def halving(offset, weight, width=128):
    row, column = iota((128, 128), 0), iota((128, 128), 1)
    return jnp.where((row // 2 + offset == column) & (row < width), weight, 0.0).astype(F32)


def doubling(width, first=0, period=128):
    row, column = iota((128, 128), 0), iota((128, 128), 1)
    hit = ((column % period) // 2 + first == row) & (row < first + width)
    return jnp.where(hit, 1.0, 0.0).astype(F32)


def inverse(a):
    return pl.reciprocal(a, approx=True)


def blocks(lo, count, block, step):
    assert count % block == 0
    if count == block:
        step(lo)
    else:

        def turn(i, _):
            step(lo + i * block)
            return 0

        lax.fori_loop(0, count // block, turn, 0)


LOWER, UPPER, LEFT, RIGHT, OUT, INNER, INVERSE, DIAGONAL, SOURCE = 0, 2, 4, 6, 8, 10, 11, 13, 15
KEPT = 17


class Level:
    def __init__(self, density, keep, value, width, cross=0, ends=False):
        self.density, self.keep, self.value = density, keep, value
        self.depth, self.width, self.cross, self.ends = value.shape[2], width, cross, ends
        self.row, self.lane = iota((1, 8, 128), 1), iota((1, 8, 128), 2)
        self.odd = (self.row + self.lane) % 2 == 1

    def choose(self, mask, a, b):
        if not isinstance(a, float):
            shape, a = a.shape, a.reshape(-1, 8, 128)
        if not isinstance(b, float):
            shape, b = b.shape, b.reshape(-1, 8, 128)
        return jnp.where(mask, a, b).reshape(shape)

    def low(self, a):
        turned = pltpu.roll(a, 1, 1)
        if self.cross:
            head = turned[:, :8]
            head = jnp.where(self.row == 0, pltpu.roll(head, self.cross, 2), head)
            turned = head if self.depth == 8 else jnp.concatenate([head, turned[:, 8:]], axis=1)
        return turned

    def high(self, a):
        turned = pltpu.roll(a, self.depth - 1, 1)
        if self.cross:
            tail = turned[:, -8:]
            tail = jnp.where(self.row == 7, pltpu.roll(tail, 128 - self.cross, 2), tail)
            turned = tail if self.depth == 8 else jnp.concatenate([turned[:, :-8], tail], axis=1)
        return turned

    def coefficients(self, source, factor, lo, count, block):
        first_x, last_x = self.lane % max(self.width, 1) == 0, self.lane % max(self.width, 1) == self.width - 1
        if self.ends:
            first, last = (self.row == 0) & (self.lane < self.width), (self.row == 7) & (self.lane >= 128 - self.width)

        def coupling(a, b):
            return 2.0 * inverse(jnp.maximum(a + b, least))

        def both(place, at, even, odd):
            self.keep[place, at] = self.choose(self.odd, odd, even)
            self.keep[place + 1, at] = self.choose(self.odd, even, odd)

        def step(j):
            at = pl.ds(j, block)
            shape = (block, 2, self.depth, 128)
            rows = self.density[pl.ds(2 * j, 2 * block)].reshape(shape)
            before = self.density[pl.ds(2 * j - 1, 2 * block)].reshape(shape)[:, 0]
            after = self.density[pl.ds(2 * j + 1, 2 * block)].reshape(shape)[:, 1]
            inner = coupling(rows[:, 0], rows[:, 1])
            out = (coupling(rows[:, 0], before), coupling(rows[:, 1], after))
            parts = []
            for k in range(2):
                d = rows[:, k]
                if self.width or self.ends:
                    edge = 2.0 * inverse(jnp.maximum(d, least))
                lower = coupling(d, self.low(d))
                upper = self.high(lower)
                if self.ends:
                    lower, upper = self.choose(first, edge, lower), self.choose(last, edge, upper)
                left = coupling(d, pltpu.roll(d, 1, 2))
                right = pltpu.roll(left, 127, 2)
                if self.width:
                    left, right = self.choose(first_x, edge, left), self.choose(last_x, edge, right)
                total = lower + upper + (out[0] + inner if k == 0 else inner + out[1]) + left + right
                if self.ends:
                    lower, upper = self.choose(first, 0.0, lower), self.choose(last, 0.0, upper)
                if self.width:
                    left, right = self.choose(first_x, 0.0, left), self.choose(last_x, 0.0, right)
                parts.append((lower, upper, left, right, jnp.where(d > 0.0, inverse(total), 0.0), total))
            for place, even, odd in zip((LOWER, UPPER, LEFT, RIGHT, INVERSE, DIAGONAL), *parts):
                both(place, at, even, odd)
            both(OUT, at, out[0], out[1])
            self.keep[INNER, at] = inner
            if source is not None:
                rows = factor * source[pl.ds(2 * j, 2 * block)].reshape(shape)
                both(SOURCE, at, rows[:, 0], rows[:, 1])

        blocks(lo, count, block, step)

    def gathered(self, colour, j, block):
        at, keep = pl.ds(j, block), self.keep
        other = self.value.at[1 - colour]
        w = other[at]
        mask = self.odd if colour else jnp.logical_not(self.odd)
        side = self.choose(mask, other[pl.ds(j - 1, block)], other[pl.ds(j + 1, block)])
        total = keep[INNER, at] * w + keep[OUT + colour, at] * side
        total += keep[LOWER + colour, at] * self.low(w) + keep[UPPER + colour, at] * self.high(w)
        total += keep[LEFT + colour, at] * pltpu.roll(w, 1, 2) + keep[RIGHT + colour, at] * pltpu.roll(w, 127, 2)
        return total

    def first(self, lo, count, block):
        def step(j):
            at = pl.ds(j, block)
            self.value[0, at] = self.keep[SOURCE, at] * self.keep[INVERSE, at]

        blocks(lo, count, block, step)

    def half(self, colour, lo, count, block):
        def step(j):
            at = pl.ds(j, block)
            total = self.keep[SOURCE + colour, at] + self.gathered(colour, j, block)
            self.value[colour, at] = total * self.keep[INVERSE + colour, at]

        blocks(lo, count, block, step)

    def residual(self, factor, j, block):
        at, out = pl.ds(j, block), []
        for colour in (0, 1):
            total = self.keep[DIAGONAL + colour, at] * self.value[colour, at] - self.gathered(colour, j, block)
            out.append((self.keep[SOURCE + colour, at] - total) * (1.0 / factor))
        return out

    def rows(self, red, black):
        return self.choose(self.odd, black, red), self.choose(self.odd, red, black)

    def clear_red(self, pairs):
        for j in pairs:
            self.value[0, j] = jnp.zeros((self.depth, 128), F32)

    def clear(self, pairs):
        for j in pairs:
            self.value[:, j] = jnp.zeros((2, self.depth, 128), F32)


def finest_rims(right_ref, labels_ref, before_ref, after_ref, s_ref, d_ref, low_ref, high_ref, source, density):
    for ref, near in ((source, 8), (density, 7)):
        ref[0:near] = jnp.zeros((near, 8, 128), F32)
        ref[64 - near : 64] = jnp.zeros((near, 8, 128), F32)
    source[8:16] = before_ref[0:8]
    source[48:56] = after_ref[0:8]
    source[16:48] = right_ref[...]
    density[7:16] = before_ref[8:17]
    density[48:57] = after_ref[8:17]
    density[16:48] = jnp.where(labels_ref[...] == 1, gas_density, 1.0)
    for start, wide, out in ((0, source, s_ref), (5, density, d_ref)):
        rows = jnp.swapaxes(wide[...], 0, 1)
        out[...] = rows
        low_ref[start : start + 5] = rows[0:5, 8:56]
        high_ref[start : start + 5] = rows[3:8, 8:56]


def finest_window(s_ref, d_ref, before_ref, after_ref, source, density):
    for ref in (source, density):
        for rows in (pl.ds(0, 6), pl.ds(14, 6)):
            ref[rows] = jnp.zeros((6, 64, 128), F32)
    source[1:6, 8:56] = before_ref[0:5]
    source[14:19, 8:56] = after_ref[0:5]
    density[1:6, 8:56] = before_ref[5:10]
    density[14:19, 8:56] = after_ref[5:10]
    source[6:14] = s_ref[...]
    density[6:14] = d_ref[...]


def finest_down(s_ref, d_ref, before_ref, after_ref, chunk_ref, low_ref, high_ref, below_ref,
                source, density, keep, value, plane):
    finest_window(s_ref, d_ref, before_ref, after_ref, source, density)
    level = Level(density, keep, value, 128)
    level.clear((0, 9))
    value[1, 1] = jnp.zeros((64, 128), F32)
    value[1, 8] = jnp.zeros((64, 128), F32)
    level.coefficients(source, 1.0, 1, 8, 1)
    level.first(1, 8, 2)
    level.half(1, 1, 8, 2)
    level.half(0, 2, 6, 2)
    level.half(1, 2, 6, 2)

    def pooling(j):
        red, black = level.residual(1.0, 3 + j, 1)
        plane[pl.ds(j, 1)] = (red + black)[:, 16:48]
        plane[pl.ds(4 + j, 1)] = (density[pl.ds(6 + 2 * j, 1)] + density[pl.ds(7 + 2 * j, 1)])[:, 16:48]

    blocks(0, 4, 1, pooling)
    pooled = plane[:, pl.ds(0, 16, stride=2)] + plane[:, pl.ds(1, 16, stride=2)]
    out = dot(pooled[:4].reshape(64, 128), halving(0, 0.125)) + dot(pooled[4:].reshape(64, 128), halving(64, 0.125))
    low_ref[...] = value[1, 3:6, 8:56]
    high_ref[...] = value[1, 4:7, 8:56]
    for peer in range(GROUP):
        chunk_ref[peer] = out
    below_ref[...] = value[1, 3:7]


def folded(ref, rows, source, density, start):
    block = ref[rows]
    near, far = block[:, :24], block[:, 24:]
    left = iota(near.shape, 2) < 64
    source[start] = jnp.where(left, near, pltpu.roll(far, 64, 2))
    density[start] = jnp.where(left, pltpu.roll(near, 64, 2), far)


def middle_down(place_ref, window_ref, before_ref, after_ref, chunk_ref, kept_ref, below_ref,
                window, source, density, keep, value, plane, source2, density2, keep2, value2):
    window[1:43, 16:32] = window_ref[...]
    for ref, near, far in ((before_ref, 0, 8), (after_ref, 32, 32)):
        window[9:35, near : near + 16] = ref[0:416].reshape(26, 16, 128)
        for start, rows in ((1, 416), (35, 480)):
            window[start : start + 8, far : far + 8] = ref[rows : rows + 64].reshape(8, 8, 128)
            clear = 0 if near == 0 else 40
            window[start : start + 8, clear : clear + 8] = jnp.zeros((8, 8, 128), F32)
    for row in (0, 43):
        window[row] = jnp.zeros((48, 128), F32)
    blocks(0, 44, 4, lambda r: folded(window, pl.ds(r, 4), source, density, pl.ds(r, 4)))
    level = Level(density, keep, value, 64, 64)
    level.clear((0, 21))
    for j in (1, 20):
        value[1, j] = jnp.zeros((24, 128), F32)
    level.coefficients(source, 4.0, 1, 20, 2)
    level.first(1, 20, 5)
    level.half(1, 1, 20, 5)
    level.half(0, 2, 18, 6)
    level.half(1, 2, 18, 6)
    kept_ref[...] = window[pl.ds(6 + 4 * place_ref[2], 20)]
    below_ref[...] = value[1, pl.ds(3 + 2 * place_ref[2], 10)]

    def pooling(j):
        red, black = level.residual(4.0, 3 + j, 4)
        plane[pl.ds(j, 4), 0:24] = red + black

    blocks(0, 16, 4, pooling)
    rows = density[4:40].reshape(18, 2, 24, 128)
    plane[16:34, 0:24] = rows[:, 0] + rows[:, 1]
    pooled = plane[:, pl.ds(0, 16, stride=2)] + plane[:, pl.ds(1, 16, stride=2)]
    pooled = dot(pooled.reshape(34 * 16, 128), halving(0, 0.125)).reshape(34, 16, 128)
    lane = iota((34, 16, 128), 2)
    near, far = jnp.where(lane < 32, pooled, 0.0), jnp.where(lane < 32, pltpu.roll(pooled, 96, 2), 0.0)
    for ref, start, parts in ((source2, 2, slice(0, 16)), (density2, 1, slice(16, 34))):
        ref[start : start + parts.stop - parts.start, 0:12] = near[parts, 0:12]
        ref[start : start + parts.stop - parts.start, 12:24] = far[parts, 0:12]
    for row in (0, 19):
        density2[row] = jnp.zeros((24, 128), F32)
    below = Level(density2, keep2, value2, 0)
    below.clear((0, 9))
    for j in (1, 8):
        value2[1, j] = jnp.zeros((24, 128), F32)
    below.coefficients(source2, 16.0, 1, 8, 2)
    below.first(1, 8, 8)
    below.half(1, 1, 8, 4)
    below.half(0, 2, 6, 6)
    below.half(1, 2, 6, 6)
    red, black = below.residual(16.0, 3, 4)
    plane[0:4, 0:24] = red + black
    rows = density2[6:14].reshape(4, 2, 24, 128)
    plane[4:8, 0:24] = rows[:, 0] + rows[:, 1]
    rows = []
    for row in range(4):
        for part in (row, 4 + row):
            rows.append(plane[part, pl.ds(8, 4, stride=2)] + plane[part, pl.ds(9, 4, stride=2)])
    pooled = dot(jnp.concatenate(rows, axis=0), halving(0, 0.125, 32))
    for row in range(4):
        total = pooled[8 * row : 8 * row + 1]
        for i in range(1, 8):
            total = total + pltpu.roll(pooled[8 * row + i : 8 * row + i + 1], 16 * i, 1)
        chunk_ref[0, 64 + row : 65 + row] = total
    for j in range(4):
        for k in range(2):
            row = 6 + 2 * j + k
            total = source2[row, 8:16] + pltpu.roll(density2[row, 8:16], 64, 1)
            if k == 0:
                total = total + pltpu.roll(value2[1, 3 + j, 8:16], 32, 1)
            chunk_ref[0, 8 * (2 * j + k) : 8 * (2 * j + k) + 8] = total
    chunk_ref[0, 68:72] = jnp.zeros((4, 128), F32)
    for peer in range(1, chunk_ref.shape[0]):
        chunk_ref[peer] = chunk_ref[0]


def coarsest(planes, place_ref, gathered_ref, near_ref, source, density, keep, value, wide):
    groups = gathered_ref.shape[0]
    lane = iota((8, 128), 1)
    for row in (0, 1, planes + 2, planes + 3):
        density[row] = jnp.zeros((8, 128), F32)

    def spread(g, _):
        tiles = [
            jnp.concatenate([gathered_ref[2 * h, g], gathered_ref[2 * h + 1, g]], axis=0) for h in range(groups // 2)
        ]
        for part, ref in enumerate((source, density)):
            for z in range(4):
                out = jnp.zeros((8, 128), F32)
                for h, block in enumerate(tiles):
                    moved = pltpu.roll(block, (16 * (h - z) - 64 * part) % 128, 1)
                    out = jnp.where(lane // 16 == h, moved, out)
                ref[2 + 4 * g + z] = out
        return 0

    lax.fori_loop(0, planes // 4, spread, 0)
    level = Level(density, keep, value, 16, 16, ends=True)
    pairs = planes // 2
    value[...] = jnp.zeros(value.shape, F32)
    level.coefficients(source, 64.0, 1, pairs, 4)

    def sweep(_, carry):
        level.half(0, 1, pairs, pairs)
        level.half(1, 1, pairs, pairs)
        return carry

    lax.fori_loop(0, 12, sweep, 0)
    wide[0:4] = jnp.zeros((4, 8, 128), F32)
    wide[planes + 4 : planes + 8] = jnp.zeros((4, 8, 128), F32)
    even, odd = level.rows(value[0, 1 : pairs + 1], value[1, 1 : pairs + 1])
    for j in range(pairs):
        wide[4 + 2 * j] = even[j]
        wide[5 + 2 * j] = odd[j]
    near_ref[...] = wide[pl.ds(4 * place_ref[0], 12)]


def way_up(devices, place_ref, near_ref, halo_ref, kept_ref, below1_ref,
           s_ref, d_ref, rim_before_ref, rim_after_ref, below0_ref, before_ref, after_ref,
           pressure_ref, remain_ref,
           source2, density2, keep2, value2, source1, density1, keep1, value1,
           source0, density0, keep0, value0, plane):
    at_y, at_group = place_ref[1], place_ref[2]

    block = halo_ref[pl.ds(2 * at_group, 18)]
    lane = iota(block.shape, 2)
    source2[2:20] = block
    for rows in (slice(0, 2), slice(20, 22)):
        density2[rows] = jnp.zeros((2, 24, 128), F32)
    density2[2:20] = jnp.where(lane < 32, pltpu.roll(block, 64, 2), 0.0)
    level = Level(density2, keep2, value2, 0)
    level.clear((0, 10))
    level.coefficients(source2, 16.0, 1, 9, 3)
    row = iota((8, 128), 0)
    near = near_ref[...]
    picked = []
    for i in range(9):
        y = at_y + i - 4
        inside = (y >= 0) & (y < devices)
        y = jnp.clip(y, 0, devices - 1)
        rows = jnp.sum(jnp.where(row == y % 8, near, 0.0), axis=1)
        rows = pltpu.roll(rows, (128 - 16 * (y // 8)) % 128, 1)
        picked.append(jnp.where(inside & (iota((12, 128), 1) < 16), rows, 0.0))
        picked.append(jnp.zeros((4, 128), F32))
    spread = dot(jnp.concatenate(picked, axis=0), doubling(16)).reshape(9, 16, 128)
    plane[0:9, pl.ds(0, 12, stride=2)] = spread[:, 0:12]
    plane[0:9, pl.ds(1, 12, stride=2)] = spread[:, 0:12]
    below = jnp.where(lane < 32, pltpu.roll(block, 96, 2), 0.0).reshape(9, 2, 24, 128)[:, 0]
    value2[1, 1:10] = below + plane[0:9, 0:24]
    level.half(0, 1, 9, 3)
    level.half(1, 2, 7, 7)
    level.half(0, 2, 7, 7)
    level.half(1, 3, 5, 5)
    even, odd = level.rows(value2[0, 3:8], value2[1, 3:8])

    blocks(0, 20, 4, lambda r: folded(kept_ref, pl.ds(r, 4), source1, density1, pl.ds(r, 4)))
    level = Level(density1, keep1, value1, 64, 64)
    level.coefficients(source1, 4.0, 1, 8, 2)
    rows = jnp.stack([even, odd], axis=1).reshape(240, 128)
    spread = dot(rows, doubling(32, 0, 64)).reshape(10, 24, 128)
    plane[0:10, pl.ds(0, 24, stride=2)] = spread
    plane[0:10, pl.ds(1, 24, stride=2)] = spread
    left = iota((10, 24, 128), 2) < 64
    value1[1] = below1_ref[...] + jnp.where(left, plane[0:10, 0:24], plane[0:10, 24:48])
    level.clear_red((0, 9))
    level.half(0, 1, 8, 4)
    level.half(1, 1, 8, 4)
    level.half(0, 2, 6, 6)
    level.half(1, 2, 6, 6)
    even, odd = level.rows(value1[0, 2:8], value1[1, 2:8])
    rows = jnp.stack([even, odd], axis=1).reshape(12, 24, 128)[1:11]

    finest_window(s_ref, d_ref, rim_before_ref, rim_after_ref, source0, density0)
    level = Level(density0, keep0, value0, 128)
    level.coefficients(source0, 1.0, 1, 8, 1)
    near = dot(rows[:, 8:24].reshape(160, 128), doubling(64)).reshape(10, 16, 128)
    far = dot(rows[:, 0:16].reshape(160, 128), doubling(64, 64)).reshape(10, 16, 128)
    for start, part in ((0, near), (32, far)):
        plane[0:10, pl.ds(start, 16, stride=2)] = part
        plane[0:10, pl.ds(start + 1, 16, stride=2)] = part
    value0[1] = plane[...]
    value0[1, 0:3, 8:56] = value0[1, 0:3, 8:56] + before_ref[...]
    value0[1, 3:7] = value0[1, 3:7] + below0_ref[...]
    value0[1, 7:10, 8:56] = value0[1, 7:10, 8:56] + after_ref[...]
    level.clear_red((0, 9))
    level.half(0, 1, 8, 2)
    level.half(1, 1, 8, 2)
    level.half(0, 2, 6, 2)
    level.half(1, 2, 6, 2)
    even, odd = level.rows(value0[0, 3:7, 16:48], value0[1, 3:7, 16:48])
    pressure_ref[...] = jnp.swapaxes(jnp.stack([even, odd], axis=1).reshape(8, 32, 128), 0, 1)

    def remaining(j):
        red, black = level.residual(1.0, 3 + j, 1)
        even, odd = level.rows(red, black)
        plane[pl.ds(2 * j, 1)] = even
        plane[pl.ds(2 * j + 1, 1)] = odd

    blocks(0, 4, 1, remaining)
    remain_ref[...] = jnp.swapaxes(plane[0:8, 16:48], 0, 1)


def pair(array_up, array_down, axis, group=1):
    groups = lax.axis_size(axis) // group
    up = [(i * group + j, (i + 2) * group - 1 - j) for i in range(groups - 1) for j in range(group)]
    down = [(j, i) for i, j in up]
    return lax.ppermute(array_up, axis, up), lax.ppermute(array_down, axis, down)


def shape(*sizes):
    return jax.ShapeDtypeStruct(sizes, F32)


def vmem(*sizes):
    return pltpu.VMEM(sizes, F32)


def params():
    return pltpu.CompilerParams(vmem_limit_bytes=24 * 1024 * 1024)


def body(right_side, labels):
    gz, xy = lax.axis_size("gz"), lax.axis_size("xy")
    density = jnp.where(labels == 1, gas_density, 1.0).astype(F32)
    before, after = pair(
        jnp.concatenate([right_side[-8:], density[-9:]], axis=0),
        jnp.concatenate([right_side[:8], density[:9]], axis=0),
        "gz",
    )
    wide_source, wide_density, low_rim, high_rim = pl.pallas_call(
        finest_rims,
        out_shape=[shape(8, 64, 128)] * 2 + [shape(10, 48, 128)] * 2,
        scratch_shapes=[vmem(64, 8, 128)] * 2,
        compiler_params=params(),
    )(right_side, labels, before, after)
    before, after = pair(high_rim, low_rim, "xy")
    finest = (wide_source, wide_density, before, after)
    at_group = lax.axis_index("xy") % GROUP
    place = jnp.stack([lax.axis_index("gz"), lax.axis_index("xy"), at_group]).astype(jnp.int32)
    smem, block = pl.BlockSpec(memory_space=pltpu.SMEM), pl.BlockSpec(memory_space=pltpu.VMEM)
    chunks, first_rows, last_rows, below0 = pl.pallas_call(
        finest_down,
        out_shape=[shape(GROUP, 64, 128), shape(3, 48, 128), shape(3, 48, 128), shape(4, 64, 128)],
        scratch_shapes=[vmem(20, 64, 128)] * 2 + [vmem(KEPT, 10, 64, 128), vmem(2, 10, 64, 128), vmem(8, 32, 128)],
        compiler_params=params(),
    )(*finest)

    teams = [[GROUP * i + j for j in range(GROUP)] for i in range(xy // GROUP)]
    chunks = lax.all_to_all(chunks, "xy", 0, 0, axis_index_groups=teams, tiled=True)
    window = chunks.reshape(4 * GROUP, 16, 128)
    before, after = pair(window[-13:], window[:13], "xy", GROUP)
    window = jnp.concatenate([before, window, after], axis=0)

    def faces(near):
        parts = (window[8:34], window[:8, near], window[34:, near])
        return jnp.concatenate([part.reshape(-1, 128) for part in parts], axis=0)

    before, after = pair(faces(slice(8, 16)), faces(slice(0, 8)), "gz")
    chunks, kept, below1 = pl.pallas_call(
        middle_down,
        out_shape=[shape(gz, 72, 128), shape(20, 48, 128), shape(10, 24, 128)],
        in_specs=[smem] + [block] * 3,
        scratch_shapes=[vmem(44, 48, 128)]
        + [vmem(44, 24, 128)] * 2
        + [vmem(KEPT, 22, 24, 128), vmem(2, 22, 24, 128), vmem(34, 32, 128)]
        + [vmem(20, 24, 128)] * 2
        + [vmem(KEPT, 10, 24, 128), vmem(2, 10, 24, 128)],
        compiler_params=params(),
    )(place, window, before, after)

    value_before, value_after = pair(last_rows, first_rows, "xy")
    column = lax.all_to_all(chunks, "gz", 0, 0, tiled=True)
    peers = [[GROUP * i + j for i in range(xy // GROUP)] for j in range(GROUP)]
    everywhere = lax.all_to_all(
        jnp.broadcast_to(column[None, :, 64:68], (xy // GROUP, gz, 4, 128)), "xy", 0, 0, axis_index_groups=peers, tiled=True
    )
    halo = jnp.pad(column[:, :64], ((1, 1), (0, 0), (0, 0)))
    halo = lax.dynamic_slice(halo, (lax.axis_index("gz"), 0, 0), (3, 64, 128)).reshape(3, 8, 8, 128)
    halo = jnp.swapaxes(halo, 0, 1).reshape(8, 24, 128)
    before, after = pair(halo, halo, "xy", GROUP)
    halo = jnp.concatenate([before, halo, after], axis=0)
    planes = 4 * gz
    near = pl.pallas_call(
        partial(coarsest, planes),
        out_shape=shape(12, 8, 128),
        in_specs=[smem, block],
        scratch_shapes=[vmem(planes + 4, 8, 128)] * 2
        + [vmem(KEPT, planes // 2 + 2, 8, 128), vmem(2, planes // 2 + 2, 8, 128), vmem(planes + 8, 8, 128)],
        compiler_params=params(),
        cost_estimate=pl.CostEstimate(flops=100_000_000, bytes_accessed=16_000_000, transcendentals=0),
    )(place, everywhere)
    return pl.pallas_call(
        partial(way_up, xy),
        out_shape=[shape(32, 8, 128)] * 2,
        in_specs=[smem] + [block] * 11,
        scratch_shapes=[vmem(22, 24, 128)] * 2
        + [vmem(KEPT, 11, 24, 128), vmem(2, 11, 24, 128)]
        + [vmem(20, 24, 128)] * 2
        + [vmem(KEPT, 10, 24, 128), vmem(2, 10, 24, 128)]
        + [vmem(20, 64, 128)] * 2
        + [vmem(KEPT, 10, 64, 128), vmem(2, 10, 64, 128), vmem(10, 64, 128)],
        compiler_params=params(),
    )(place, near, halo, kept, below1, *finest, below0, value_before, value_after)


def solution(mesh):
    return jax.shard_map(
        body,
        mesh=mesh,
        in_specs=(P("gz", "xy", None), P("gz", "xy", None)),
        out_specs=(P("gz", "xy", None), P("gz", "xy", None)),
        check_vma=False,
    )
```

```python
from functools import partial

import jax
import jax.numpy as jnp
from jax import lax
from jax.experimental import pallas as pl
from jax.experimental.pallas import tpu as pltpu
from jax.sharding import PartitionSpec as P

gas_density = 0.001
least = 1e-4
F32 = jnp.float32
GROUP = 4


def dot(a, b):
    return lax.dot_general(
        a, b, (((1,), (0,)), ((), ())), precision=lax.Precision.HIGHEST, preferred_element_type=F32
    )


def iota(shape, axis):
    return lax.broadcasted_iota(jnp.int32, shape, axis)


def halving(offset, weight, width=128):
    row, column = iota((128, 128), 0), iota((128, 128), 1)
    return jnp.where((row // 2 + offset == column) & (row < width), weight, 0.0).astype(F32)


def doubling(width, first=0, period=128):
    row, column = iota((128, 128), 0), iota((128, 128), 1)
    hit = ((column % period) // 2 + first == row) & (row < first + width)
    return jnp.where(hit, 1.0, 0.0).astype(F32)


def inverse(a):
    return pl.reciprocal(a, approx=True)


def blocks(lo, count, block, step):
    assert count % block == 0
    if count == block:
        step(lo)
    else:

        def turn(i, _):
            step(lo + i * block)
            return 0

        lax.fori_loop(0, count // block, turn, 0)


LOWER, UPPER, LEFT, RIGHT, OUT, INNER, INVERSE, DIAGONAL, SOURCE = 0, 2, 4, 6, 8, 10, 11, 13, 15
KEPT = 17


class Level:
    def __init__(self, density, keep, value, width, cross=0, ends=False):
        self.density, self.keep, self.value = density, keep, value
        self.depth, self.width, self.cross, self.ends = value.shape[2], width, cross, ends
        self.row, self.lane = iota((1, 8, 128), 1), iota((1, 8, 128), 2)
        self.odd = (self.row + self.lane) % 2 == 1

    def choose(self, mask, a, b):
        if not isinstance(a, float):
            shape, a = a.shape, a.reshape(-1, 8, 128)
        if not isinstance(b, float):
            shape, b = b.shape, b.reshape(-1, 8, 128)
        return jnp.where(mask, a, b).reshape(shape)

    def low(self, a):
        turned = pltpu.roll(a, 1, 1)
        if self.cross:
            head = turned[:, :8]
            head = jnp.where(self.row == 0, pltpu.roll(head, self.cross, 2), head)
            turned = head if self.depth == 8 else jnp.concatenate([head, turned[:, 8:]], axis=1)
        return turned

    def high(self, a):
        turned = pltpu.roll(a, self.depth - 1, 1)
        if self.cross:
            tail = turned[:, -8:]
            tail = jnp.where(self.row == 7, pltpu.roll(tail, 128 - self.cross, 2), tail)
            turned = tail if self.depth == 8 else jnp.concatenate([turned[:, :-8], tail], axis=1)
        return turned

    def coefficients(self, source, factor, lo, count, block):
        first_x, last_x = self.lane % max(self.width, 1) == 0, self.lane % max(self.width, 1) == self.width - 1
        if self.ends:
            first, last = (self.row == 0) & (self.lane < self.width), (self.row == 7) & (self.lane >= 128 - self.width)

        def coupling(a, b):
            return 2.0 * inverse(jnp.maximum(a + b, least))

        def both(place, at, even, odd):
            self.keep[place, at] = self.choose(self.odd, odd, even)
            self.keep[place + 1, at] = self.choose(self.odd, even, odd)

        def step(j):
            at = pl.ds(j, block)
            shape = (block, 2, self.depth, 128)
            rows = self.density[pl.ds(2 * j, 2 * block)].reshape(shape)
            before = self.density[pl.ds(2 * j - 1, 2 * block)].reshape(shape)[:, 0]
            after = self.density[pl.ds(2 * j + 1, 2 * block)].reshape(shape)[:, 1]
            inner = coupling(rows[:, 0], rows[:, 1])
            out = (coupling(rows[:, 0], before), coupling(rows[:, 1], after))
            parts = []
            for k in range(2):
                d = rows[:, k]
                if self.width or self.ends:
                    edge = 2.0 * inverse(jnp.maximum(d, least))
                lower = coupling(d, self.low(d))
                upper = self.high(lower)
                if self.ends:
                    lower, upper = self.choose(first, edge, lower), self.choose(last, edge, upper)
                left = coupling(d, pltpu.roll(d, 1, 2))
                right = pltpu.roll(left, 127, 2)
                if self.width:
                    left, right = self.choose(first_x, edge, left), self.choose(last_x, edge, right)
                total = lower + upper + (out[0] + inner if k == 0 else inner + out[1]) + left + right
                if self.ends:
                    lower, upper = self.choose(first, 0.0, lower), self.choose(last, 0.0, upper)
                if self.width:
                    left, right = self.choose(first_x, 0.0, left), self.choose(last_x, 0.0, right)
                parts.append((lower, upper, left, right, jnp.where(d > 0.0, inverse(total), 0.0), total))
            for place, even, odd in zip((LOWER, UPPER, LEFT, RIGHT, INVERSE, DIAGONAL), *parts):
                both(place, at, even, odd)
            both(OUT, at, out[0], out[1])
            self.keep[INNER, at] = inner
            if source is not None:
                rows = factor * source[pl.ds(2 * j, 2 * block)].reshape(shape)
                both(SOURCE, at, rows[:, 0], rows[:, 1])

        blocks(lo, count, block, step)

    def gathered(self, colour, j, block):
        at, keep = pl.ds(j, block), self.keep
        other = self.value.at[1 - colour]
        w = other[at]
        before, after = other[pl.ds(j - 1, block)], other[pl.ds(j + 1, block)]
        side = self.choose(self.odd, before, after) if colour else self.choose(self.odd, after, before)
        total = keep[INNER, at] * w + keep[OUT + colour, at] * side
        total += keep[LOWER + colour, at] * self.low(w) + keep[UPPER + colour, at] * self.high(w)
        total += keep[LEFT + colour, at] * pltpu.roll(w, 1, 2) + keep[RIGHT + colour, at] * pltpu.roll(w, 127, 2)
        return total

    def first(self, lo, count, block):
        def step(j):
            at = pl.ds(j, block)
            self.value[0, at] = self.keep[SOURCE, at] * self.keep[INVERSE, at]

        blocks(lo, count, block, step)

    def half(self, colour, lo, count, block):
        def step(j):
            at = pl.ds(j, block)
            total = self.keep[SOURCE + colour, at] + self.gathered(colour, j, block)
            self.value[colour, at] = total * self.keep[INVERSE + colour, at]

        blocks(lo, count, block, step)

    def residual(self, factor, j, block):
        at, out = pl.ds(j, block), []
        for colour in (0, 1):
            total = self.keep[DIAGONAL + colour, at] * self.value[colour, at] - self.gathered(colour, j, block)
            out.append((self.keep[SOURCE + colour, at] - total) * (1.0 / factor))
        return out

    def rows(self, red, black):
        return self.choose(self.odd, black, red), self.choose(self.odd, red, black)

    def clear_red(self, pairs):
        for j in pairs:
            self.value[0, j] = jnp.zeros((self.depth, 128), F32)

    def clear(self, pairs):
        for j in pairs:
            self.value[:, j] = jnp.zeros((2, self.depth, 128), F32)


def finest_rims(right_ref, labels_ref, before_ref, after_ref, s_ref, d_ref, low_ref, high_ref, source, density):
    for ref, near in ((source, 8), (density, 7)):
        ref[0:near] = jnp.zeros((near, 8, 128), F32)
        ref[64 - near : 64] = jnp.zeros((near, 8, 128), F32)
    source[8:16] = before_ref[0:8]
    source[48:56] = after_ref[0:8]
    source[16:48] = right_ref[...]
    density[7:16] = before_ref[8:17]
    density[48:57] = after_ref[8:17]
    density[16:48] = jnp.where(labels_ref[...] == 1, gas_density, 1.0)
    for start, wide, out in ((0, source, s_ref), (5, density, d_ref)):
        rows = jnp.swapaxes(wide[...], 0, 1)
        out[...] = rows
        low_ref[start : start + 5] = rows[0:5, 8:56]
        high_ref[start : start + 5] = rows[3:8, 8:56]


def finest_window(s_ref, d_ref, before_ref, after_ref, source, density):
    for ref in (source, density):
        for rows in (pl.ds(0, 6), pl.ds(14, 6)):
            ref[rows] = jnp.zeros((6, 64, 128), F32)
    source[1:6, 8:56] = before_ref[0:5]
    source[14:19, 8:56] = after_ref[0:5]
    density[1:6, 8:56] = before_ref[5:10]
    density[14:19, 8:56] = after_ref[5:10]
    source[6:14] = s_ref[...]
    density[6:14] = d_ref[...]


def finest_down(s_ref, d_ref, before_ref, after_ref, chunk_ref, low_ref, high_ref, below_ref, keep,
                source, density, value, plane):
    finest_window(s_ref, d_ref, before_ref, after_ref, source, density)
    level = Level(density, keep, value, 128)
    level.clear((0, 9))
    value[1, 1] = jnp.zeros((64, 128), F32)
    value[1, 8] = jnp.zeros((64, 128), F32)
    level.coefficients(source, 1.0, 1, 8, 1)
    level.first(1, 8, 2)
    level.half(1, 1, 8, 2)
    level.half(0, 2, 6, 2)
    level.half(1, 2, 6, 2)

    def pooling(j):
        red, black = level.residual(1.0, 3 + j, 1)
        plane[pl.ds(j, 1)] = (red + black)[:, 16:48]
        plane[pl.ds(4 + j, 1)] = (density[pl.ds(6 + 2 * j, 1)] + density[pl.ds(7 + 2 * j, 1)])[:, 16:48]

    blocks(0, 4, 1, pooling)
    pooled = plane[:, pl.ds(0, 16, stride=2)] + plane[:, pl.ds(1, 16, stride=2)]
    out = dot(pooled[:4].reshape(64, 128), halving(0, 0.125)) + dot(pooled[4:].reshape(64, 128), halving(64, 0.125))
    low_ref[...] = value[1, 3:6, 8:56]
    high_ref[...] = value[1, 4:7, 8:56]
    for peer in range(GROUP):
        chunk_ref[peer] = out
    below_ref[...] = value[1, 3:7]


def folded(ref, rows, source, density, start):
    block = ref[rows]
    near, far = block[:, :24], block[:, 24:]
    left = iota(near.shape, 2) < 64
    source[start] = jnp.where(left, near, pltpu.roll(far, 64, 2))
    density[start] = jnp.where(left, pltpu.roll(near, 64, 2), far)


def middle_down(place_ref, window_ref, before_ref, after_ref, chunk_ref, below_ref, keep,
                window, source, density, value, plane, source2, density2, keep2, value2):
    window[1:43, 16:32] = window_ref[...]
    for ref, near, far in ((before_ref, 0, 8), (after_ref, 32, 32)):
        window[9:35, near : near + 16] = ref[0:416].reshape(26, 16, 128)
        for start, rows in ((1, 416), (35, 480)):
            window[start : start + 8, far : far + 8] = ref[rows : rows + 64].reshape(8, 8, 128)
            clear = 0 if near == 0 else 40
            window[start : start + 8, clear : clear + 8] = jnp.zeros((8, 8, 128), F32)
    for row in (0, 43):
        window[row] = jnp.zeros((48, 128), F32)
    blocks(0, 44, 4, lambda r: folded(window, pl.ds(r, 4), source, density, pl.ds(r, 4)))
    level = Level(density, keep, value, 64, 64)
    level.clear((0, 21))
    for j in (1, 20):
        value[1, j] = jnp.zeros((24, 128), F32)
    level.coefficients(source, 4.0, 1, 20, 2)
    level.first(1, 20, 5)
    level.half(1, 1, 20, 5)
    level.half(0, 2, 18, 6)
    level.half(1, 2, 18, 6)
    below_ref[...] = value[1, pl.ds(3 + 2 * place_ref[2], 10)]

    def pooling(j):
        red, black = level.residual(4.0, 3 + j, 4)
        plane[pl.ds(j, 4), 0:24] = red + black

    blocks(0, 16, 4, pooling)
    rows = density[4:40].reshape(18, 2, 24, 128)
    plane[16:34, 0:24] = rows[:, 0] + rows[:, 1]
    pooled = plane[:, pl.ds(0, 16, stride=2)] + plane[:, pl.ds(1, 16, stride=2)]
    pooled = dot(pooled.reshape(34 * 16, 128), halving(0, 0.125)).reshape(34, 16, 128)
    lane = iota((34, 16, 128), 2)
    near, far = jnp.where(lane < 32, pooled, 0.0), jnp.where(lane < 32, pltpu.roll(pooled, 96, 2), 0.0)
    for ref, start, parts in ((source2, 2, slice(0, 16)), (density2, 1, slice(16, 34))):
        ref[start : start + parts.stop - parts.start, 0:12] = near[parts, 0:12]
        ref[start : start + parts.stop - parts.start, 12:24] = far[parts, 0:12]
    for row in (0, 19):
        density2[row] = jnp.zeros((24, 128), F32)
    below = Level(density2, keep2, value2, 0)
    below.clear((0, 9))
    for j in (1, 8):
        value2[1, j] = jnp.zeros((24, 128), F32)
    below.coefficients(source2, 16.0, 1, 8, 2)
    below.first(1, 8, 8)
    below.half(1, 1, 8, 4)
    below.half(0, 2, 6, 6)
    below.half(1, 2, 6, 6)
    red, black = below.residual(16.0, 3, 4)
    plane[0:4, 0:24] = red + black
    rows = density2[6:14].reshape(4, 2, 24, 128)
    plane[4:8, 0:24] = rows[:, 0] + rows[:, 1]
    rows = []
    for row in range(4):
        for part in (row, 4 + row):
            rows.append(plane[part, pl.ds(8, 4, stride=2)] + plane[part, pl.ds(9, 4, stride=2)])
    pooled = dot(jnp.concatenate(rows, axis=0), halving(0, 0.125, 32))
    for row in range(4):
        total = pooled[8 * row : 8 * row + 1]
        for i in range(1, 8):
            total = total + pltpu.roll(pooled[8 * row + i : 8 * row + i + 1], 16 * i, 1)
        chunk_ref[0, 64 + row : 65 + row] = total
    for j in range(4):
        for k in range(2):
            row = 6 + 2 * j + k
            total = source2[row, 8:16] + pltpu.roll(density2[row, 8:16], 64, 1)
            if k == 0:
                total = total + pltpu.roll(value2[1, 3 + j, 8:16], 32, 1)
            chunk_ref[0, 8 * (2 * j + k) : 8 * (2 * j + k) + 8] = total
    chunk_ref[0, 68:72] = jnp.zeros((4, 128), F32)
    for peer in range(1, chunk_ref.shape[0]):
        chunk_ref[peer] = chunk_ref[0]


def coarsest(planes, place_ref, gathered_ref, near_ref, source, density, keep, value, wide):
    groups = gathered_ref.shape[0]
    lane = iota((8, 128), 1)
    for row in (0, 1, planes + 2, planes + 3):
        density[row] = jnp.zeros((8, 128), F32)

    def spread(g):
        tiles = [
            jnp.concatenate([gathered_ref[2 * h, g], gathered_ref[2 * h + 1, g]], axis=0) for h in range(groups // 2)
        ]
        tiles += [jnp.zeros((8, 128), F32)] * (8 - len(tiles))
        for step in (1, 2, 4):
            upper = (lane // 16) % (2 * step) >= step
            for i in range(8):
                if i % (2 * step) < step:
                    a, b = tiles[i], tiles[i + step]
                    tiles[i] = jnp.where(upper, pltpu.roll(b, 16 * step, 1), a)
                    tiles[i + step] = jnp.where(upper, b, pltpu.roll(a, 128 - 16 * step, 1))
        for z in range(4):
            source[2 + 4 * g + z] = tiles[z]
            density[2 + 4 * g + z] = tiles[4 + z]

    for g in range(planes // 4):
        spread(g)
    level = Level(density, keep, value, 16, 16, ends=True)
    pairs = planes // 2
    value[...] = jnp.zeros(value.shape, F32)
    level.coefficients(source, 64.0, 1, pairs, 4)

    def sweep(_, carry):
        level.half(0, 1, pairs, pairs)
        level.half(1, 1, pairs, pairs)
        return carry

    lax.fori_loop(0, 12, sweep, 0)
    wide[0:4] = jnp.zeros((4, 8, 128), F32)
    wide[planes + 4 : planes + 8] = jnp.zeros((4, 8, 128), F32)
    even, odd = level.rows(value[0, 1 : pairs + 1], value[1, 1 : pairs + 1])
    for j in range(pairs):
        wide[4 + 2 * j] = even[j]
        wide[5 + 2 * j] = odd[j]
    near_ref[...] = wide[pl.ds(4 * place_ref[0], 12)]


def way_up(devices, place_ref, near_ref, halo_ref, keep1, below1_ref, keep0, below0_ref, before_ref, after_ref,
           pressure_ref, remain_ref,
           source2, density2, keep2, value2, value1, value0, plane):
    at_y, at_group = place_ref[1], place_ref[2]

    block = halo_ref[pl.ds(2 * at_group, 18)]
    lane = iota(block.shape, 2)
    source2[2:20] = block
    for rows in (slice(0, 2), slice(20, 22)):
        density2[rows] = jnp.zeros((2, 24, 128), F32)
    density2[2:20] = jnp.where(lane < 32, pltpu.roll(block, 64, 2), 0.0)
    level = Level(density2, keep2, value2, 0)
    level.clear((0, 10))
    level.coefficients(source2, 16.0, 1, 9, 3)
    row = iota((8, 128), 0)
    near = near_ref[...]
    picked = []
    for i in range(9):
        y = at_y + i - 4
        inside = (y >= 0) & (y < devices)
        y = jnp.clip(y, 0, devices - 1)
        rows = jnp.sum(jnp.where(row == y % 8, near, 0.0), axis=1)
        rows = pltpu.roll(rows, (128 - 16 * (y // 8)) % 128, 1)
        picked.append(jnp.where(inside & (iota((12, 128), 1) < 16), rows, 0.0))
        picked.append(jnp.zeros((4, 128), F32))
    spread = dot(jnp.concatenate(picked, axis=0), doubling(16)).reshape(9, 16, 128)
    plane[0:9, pl.ds(0, 12, stride=2)] = spread[:, 0:12]
    plane[0:9, pl.ds(1, 12, stride=2)] = spread[:, 0:12]
    below = jnp.where(lane < 32, pltpu.roll(block, 96, 2), 0.0).reshape(9, 2, 24, 128)[:, 0]
    value2[1, 1:10] = below + plane[0:9, 0:24]
    level.half(0, 1, 9, 3)
    level.half(1, 2, 7, 7)
    level.half(0, 2, 7, 7)
    level.half(1, 3, 5, 5)
    even, odd = level.rows(value2[0, 3:8], value2[1, 3:8])

    first = 3 + 2 * at_group
    level = Level(None, keep1, value1, 64, 64)
    rows = jnp.stack([even, odd], axis=1).reshape(240, 128)
    spread = dot(rows, doubling(32, 0, 64)).reshape(10, 24, 128)
    plane[0:10, pl.ds(0, 24, stride=2)] = spread
    plane[0:10, pl.ds(1, 24, stride=2)] = spread
    left = iota((10, 24, 128), 2) < 64
    value1[1, pl.ds(first, 10)] = below1_ref[...] + jnp.where(left, plane[0:10, 0:24], plane[0:10, 24:48])
    level.clear_red((first, first + 9))
    level.half(0, first + 1, 8, 4)
    level.half(1, first + 1, 8, 4)
    level.half(0, first + 2, 6, 6)
    level.half(1, first + 2, 6, 6)
    inside = pl.ds(first + 2, 6)
    even, odd = level.rows(value1[0, inside], value1[1, inside])
    rows = jnp.stack([even, odd], axis=1).reshape(12, 24, 128)[1:11]

    level = Level(None, keep0, value0, 128)
    near = dot(rows[:, 8:24].reshape(160, 128), doubling(64)).reshape(10, 16, 128)
    far = dot(rows[:, 0:16].reshape(160, 128), doubling(64, 64)).reshape(10, 16, 128)
    for start, part in ((0, near), (32, far)):
        plane[0:10, pl.ds(start, 16, stride=2)] = part
        plane[0:10, pl.ds(start + 1, 16, stride=2)] = part
    value0[1] = plane[...]
    value0[1, 0:3, 8:56] = value0[1, 0:3, 8:56] + before_ref[...]
    value0[1, 3:7] = value0[1, 3:7] + below0_ref[...]
    value0[1, 7:10, 8:56] = value0[1, 7:10, 8:56] + after_ref[...]
    level.clear_red((0, 9))
    level.half(0, 1, 8, 2)
    level.half(1, 1, 8, 2)
    level.half(0, 2, 6, 2)
    level.half(1, 2, 6, 2)
    even, odd = level.rows(value0[0, 3:7, 16:48], value0[1, 3:7, 16:48])
    pressure_ref[...] = jnp.swapaxes(jnp.stack([even, odd], axis=1).reshape(8, 32, 128), 0, 1)

    def remaining(j):
        red, black = level.residual(1.0, 3 + j, 1)
        even, odd = level.rows(red, black)
        plane[pl.ds(2 * j, 1)] = even
        plane[pl.ds(2 * j + 1, 1)] = odd

    blocks(0, 4, 1, remaining)
    remain_ref[...] = jnp.swapaxes(plane[0:8, 16:48], 0, 1)


def pair(array_up, array_down, axis, group=1):
    groups = lax.axis_size(axis) // group
    up = [(i * group + j, (i + 2) * group - 1 - j) for i in range(groups - 1) for j in range(group)]
    down = [(j, i) for i, j in up]
    return lax.ppermute(array_up, axis, up), lax.ppermute(array_down, axis, down)


def shape(*sizes):
    return jax.ShapeDtypeStruct(sizes, F32)


def vmem(*sizes):
    return pltpu.VMEM(sizes, F32)


def params():
    return pltpu.CompilerParams(vmem_limit_bytes=24 * 1024 * 1024)


def body(right_side, labels):
    gz, xy = lax.axis_size("gz"), lax.axis_size("xy")
    density = jnp.where(labels == 1, gas_density, 1.0).astype(F32)
    before, after = pair(
        jnp.concatenate([right_side[-8:], density[-9:]], axis=0),
        jnp.concatenate([right_side[:8], density[:9]], axis=0),
        "gz",
    )
    wide_source, wide_density, low_rim, high_rim = pl.pallas_call(
        finest_rims,
        out_shape=[shape(8, 64, 128)] * 2 + [shape(10, 48, 128)] * 2,
        scratch_shapes=[vmem(64, 8, 128)] * 2,
        compiler_params=params(),
    )(right_side, labels, before, after)
    before, after = pair(high_rim, low_rim, "xy")
    finest = (wide_source, wide_density, before, after)
    at_group = lax.axis_index("xy") % GROUP
    place = jnp.stack([lax.axis_index("gz"), lax.axis_index("xy"), at_group]).astype(jnp.int32)
    smem, block = pl.BlockSpec(memory_space=pltpu.SMEM), pl.BlockSpec(memory_space=pltpu.VMEM)
    chunks, first_rows, last_rows, below0, keep0 = pl.pallas_call(
        finest_down,
        out_shape=[shape(GROUP, 64, 128), shape(3, 48, 128), shape(3, 48, 128), shape(4, 64, 128), shape(KEPT, 10, 64, 128)],
        scratch_shapes=[vmem(20, 64, 128)] * 2 + [vmem(2, 10, 64, 128), vmem(8, 32, 128)],
        compiler_params=params(),
    )(*finest)

    teams = [[GROUP * i + j for j in range(GROUP)] for i in range(xy // GROUP)]
    chunks = lax.all_to_all(chunks, "xy", 0, 0, axis_index_groups=teams, tiled=True)
    window = chunks.reshape(4 * GROUP, 16, 128)
    before, after = pair(window[-13:], window[:13], "xy", GROUP)
    window = jnp.concatenate([before, window, after], axis=0)

    def faces(near):
        parts = (window[8:34], window[:8, near], window[34:, near])
        return jnp.concatenate([part.reshape(-1, 128) for part in parts], axis=0)

    before, after = pair(faces(slice(8, 16)), faces(slice(0, 8)), "gz")
    chunks, below1, keep1 = pl.pallas_call(
        middle_down,
        out_shape=[shape(gz, 72, 128), shape(10, 24, 128), shape(KEPT, 22, 24, 128)],
        in_specs=[smem] + [block] * 3,
        scratch_shapes=[vmem(44, 48, 128)]
        + [vmem(44, 24, 128)] * 2
        + [vmem(2, 22, 24, 128), vmem(34, 32, 128)]
        + [vmem(20, 24, 128)] * 2
        + [vmem(KEPT, 10, 24, 128), vmem(2, 10, 24, 128)],
        compiler_params=params(),
    )(place, window, before, after)

    value_before, value_after = pair(last_rows, first_rows, "xy")
    column = lax.all_to_all(chunks, "gz", 0, 0, tiled=True)
    peers = [[GROUP * i + j for i in range(xy // GROUP)] for j in range(GROUP)]
    everywhere = lax.all_to_all(
        jnp.broadcast_to(column[None, :, 64:68], (xy // GROUP, gz, 4, 128)), "xy", 0, 0, axis_index_groups=peers, tiled=True
    )
    halo = jnp.pad(column[:, :64], ((1, 1), (0, 0), (0, 0)))
    halo = lax.dynamic_slice(halo, (lax.axis_index("gz"), 0, 0), (3, 64, 128)).reshape(3, 8, 8, 128)
    halo = jnp.swapaxes(halo, 0, 1).reshape(8, 24, 128)
    before, after = pair(halo, halo, "xy", GROUP)
    halo = jnp.concatenate([before, halo, after], axis=0)
    planes = 4 * gz
    near = pl.pallas_call(
        partial(coarsest, planes),
        out_shape=shape(12, 8, 128),
        in_specs=[smem, block],
        scratch_shapes=[vmem(planes + 4, 8, 128)] * 2
        + [vmem(KEPT, planes // 2 + 2, 8, 128), vmem(2, planes // 2 + 2, 8, 128), vmem(planes + 8, 8, 128)],
        compiler_params=params(),
        cost_estimate=pl.CostEstimate(flops=100_000_000, bytes_accessed=16_000_000, transcendentals=0),
    )(place, everywhere)
    return pl.pallas_call(
        partial(way_up, xy),
        out_shape=[shape(32, 8, 128)] * 2,
        in_specs=[smem] + [block] * 8,
        scratch_shapes=[vmem(22, 24, 128)] * 2
        + [vmem(KEPT, 11, 24, 128), vmem(2, 11, 24, 128)]
        + [vmem(2, 22, 24, 128), vmem(2, 10, 64, 128), vmem(10, 64, 128)],
        compiler_params=params(),
    )(place, near, halo, keep1, below1, keep0, below0, value_before, value_after)


def solution(mesh):
    return jax.shard_map(
        body,
        mesh=mesh,
        in_specs=(P("gz", "xy", None), P("gz", "xy", None)),
        out_specs=(P("gz", "xy", None), P("gz", "xy", None)),
        check_vma=False,
    )
```

```python
from functools import partial

import jax
import jax.numpy as jnp
from jax import lax
from jax.experimental import pallas as pl
from jax.experimental.pallas import tpu as pltpu
from jax.sharding import PartitionSpec as P

gas_density = 0.001
least = 1e-4
F32 = jnp.float32
GROUP = 4
FACES = (
    (range(13, 29), 13),
    (range(9, 13), 12),
    (range(29, 33), 12),
    (range(5, 9), 8),
    (range(33, 37), 8),
    (range(1, 5), 4),
    (range(37, 41), 4),
)


def dot(a, b):
    return lax.dot_general(
        a, b, (((1,), (0,)), ((), ())), precision=lax.Precision.HIGHEST, preferred_element_type=F32
    )


def iota(shape, axis):
    return lax.broadcasted_iota(jnp.int32, shape, axis)


def halving(offset, weight, width=128):
    row, column = iota((128, 128), 0), iota((128, 128), 1)
    return jnp.where((row // 2 + offset == column) & (row < width), weight, 0.0).astype(F32)


def doubling(width, first=0, period=128):
    row, column = iota((128, 128), 0), iota((128, 128), 1)
    hit = ((column % period) // 2 + first == row) & (row < first + width)
    return jnp.where(hit, 1.0, 0.0).astype(F32)


def inverse(a):
    return pl.reciprocal(a, approx=True)


def blocks(lo, count, block, step):
    assert count % block == 0
    if count == block:
        step(lo)
    else:

        def turn(i, _):
            step(lo + i * block)
            return 0

        lax.fori_loop(0, count // block, turn, 0)


LOWER, LEFT, OUT, INNER, INVERSE, DIAGONAL, SOURCE = 0, 2, 4, 6, 7, 9, 11
KEPT = 13


class Level:
    def __init__(self, density, keep, value, width, cross=0, ends=False):
        self.density, self.keep, self.value = density, keep, value
        self.depth, self.width, self.cross, self.ends = value.shape[2], width, cross, ends
        self.row, self.lane = iota((1, 8, 128), 1), iota((1, 8, 128), 2)
        self.odd = (self.row + self.lane) % 2 == 1

    def choose(self, mask, a, b):
        if not isinstance(a, float):
            shape, a = a.shape, a.reshape(-1, 8, 128)
        if not isinstance(b, float):
            shape, b = b.shape, b.reshape(-1, 8, 128)
        return jnp.where(mask, a, b).reshape(shape)

    def low(self, a):
        turned = pltpu.roll(a, 1, 1)
        if self.cross:
            head = turned[:, :8]
            head = jnp.where(self.row == 0, pltpu.roll(head, self.cross, 2), head)
            turned = head if self.depth == 8 else jnp.concatenate([head, turned[:, 8:]], axis=1)
        return turned

    def high(self, a):
        turned = pltpu.roll(a, self.depth - 1, 1)
        if self.cross:
            tail = turned[:, -8:]
            tail = jnp.where(self.row == 7, pltpu.roll(tail, 128 - self.cross, 2), tail)
            turned = tail if self.depth == 8 else jnp.concatenate([turned[:, :-8], tail], axis=1)
        return turned

    def coefficients(self, source, factor, lo, count, block):
        first_x, last_x = self.lane % max(self.width, 1) == 0, self.lane % max(self.width, 1) == self.width - 1
        if self.ends:
            first, last = (self.row == 0) & (self.lane < self.width), (self.row == 7) & (self.lane >= 128 - self.width)

        def coupling(a, b):
            return 2.0 * inverse(jnp.maximum(a + b, least))

        def both(place, at, even, odd):
            self.keep[place, at] = self.choose(self.odd, odd, even)
            self.keep[place + 1, at] = self.choose(self.odd, even, odd)

        def step(j):
            at = pl.ds(j, block)
            shape = (block, 2, self.depth, 128)
            rows = self.density[pl.ds(2 * j, 2 * block)].reshape(shape)
            before = self.density[pl.ds(2 * j - 1, 2 * block)].reshape(shape)[:, 0]
            after = self.density[pl.ds(2 * j + 1, 2 * block)].reshape(shape)[:, 1]
            inner = coupling(rows[:, 0], rows[:, 1])
            out = (coupling(rows[:, 0], before), coupling(rows[:, 1], after))
            parts = []
            for k in range(2):
                d = rows[:, k]
                if self.width or self.ends:
                    edge = 2.0 * inverse(jnp.maximum(d, least))
                lower = coupling(d, self.low(d))
                upper = self.high(lower)
                if self.ends:
                    lower, upper = self.choose(first, edge, lower), self.choose(last, edge, upper)
                left = coupling(d, pltpu.roll(d, 1, 2))
                right = pltpu.roll(left, 127, 2)
                if self.width:
                    left, right = self.choose(first_x, edge, left), self.choose(last_x, edge, right)
                total = lower + upper + (out[0] + inner if k == 0 else inner + out[1]) + left + right
                if self.ends:
                    lower = self.choose(first, 0.0, lower)
                if self.width:
                    left = self.choose(first_x, 0.0, left)
                parts.append((lower, left, jnp.where(d > 0.0, inverse(total), 0.0), total))
            for place, even, odd in zip((LOWER, LEFT, INVERSE, DIAGONAL), *parts):
                both(place, at, even, odd)
            both(OUT, at, out[0], out[1])
            self.keep[INNER, at] = inner
            if source is not None:
                rows = factor * source[pl.ds(2 * j, 2 * block)].reshape(shape)
                both(SOURCE, at, rows[:, 0], rows[:, 1])

        blocks(lo, count, block, step)

    def gathered(self, colour, j, block):
        at, keep = pl.ds(j, block), self.keep
        other = self.value.at[1 - colour]
        w = other[at]
        before, after = other[pl.ds(j - 1, block)], other[pl.ds(j + 1, block)]
        side = self.choose(self.odd, before, after) if colour else self.choose(self.odd, after, before)
        total = keep[INNER, at] * w + keep[OUT + colour, at] * side
        total += keep[LOWER + colour, at] * self.low(w) + self.high(keep[LOWER + 1 - colour, at] * w)
        total += keep[LEFT + colour, at] * pltpu.roll(w, 1, 2) + pltpu.roll(keep[LEFT + 1 - colour, at] * w, 127, 2)
        return total

    def first(self, lo, count, block):
        def step(j):
            at = pl.ds(j, block)
            self.value[0, at] = self.keep[SOURCE, at] * self.keep[INVERSE, at]

        blocks(lo, count, block, step)

    def half(self, colour, lo, count, block):
        def step(j):
            at = pl.ds(j, block)
            total = self.keep[SOURCE + colour, at] + self.gathered(colour, j, block)
            self.value[colour, at] = total * self.keep[INVERSE + colour, at]

        blocks(lo, count, block, step)

    def residual(self, factor, j, block):
        at, out = pl.ds(j, block), []
        for colour in (0, 1):
            total = self.keep[DIAGONAL + colour, at] * self.value[colour, at] - self.gathered(colour, j, block)
            out.append((self.keep[SOURCE + colour, at] - total) * (1.0 / factor))
        return out

    def rows(self, red, black):
        return self.choose(self.odd, black, red), self.choose(self.odd, red, black)

    def clear_red(self, pairs):
        for j in pairs:
            self.value[0, j] = jnp.zeros((self.depth, 128), F32)

    def clear(self, pairs):
        for j in pairs:
            self.value[:, j] = jnp.zeros((2, self.depth, 128), F32)


def finest_rims(right_ref, labels_ref, before_ref, after_ref, s_ref, d_ref, low_ref, high_ref, source, density):
    for ref, near in ((source, 8), (density, 7)):
        ref[0:near] = jnp.zeros((near, 8, 128), F32)
        ref[64 - near : 64] = jnp.zeros((near, 8, 128), F32)
    source[8:16] = before_ref[0:8]
    source[48:56] = after_ref[0:8]
    source[16:48] = right_ref[...]
    density[7:16] = before_ref[8:17]
    density[48:57] = after_ref[8:17]
    density[16:48] = jnp.where(labels_ref[...] == 1, gas_density, 1.0)
    for start, wide, out in ((0, source, s_ref), (5, density, d_ref)):
        rows = jnp.swapaxes(wide[...], 0, 1)
        out[...] = rows
        low_ref[start : start + 5] = rows[0:5, 8:56]
        high_ref[start : start + 5] = rows[3:8, 8:56]


def finest_window(s_ref, d_ref, before_ref, after_ref, source, density):
    for ref in (source, density):
        for rows in (pl.ds(0, 6), pl.ds(14, 6)):
            ref[rows] = jnp.zeros((6, 64, 128), F32)
    source[1:6, 8:56] = before_ref[0:5]
    source[14:19, 8:56] = after_ref[0:5]
    density[1:6, 8:56] = before_ref[5:10]
    density[14:19, 8:56] = after_ref[5:10]
    source[6:14] = s_ref[...]
    density[6:14] = d_ref[...]


def finest_down(s_ref, d_ref, before_ref, after_ref, chunk_ref, low_ref, high_ref, below_ref,
                source, density, keep, value, plane):
    finest_window(s_ref, d_ref, before_ref, after_ref, source, density)
    level = Level(density, keep, value, 128)
    level.clear((0, 9))
    value[1, 1] = jnp.zeros((64, 128), F32)
    value[1, 8] = jnp.zeros((64, 128), F32)
    level.coefficients(source, 1.0, 1, 8, 1)
    level.first(1, 8, 2)
    level.half(1, 1, 8, 2)
    level.half(0, 2, 6, 2)
    level.half(1, 2, 6, 2)

    def pooling(j):
        red, black = level.residual(1.0, 3 + j, 1)
        plane[pl.ds(j, 1)] = (red + black)[:, 16:48]
        plane[pl.ds(4 + j, 1)] = (density[pl.ds(6 + 2 * j, 1)] + density[pl.ds(7 + 2 * j, 1)])[:, 16:48]

    blocks(0, 4, 1, pooling)
    pooled = plane[:, pl.ds(0, 16, stride=2)] + plane[:, pl.ds(1, 16, stride=2)]
    out = dot(pooled[:4].reshape(64, 128), halving(0, 0.125)) + dot(pooled[4:].reshape(64, 128), halving(64, 0.125))
    low_ref[...] = value[1, 3:6, 8:56]
    high_ref[...] = value[1, 4:7, 8:56]
    for peer in range(GROUP):
        chunk_ref[peer] = out
    below_ref[...] = value[1, 3:7]


def folded(ref, rows, source, density, start):
    block = ref[rows]
    near, far = block[:, :24], block[:, 24:]
    left = iota(near.shape, 2) < 64
    source[start] = jnp.where(left, near, pltpu.roll(far, 64, 2))
    density[start] = jnp.where(left, pltpu.roll(near, 64, 2), far)


def middle_down(place_ref, window_ref, before_ref, after_ref, chunk_ref, kept_ref, below_ref,
                window, source, density, keep, value, plane, source2, density2, keep2, value2):
    for near, ref in ((0, before_ref), (32, after_ref)):
        window[0:44, near : near + 16] = jnp.zeros((44, 16, 128), F32)
        start = 0
        for rows, planes in FACES:
            low = 16 - planes if near == 0 else 32
            for row in rows:
                window[row + 1, low : low + planes] = ref[start : start + planes]
                start += planes
    window[1:43, 16:32] = window_ref[...]
    for row in (0, 43):
        window[row] = jnp.zeros((48, 128), F32)
    blocks(0, 44, 4, lambda r: folded(window, pl.ds(r, 4), source, density, pl.ds(r, 4)))
    level = Level(density, keep, value, 64, 64)
    level.clear((0, 21))
    for j in (1, 20):
        value[1, j] = jnp.zeros((24, 128), F32)
    level.coefficients(source, 4.0, 1, 20, 2)
    level.first(1, 20, 5)
    level.half(1, 1, 20, 5)
    level.half(0, 2, 18, 6)
    level.half(1, 2, 18, 6)
    kept_ref[...] = window[pl.ds(6 + 4 * place_ref[2], 20)]
    below_ref[...] = value[1, pl.ds(3 + 2 * place_ref[2], 10)]

    def pooling(j):
        red, black = level.residual(4.0, 3 + j, 4)
        plane[pl.ds(j, 4), 0:24] = red + black

    blocks(0, 16, 4, pooling)
    rows = density[4:40].reshape(18, 2, 24, 128)
    plane[16:34, 0:24] = rows[:, 0] + rows[:, 1]
    pooled = plane[:, pl.ds(0, 16, stride=2)] + plane[:, pl.ds(1, 16, stride=2)]
    pooled = dot(pooled.reshape(34 * 16, 128), halving(0, 0.125)).reshape(34, 16, 128)
    lane = iota((34, 16, 128), 2)
    near, far = jnp.where(lane < 32, pooled, 0.0), jnp.where(lane < 32, pltpu.roll(pooled, 96, 2), 0.0)
    for ref, start, parts in ((source2, 2, slice(0, 16)), (density2, 1, slice(16, 34))):
        ref[start : start + parts.stop - parts.start, 0:12] = near[parts, 0:12]
        ref[start : start + parts.stop - parts.start, 12:24] = far[parts, 0:12]
    for row in (0, 19):
        density2[row] = jnp.zeros((24, 128), F32)
    below = Level(density2, keep2, value2, 0)
    below.clear((0, 9))
    for j in (1, 8):
        value2[1, j] = jnp.zeros((24, 128), F32)
    below.coefficients(source2, 16.0, 1, 8, 2)
    below.first(1, 8, 8)
    below.half(1, 1, 8, 4)
    below.half(0, 2, 6, 6)
    below.half(1, 2, 6, 6)
    red, black = below.residual(16.0, 3, 4)
    plane[0:4, 0:24] = red + black
    rows = density2[6:14].reshape(4, 2, 24, 128)
    plane[4:8, 0:24] = rows[:, 0] + rows[:, 1]
    rows = []
    for row in range(4):
        for part in (row, 4 + row):
            rows.append(plane[part, pl.ds(8, 4, stride=2)] + plane[part, pl.ds(9, 4, stride=2)])
    pooled = dot(jnp.concatenate(rows, axis=0), halving(0, 0.125, 32))
    for row in range(4):
        total = pooled[8 * row : 8 * row + 1]
        for i in range(1, 8):
            total = total + pltpu.roll(pooled[8 * row + i : 8 * row + i + 1], 16 * i, 1)
        chunk_ref[0, 40 + row : 41 + row] = total
    black = jnp.zeros((8, 128), F32)
    for j in range(4):
        total = black
        for k, ref in enumerate((source2, density2, source2, density2)):
            total = total + pltpu.roll(ref[6 + 2 * j + k // 2, 8:16], 32 * k, 1)
        chunk_ref[0, 8 * j : 8 * j + 8] = total
    for j in range(4):
        black = black + pltpu.roll(value2[1, 3 + j, 8:16], 32 * j, 1)
    chunk_ref[0, 32:40] = black
    chunk_ref[0, 44:48] = jnp.zeros((4, 128), F32)
    for peer in range(1, chunk_ref.shape[0]):
        chunk_ref[peer] = chunk_ref[0]


def coarsest(planes, place_ref, gathered_ref, near_ref, source, density, keep, value, wide):
    groups = gathered_ref.shape[0]
    lane = iota((8, 128), 1)
    for row in (0, 1, planes + 2, planes + 3):
        density[row] = jnp.zeros((8, 128), F32)

    def spread(g):
        tiles = [
            jnp.concatenate([gathered_ref[2 * h + k, 4 * g : 4 * g + 4] for k in range(2)], axis=0)
            for h in range(groups // 2)
        ]
        tiles += [jnp.zeros((8, 128), F32)] * (8 - len(tiles))
        for step in (1, 2, 4):
            upper = (lane // 16) % (2 * step) >= step
            for i in range(8):
                if i % (2 * step) < step:
                    a, b = tiles[i], tiles[i + step]
                    tiles[i] = jnp.where(upper, pltpu.roll(b, 16 * step, 1), a)
                    tiles[i + step] = jnp.where(upper, b, pltpu.roll(a, 128 - 16 * step, 1))
        for z in range(4):
            source[2 + 4 * g + z] = tiles[z]
            density[2 + 4 * g + z] = tiles[4 + z]

    for g in range(planes // 4):
        spread(g)
    level = Level(density, keep, value, 16, 16, ends=True)
    pairs = planes // 2
    value[...] = jnp.zeros(value.shape, F32)
    level.coefficients(source, 64.0, 1, pairs, 4)

    def sweep(_, carry):
        level.half(0, 1, pairs, pairs)
        level.half(1, 1, pairs, pairs)
        return carry

    lax.fori_loop(0, 12, sweep, 0)
    wide[0:4] = jnp.zeros((4, 8, 128), F32)
    wide[planes + 4 : planes + 8] = jnp.zeros((4, 8, 128), F32)
    even, odd = level.rows(value[0, 1 : pairs + 1], value[1, 1 : pairs + 1])
    for j in range(pairs):
        wide[4 + 2 * j] = even[j]
        wide[5 + 2 * j] = odd[j]
    near_ref[...] = wide[pl.ds(4 * place_ref[0], 12)]


def way_up(devices, place_ref, near_ref, halo_ref, kept_ref, below1_ref,
           s_ref, d_ref, rim_before_ref, rim_after_ref, below0_ref, before_ref, after_ref,
           pressure_ref, remain_ref,
           source2, density2, keep2, value2, source1, density1, keep1, value1,
           source0, density0, keep0, value0, plane):
    at_y, at_group = place_ref[1], place_ref[2]

    lane = iota((24, 128), 1)
    for rows in (slice(0, 2), slice(20, 22)):
        density2[rows] = jnp.zeros((2, 24, 128), F32)
    for i in range(9):
        group, part = (at_group + i) // 4, (at_group + i) % 4
        block = halo_ref[5 * group + part]
        for k in range(2):
            row = 2 + 2 * i + k
            source2[row] = pltpu.roll(block, 64, 1) if k else block
            density2[row] = jnp.where(lane < 32, pltpu.roll(block, 96 - 64 * k, 1), 0.0)
        black = pltpu.roll(halo_ref[5 * group + 4], (128 - 32 * part) % 128, 1)
        value2[1, 1 + i] = jnp.where(lane < 32, black, 0.0)
    level = Level(density2, keep2, value2, 0)
    level.clear((0, 10))
    level.coefficients(source2, 16.0, 1, 9, 3)
    row = iota((8, 128), 0)
    near = near_ref[...]
    picked = []
    for i in range(9):
        y = at_y + i - 4
        inside = (y >= 0) & (y < devices)
        y = jnp.clip(y, 0, devices - 1)
        rows = jnp.sum(jnp.where(row == y % 8, near, 0.0), axis=1)
        rows = pltpu.roll(rows, (128 - 16 * (y // 8)) % 128, 1)
        picked.append(jnp.where(inside & (iota((12, 128), 1) < 16), rows, 0.0))
        picked.append(jnp.zeros((4, 128), F32))
    spread = dot(jnp.concatenate(picked, axis=0), doubling(16)).reshape(9, 16, 128)
    plane[0:9, pl.ds(0, 12, stride=2)] = spread[:, 0:12]
    plane[0:9, pl.ds(1, 12, stride=2)] = spread[:, 0:12]
    value2[1, 1:10] = value2[1, 1:10] + plane[0:9, 0:24]
    level.half(0, 1, 9, 3)
    level.half(1, 2, 7, 7)
    level.half(0, 2, 7, 7)
    level.half(1, 3, 5, 5)
    even, odd = level.rows(value2[0, 3:8], value2[1, 3:8])

    blocks(0, 20, 4, lambda r: folded(kept_ref, pl.ds(r, 4), source1, density1, pl.ds(r, 4)))
    level = Level(density1, keep1, value1, 64, 64)
    level.coefficients(source1, 4.0, 1, 8, 2)
    rows = jnp.stack([even, odd], axis=1).reshape(240, 128)
    spread = dot(rows, doubling(32, 0, 64)).reshape(10, 24, 128)
    plane[0:10, pl.ds(0, 24, stride=2)] = spread
    plane[0:10, pl.ds(1, 24, stride=2)] = spread
    left = iota((10, 24, 128), 2) < 64
    value1[1] = below1_ref[...] + jnp.where(left, plane[0:10, 0:24], plane[0:10, 24:48])
    level.clear_red((0, 9))
    level.half(0, 1, 8, 4)
    level.half(1, 1, 8, 4)
    level.half(0, 2, 6, 6)
    level.half(1, 2, 6, 6)
    even, odd = level.rows(value1[0, 2:8], value1[1, 2:8])
    rows = jnp.stack([even, odd], axis=1).reshape(12, 24, 128)[1:11]

    finest_window(s_ref, d_ref, rim_before_ref, rim_after_ref, source0, density0)
    level = Level(density0, keep0, value0, 128)
    level.coefficients(source0, 1.0, 1, 8, 1)
    near = dot(rows[:, 8:24].reshape(160, 128), doubling(64)).reshape(10, 16, 128)
    far = dot(rows[:, 0:16].reshape(160, 128), doubling(64, 64)).reshape(10, 16, 128)
    for start, part in ((0, near), (32, far)):
        plane[0:10, pl.ds(start, 16, stride=2)] = part
        plane[0:10, pl.ds(start + 1, 16, stride=2)] = part
    value0[1] = plane[...]
    value0[1, 0:3, 8:56] = value0[1, 0:3, 8:56] + before_ref[...]
    value0[1, 3:7] = value0[1, 3:7] + below0_ref[...]
    value0[1, 7:10, 8:56] = value0[1, 7:10, 8:56] + after_ref[...]
    level.clear_red((0, 9))
    level.half(0, 1, 8, 2)
    level.half(1, 1, 8, 2)
    level.half(0, 2, 6, 2)
    level.half(1, 2, 6, 2)
    even, odd = level.rows(value0[0, 3:7, 16:48], value0[1, 3:7, 16:48])
    pressure_ref[...] = jnp.swapaxes(jnp.stack([even, odd], axis=1).reshape(8, 32, 128), 0, 1)

    def remaining(j):
        red, black = level.residual(1.0, 3 + j, 1)
        even, odd = level.rows(red, black)
        plane[pl.ds(2 * j, 1)] = even
        plane[pl.ds(2 * j + 1, 1)] = odd

    blocks(0, 4, 1, remaining)
    remain_ref[...] = jnp.swapaxes(plane[0:8, 16:48], 0, 1)


def pair(array_up, array_down, axis, group=1):
    groups = lax.axis_size(axis) // group
    up = [(i * group + j, (i + 2) * group - 1 - j) for i in range(groups - 1) for j in range(group)]
    down = [(j, i) for i, j in up]
    return lax.ppermute(array_up, axis, up), lax.ppermute(array_down, axis, down)


def shape(*sizes):
    return jax.ShapeDtypeStruct(sizes, F32)


def vmem(*sizes):
    return pltpu.VMEM(sizes, F32)


def params():
    return pltpu.CompilerParams(vmem_limit_bytes=24 * 1024 * 1024)


def body(right_side, labels):
    gz, xy = lax.axis_size("gz"), lax.axis_size("xy")
    density = jnp.where(labels == 1, gas_density, 1.0).astype(F32)
    before, after = pair(
        jnp.concatenate([right_side[-8:], density[-9:]], axis=0),
        jnp.concatenate([right_side[:8], density[:9]], axis=0),
        "gz",
    )
    wide_source, wide_density, low_rim, high_rim = pl.pallas_call(
        finest_rims,
        out_shape=[shape(8, 64, 128)] * 2 + [shape(10, 48, 128)] * 2,
        scratch_shapes=[vmem(64, 8, 128)] * 2,
        compiler_params=params(),
    )(right_side, labels, before, after)
    before, after = pair(high_rim, low_rim, "xy")
    finest = (wide_source, wide_density, before, after)
    at_group = lax.axis_index("xy") % GROUP
    place = jnp.stack([lax.axis_index("gz"), lax.axis_index("xy"), at_group]).astype(jnp.int32)
    smem, block = pl.BlockSpec(memory_space=pltpu.SMEM), pl.BlockSpec(memory_space=pltpu.VMEM)
    chunks, first_rows, last_rows, below0 = pl.pallas_call(
        finest_down,
        out_shape=[shape(GROUP, 64, 128), shape(3, 48, 128), shape(3, 48, 128), shape(4, 64, 128)],
        scratch_shapes=[vmem(20, 64, 128)] * 2 + [vmem(KEPT, 10, 64, 128), vmem(2, 10, 64, 128), vmem(8, 32, 128)],
        compiler_params=params(),
    )(*finest)

    teams = [[GROUP * i + j for j in range(GROUP)] for i in range(xy // GROUP)]
    chunks = lax.all_to_all(chunks, "xy", 0, 0, axis_index_groups=teams, tiled=True)
    window = chunks.reshape(4 * GROUP, 16, 128)
    before, after = pair(window[-13:], window[:13], "xy", GROUP)
    window = jnp.concatenate([before, window, after], axis=0)

    def faces(up):
        parts = []
        for rows, planes in FACES:
            part = window[rows.start : rows.stop, 16 - planes :] if up else window[rows.start : rows.stop, :planes]
            parts.append(part.reshape(-1, 128))
        return jnp.concatenate(parts, axis=0)

    before, after = pair(faces(True), faces(False), "gz")
    chunks, kept, below1 = pl.pallas_call(
        middle_down,
        out_shape=[shape(gz, 48, 128), shape(20, 48, 128), shape(10, 24, 128)],
        in_specs=[smem] + [block] * 3,
        scratch_shapes=[vmem(44, 48, 128)]
        + [vmem(44, 24, 128)] * 2
        + [vmem(KEPT, 22, 24, 128), vmem(2, 22, 24, 128), vmem(34, 32, 128)]
        + [vmem(20, 24, 128)] * 2
        + [vmem(KEPT, 10, 24, 128), vmem(2, 10, 24, 128)],
        compiler_params=params(),
    )(place, window, before, after)

    value_before, value_after = pair(last_rows, first_rows, "xy")
    column = lax.all_to_all(chunks, "gz", 0, 0, tiled=True)
    peers = [[GROUP * i + j for i in range(xy // GROUP)] for j in range(GROUP)]
    everywhere = lax.all_to_all(
        jnp.broadcast_to(column[:, 40:44].reshape(1, 4 * gz, 128), (xy // GROUP, 4 * gz, 128)),
        "xy", 0, 0, axis_index_groups=peers, tiled=True,
    )
    halo = jnp.pad(column[:, :40], ((1, 1), (0, 0), (0, 0)))
    halo = lax.dynamic_slice(halo, (lax.axis_index("gz"), 0, 0), (3, 40, 128)).reshape(3, 5, 8, 128)
    halo = jnp.swapaxes(halo, 0, 1).reshape(5, 24, 128)
    before, after = pair(halo, halo, "xy", GROUP)
    halo = jnp.concatenate([before, halo, after], axis=0)
    planes = 4 * gz
    near = pl.pallas_call(
        partial(coarsest, planes),
        out_shape=shape(12, 8, 128),
        in_specs=[smem, block],
        scratch_shapes=[vmem(planes + 4, 8, 128)] * 2
        + [vmem(KEPT, planes // 2 + 2, 8, 128), vmem(2, planes // 2 + 2, 8, 128), vmem(planes + 8, 8, 128)],
        compiler_params=params(),
        cost_estimate=pl.CostEstimate(flops=100_000_000, bytes_accessed=16_000_000, transcendentals=0),
    )(place, everywhere)
    return pl.pallas_call(
        partial(way_up, xy),
        out_shape=[shape(32, 8, 128)] * 2,
        in_specs=[smem] + [block] * 11,
        scratch_shapes=[vmem(22, 24, 128)] * 2
        + [vmem(KEPT, 11, 24, 128), vmem(2, 11, 24, 128)]
        + [vmem(20, 24, 128)] * 2
        + [vmem(KEPT, 10, 24, 128), vmem(2, 10, 24, 128)]
        + [vmem(20, 64, 128)] * 2
        + [vmem(KEPT, 10, 64, 128), vmem(2, 10, 64, 128), vmem(10, 64, 128)],
        compiler_params=params(),
    )(place, near, halo, kept, below1, *finest, below0, value_before, value_after)


def solution(mesh):
    return jax.shard_map(
        body,
        mesh=mesh,
        in_specs=(P("gz", "xy", None), P("gz", "xy", None)),
        out_specs=(P("gz", "xy", None), P("gz", "xy", None)),
        check_vma=False,
    )
```

```python
from functools import partial

import jax
import jax.numpy as jnp
from jax import lax
from jax.experimental import pallas as pl
from jax.experimental.pallas import tpu as pltpu
from jax.sharding import PartitionSpec as P

gas_density = 0.001
least = 1e-4
F32 = jnp.float32
GROUP = 4
FACES = (
    (range(13, 29), 13),
    (range(9, 13), 12),
    (range(29, 33), 12),
    (range(5, 9), 8),
    (range(33, 37), 8),
    (range(1, 5), 4),
    (range(37, 41), 4),
)


def dot(a, b):
    return lax.dot_general(
        a, b, (((1,), (0,)), ((), ())), precision=lax.Precision.HIGHEST, preferred_element_type=F32
    )


def iota(shape, axis):
    return lax.broadcasted_iota(jnp.int32, shape, axis)


def halving(offset, weight, width=128):
    row, column = iota((128, 128), 0), iota((128, 128), 1)
    return jnp.where((row // 2 + offset == column) & (row < width), weight, 0.0).astype(F32)


def doubling(width, first=0, period=128):
    row, column = iota((128, 128), 0), iota((128, 128), 1)
    hit = ((column % period) // 2 + first == row) & (row < first + width)
    return jnp.where(hit, 1.0, 0.0).astype(F32)


def inverse(a):
    return pl.reciprocal(a, approx=True)


def blocks(lo, count, block, step):
    assert count % block == 0
    if count == block:
        step(lo)
    else:

        def turn(i, _):
            step(lo + i * block)
            return 0

        lax.fori_loop(0, count // block, turn, 0)


LOWER, LEFT, OUT, INNER, INVERSE, DIAGONAL, SOURCE = 0, 2, 4, 6, 7, 9, 11
KEPT = 13


class Level:
    def __init__(self, density, keep, value, width, cross=0, ends=False):
        self.density, self.keep, self.value = density, keep, value
        self.depth, self.width, self.cross, self.ends = value.shape[2], width, cross, ends
        self.row, self.lane = iota((1, 8, 128), 1), iota((1, 8, 128), 2)
        self.odd = (self.row + self.lane) % 2 == 1

    def choose(self, mask, a, b):
        if not isinstance(a, float):
            shape, a = a.shape, a.reshape(-1, 8, 128)
        if not isinstance(b, float):
            shape, b = b.shape, b.reshape(-1, 8, 128)
        return jnp.where(mask, a, b).reshape(shape)

    def low(self, a):
        turned = pltpu.roll(a, 1, 1)
        if self.cross:
            head = turned[:, :8]
            head = jnp.where(self.row == 0, pltpu.roll(head, self.cross, 2), head)
            turned = head if self.depth == 8 else jnp.concatenate([head, turned[:, 8:]], axis=1)
        return turned

    def high(self, a):
        turned = pltpu.roll(a, self.depth - 1, 1)
        if self.cross:
            tail = turned[:, -8:]
            tail = jnp.where(self.row == 7, pltpu.roll(tail, 128 - self.cross, 2), tail)
            turned = tail if self.depth == 8 else jnp.concatenate([turned[:, :-8], tail], axis=1)
        return turned

    def coefficients(self, source, factor, lo, count, block):
        first_x, last_x = self.lane % max(self.width, 1) == 0, self.lane % max(self.width, 1) == self.width - 1
        if self.ends:
            first, last = (self.row == 0) & (self.lane < self.width), (self.row == 7) & (self.lane >= 128 - self.width)

        def coupling(a, b):
            return 2.0 * inverse(jnp.maximum(a + b, least))

        def both(place, at, even, odd):
            self.keep[place, at] = self.choose(self.odd, odd, even)
            self.keep[place + 1, at] = self.choose(self.odd, even, odd)

        def step(j):
            at = pl.ds(j, block)
            shape = (block, 2, self.depth, 128)
            rows = self.density[pl.ds(2 * j, 2 * block)].reshape(shape)
            before = self.density[pl.ds(2 * j - 1, 2 * block)].reshape(shape)[:, 0]
            after = self.density[pl.ds(2 * j + 1, 2 * block)].reshape(shape)[:, 1]
            inner = coupling(rows[:, 0], rows[:, 1])
            out = (coupling(rows[:, 0], before), coupling(rows[:, 1], after))
            parts = []
            for k in range(2):
                d = rows[:, k]
                if self.width or self.ends:
                    edge = 2.0 * inverse(jnp.maximum(d, least))
                lower = coupling(d, self.low(d))
                upper = self.high(lower)
                if self.ends:
                    lower, upper = self.choose(first, edge, lower), self.choose(last, edge, upper)
                left = coupling(d, pltpu.roll(d, 1, 2))
                right = pltpu.roll(left, 127, 2)
                if self.width:
                    left, right = self.choose(first_x, edge, left), self.choose(last_x, edge, right)
                total = lower + upper + (out[0] + inner if k == 0 else inner + out[1]) + left + right
                if self.ends:
                    lower = self.choose(first, 0.0, lower)
                if self.width:
                    left = self.choose(first_x, 0.0, left)
                parts.append((lower, left, jnp.where(d > 0.0, inverse(total), 0.0), total))
            for place, even, odd in zip((LOWER, LEFT, INVERSE, DIAGONAL), *parts):
                both(place, at, even, odd)
            both(OUT, at, out[0], out[1])
            self.keep[INNER, at] = inner
            if source is not None:
                rows = factor * source[pl.ds(2 * j, 2 * block)].reshape(shape)
                both(SOURCE, at, rows[:, 0], rows[:, 1])

        blocks(lo, count, block, step)

    def gathered(self, colour, j, block):
        at, keep = pl.ds(j, block), self.keep
        other = self.value.at[1 - colour]
        w = other[at]
        before, after = other[pl.ds(j - 1, block)], other[pl.ds(j + 1, block)]
        side = self.choose(self.odd, before, after) if colour else self.choose(self.odd, after, before)
        total = keep[INNER, at] * w + keep[OUT + colour, at] * side
        total += keep[LOWER + colour, at] * self.low(w) + self.high(keep[LOWER + 1 - colour, at] * w)
        total += keep[LEFT + colour, at] * pltpu.roll(w, 1, 2) + pltpu.roll(keep[LEFT + 1 - colour, at] * w, 127, 2)
        return total

    def first(self, lo, count, block):
        def step(j):
            at = pl.ds(j, block)
            self.value[0, at] = self.keep[SOURCE, at] * self.keep[INVERSE, at]

        blocks(lo, count, block, step)

    def half(self, colour, lo, count, block):
        def step(j):
            at = pl.ds(j, block)
            total = self.keep[SOURCE + colour, at] + self.gathered(colour, j, block)
            self.value[colour, at] = total * self.keep[INVERSE + colour, at]

        blocks(lo, count, block, step)

    def residual(self, factor, j, block):
        at, out = pl.ds(j, block), []
        for colour in (0, 1):
            total = self.keep[DIAGONAL + colour, at] * self.value[colour, at] - self.gathered(colour, j, block)
            out.append((self.keep[SOURCE + colour, at] - total) * (1.0 / factor))
        return out

    def rows(self, red, black):
        return self.choose(self.odd, black, red), self.choose(self.odd, red, black)

    def clear_red(self, pairs):
        for j in pairs:
            self.value[0, j] = jnp.zeros((self.depth, 128), F32)

    def clear(self, pairs):
        for j in pairs:
            self.value[:, j] = jnp.zeros((2, self.depth, 128), F32)


def finest_rims(right_ref, labels_ref, before_ref, after_ref, s_ref, d_ref, low_ref, high_ref, source, density):
    for ref, near in ((source, 8), (density, 7)):
        ref[0:near] = jnp.zeros((near, 8, 128), F32)
        ref[64 - near : 64] = jnp.zeros((near, 8, 128), F32)
    source[8:16] = before_ref[0:8]
    source[48:56] = after_ref[0:8]
    source[16:48] = right_ref[...]
    density[7:16] = before_ref[8:17]
    density[48:57] = after_ref[8:17]
    density[16:48] = jnp.where(labels_ref[...] == 1, gas_density, 1.0)
    for start, wide, out in ((0, source, s_ref), (5, density, d_ref)):
        rows = jnp.swapaxes(wide[...], 0, 1)
        out[...] = rows
        low_ref[start : start + 5] = rows[0:5, 8:56]
        high_ref[start : start + 5] = rows[3:8, 8:56]


def finest_window(s_ref, d_ref, before_ref, after_ref, source, density):
    for ref in (source, density):
        for rows in (pl.ds(0, 6), pl.ds(14, 6)):
            ref[rows] = jnp.zeros((6, 64, 128), F32)
    source[1:6, 8:56] = before_ref[0:5]
    source[14:19, 8:56] = after_ref[0:5]
    density[1:6, 8:56] = before_ref[5:10]
    density[14:19, 8:56] = after_ref[5:10]
    source[6:14] = s_ref[...]
    density[6:14] = d_ref[...]


def finest_down(s_ref, d_ref, before_ref, after_ref, chunk_ref, low_ref, high_ref, below_ref,
                source, density, keep, value, plane):
    finest_window(s_ref, d_ref, before_ref, after_ref, source, density)
    level = Level(density, keep, value, 128)
    level.clear((0, 9))
    value[1, 1] = jnp.zeros((64, 128), F32)
    value[1, 8] = jnp.zeros((64, 128), F32)
    level.coefficients(source, 1.0, 1, 8, 2)
    level.first(1, 8, 4)
    level.half(1, 1, 8, 4)
    level.half(0, 2, 6, 3)
    level.half(1, 2, 6, 3)

    def pooling(j):
        red, black = level.residual(1.0, 3 + j, 2)
        plane[pl.ds(j, 2)] = (red + black)[:, 16:48]
        rows = density[pl.ds(6 + 2 * j, 4), 16:48].reshape(2, 2, 32, 128)
        plane[pl.ds(4 + j, 2)] = rows[:, 0] + rows[:, 1]

    blocks(0, 4, 2, pooling)
    pooled = plane[:, pl.ds(0, 16, stride=2)] + plane[:, pl.ds(1, 16, stride=2)]
    out = dot(pooled[:4].reshape(64, 128), halving(0, 0.125)) + dot(pooled[4:].reshape(64, 128), halving(64, 0.125))
    low_ref[...] = value[1, 3:6, 8:56]
    high_ref[...] = value[1, 4:7, 8:56]
    for peer in range(GROUP):
        chunk_ref[peer] = out
    below_ref[...] = value[1, 3:7]


def folded(ref, rows, source, density, start):
    block = ref[rows]
    near, far = block[:, :24], block[:, 24:]
    left = iota(near.shape, 2) < 64
    source[start] = jnp.where(left, near, pltpu.roll(far, 64, 2))
    density[start] = jnp.where(left, pltpu.roll(near, 64, 2), far)


def middle_down(place_ref, window_ref, before_ref, after_ref, chunk_ref, kept_ref, below_ref,
                window, source, density, keep, value, plane, source2, density2, keep2, value2):
    for near, ref in ((0, before_ref), (32, after_ref)):
        window[0:44, near : near + 16] = jnp.zeros((44, 16, 128), F32)
        start = 0
        for rows, planes in FACES:
            low = 16 - planes if near == 0 else 32
            for row in rows:
                window[row + 1, low : low + planes] = ref[start : start + planes]
                start += planes
    window[1:43, 16:32] = window_ref[...]
    for row in (0, 43):
        window[row] = jnp.zeros((48, 128), F32)
    blocks(0, 44, 11, lambda r: folded(window, pl.ds(r, 11), source, density, pl.ds(r, 11)))
    level = Level(density, keep, value, 64, 64)
    level.clear((0, 21))
    for j in (1, 20):
        value[1, j] = jnp.zeros((24, 128), F32)
    level.coefficients(source, 4.0, 1, 20, 5)
    level.first(1, 20, 10)
    level.half(1, 1, 20, 10)
    level.half(0, 2, 18, 9)
    level.half(1, 2, 18, 9)
    kept_ref[...] = window[pl.ds(6 + 4 * place_ref[2], 20)]
    below_ref[...] = value[1, pl.ds(3 + 2 * place_ref[2], 10)]

    def pooling(j):
        red, black = level.residual(4.0, 3 + j, 8)
        plane[pl.ds(j, 8), 0:24] = red + black

    blocks(0, 16, 8, pooling)
    rows = density[4:40].reshape(18, 2, 24, 128)
    plane[16:34, 0:24] = rows[:, 0] + rows[:, 1]
    pooled = plane[:, pl.ds(0, 16, stride=2)] + plane[:, pl.ds(1, 16, stride=2)]
    pooled = dot(pooled.reshape(34 * 16, 128), halving(0, 0.125)).reshape(34, 16, 128)
    lane = iota((34, 16, 128), 2)
    near, far = jnp.where(lane < 32, pooled, 0.0), jnp.where(lane < 32, pltpu.roll(pooled, 96, 2), 0.0)
    for ref, start, parts in ((source2, 2, slice(0, 16)), (density2, 1, slice(16, 34))):
        ref[start : start + parts.stop - parts.start, 0:12] = near[parts, 0:12]
        ref[start : start + parts.stop - parts.start, 12:24] = far[parts, 0:12]
    for row in (0, 19):
        density2[row] = jnp.zeros((24, 128), F32)
    below = Level(density2, keep2, value2, 0)
    below.clear((0, 9))
    for j in (1, 8):
        value2[1, j] = jnp.zeros((24, 128), F32)
    below.coefficients(source2, 16.0, 1, 8, 4)
    below.first(1, 8, 8)
    below.half(1, 1, 8, 8)
    below.half(0, 2, 6, 6)
    below.half(1, 2, 6, 6)
    red, black = below.residual(16.0, 3, 4)
    plane[0:4, 0:24] = red + black
    rows = density2[6:14].reshape(4, 2, 24, 128)
    plane[4:8, 0:24] = rows[:, 0] + rows[:, 1]
    rows = []
    for row in range(4):
        for part in (row, 4 + row):
            rows.append(plane[part, pl.ds(8, 4, stride=2)] + plane[part, pl.ds(9, 4, stride=2)])
    pooled = dot(jnp.concatenate(rows, axis=0), halving(0, 0.125, 32))
    for row in range(4):
        total = pooled[8 * row : 8 * row + 1]
        for i in range(1, 8):
            total = total + pltpu.roll(pooled[8 * row + i : 8 * row + i + 1], 16 * i, 1)
        chunk_ref[0, 40 + row : 41 + row] = total
    black = jnp.zeros((8, 128), F32)
    for j in range(4):
        total = black
        for k, ref in enumerate((source2, density2, source2, density2)):
            total = total + pltpu.roll(ref[6 + 2 * j + k // 2, 8:16], 32 * k, 1)
        chunk_ref[0, 8 * j : 8 * j + 8] = total
    for j in range(4):
        black = black + pltpu.roll(value2[1, 3 + j, 8:16], 32 * j, 1)
    chunk_ref[0, 32:40] = black
    chunk_ref[0, 44:48] = jnp.zeros((4, 128), F32)
    for peer in range(1, chunk_ref.shape[0]):
        chunk_ref[peer] = chunk_ref[0]


def coarsest(place_ref, gathered_ref, source, density, keep, value, wide, besides):
    planes = wide.shape[0] - 8
    groups = gathered_ref.shape[0]
    lane = iota((8, 128), 1)
    for row in (0, 1, planes + 2, planes + 3):
        density[row] = jnp.zeros((8, 128), F32)

    def spread(g):
        tiles = [
            jnp.concatenate([gathered_ref[2 * h + k, 4 * g : 4 * g + 4] for k in range(2)], axis=0)
            for h in range(groups // 2)
        ]
        tiles += [jnp.zeros((8, 128), F32)] * (8 - len(tiles))
        for step in (1, 2, 4):
            upper = (lane // 16) % (2 * step) >= step
            for i in range(8):
                if i % (2 * step) < step:
                    a, b = tiles[i], tiles[i + step]
                    tiles[i] = jnp.where(upper, pltpu.roll(b, 16 * step, 1), a)
                    tiles[i + step] = jnp.where(upper, b, pltpu.roll(a, 128 - 16 * step, 1))
        for z in range(4):
            source[2 + 4 * g + z] = tiles[z]
            density[2 + 4 * g + z] = tiles[4 + z]

    for g in range(planes // 4):
        spread(g)
    level = Level(density, keep, value, 16, 16, ends=True)
    pairs = planes // 2
    value[...] = jnp.zeros(value.shape, F32)
    level.coefficients(source, 64.0, 1, pairs, 4)

    for turns, beside in besides:

        def sweep(i, carry):
            beside(i)
            level.half(0, 1, pairs, pairs)
            level.half(1, 1, pairs, pairs)
            return carry

        lax.fori_loop(0, turns, sweep, 0)
    wide[0:4] = jnp.zeros((4, 8, 128), F32)
    wide[planes + 4 : planes + 8] = jnp.zeros((4, 8, 128), F32)
    even, odd = level.rows(value[0, 1 : pairs + 1], value[1, 1 : pairs + 1])
    for j in range(pairs):
        wide[4 + 2 * j] = even[j]
        wide[5 + 2 * j] = odd[j]
    return wide[pl.ds(4 * place_ref[0], 12)]


def way_up(devices, place_ref, gathered_ref, halo_ref, kept_ref, below1_ref,
           s_ref, d_ref, rim_before_ref, rim_after_ref, below0_ref, before_ref, after_ref,
           pressure_ref, remain_ref,
           source3, density3, keep3, value3, wide,
           source2, density2, keep2, value2, source1, density1, keep1, value1,
           source0, density0, keep0, value0, plane):
    at_y, at_group = place_ref[1], place_ref[2]
    level1 = Level(density1, keep1, value1, 64, 64)
    finest_window(s_ref, d_ref, rim_before_ref, rim_after_ref, source0, density0)
    level0 = Level(density0, keep0, value0, 128)
    lane = iota((24, 128), 1)
    for rows in (slice(0, 2), slice(20, 22)):
        density2[rows] = jnp.zeros((2, 24, 128), F32)
    for i in range(9):
        group, part = (at_group + i) // 4, (at_group + i) % 4
        block = halo_ref[5 * group + part]
        for k in range(2):
            row = 2 + 2 * i + k
            source2[row] = pltpu.roll(block, 64, 1) if k else block
            density2[row] = jnp.where(lane < 32, pltpu.roll(block, 96 - 64 * k, 1), 0.0)
        black = pltpu.roll(halo_ref[5 * group + 4], (128 - 32 * part) % 128, 1)
        value2[1, 1 + i] = jnp.where(lane < 32, black, 0.0)
    level = Level(density2, keep2, value2, 0)
    level.clear((0, 10))

    def finest(i):
        level0.coefficients(source0, 1.0, 1 + 2 * i, 2, 2)

    def folding(i):
        rows = pl.ds(5 * i, 5)
        folded(kept_ref, rows, source1, density1, rows)
        finest(i)

    near = coarsest(
        place_ref, gathered_ref, source3, density3, keep3, value3, wide,
        (
            (4, folding),
            (3, lambda i: level.coefficients(source2, 16.0, 1 + 3 * i, 3, 3)),
            (4, lambda i: level1.coefficients(source1, 4.0, 1 + 2 * i, 2, 2)),
            (1, lambda i: None),
        ),
    )
    row = iota((8, 128), 0)
    picked = []
    for i in range(9):
        y = at_y + i - 4
        inside = (y >= 0) & (y < devices)
        y = jnp.clip(y, 0, devices - 1)
        rows = jnp.sum(jnp.where(row == y % 8, near, 0.0), axis=1)
        rows = pltpu.roll(rows, (128 - 16 * (y // 8)) % 128, 1)
        picked.append(jnp.where(inside & (iota((12, 128), 1) < 16), rows, 0.0))
        picked.append(jnp.zeros((4, 128), F32))
    spread = dot(jnp.concatenate(picked, axis=0), doubling(16)).reshape(9, 16, 128)
    plane[0:9, pl.ds(0, 12, stride=2)] = spread[:, 0:12]
    plane[0:9, pl.ds(1, 12, stride=2)] = spread[:, 0:12]
    value2[1, 1:10] = value2[1, 1:10] + plane[0:9, 0:24]
    level.half(0, 1, 9, 9)
    level.half(1, 2, 7, 7)
    level.half(0, 2, 7, 7)
    level.half(1, 3, 5, 5)
    even, odd = level.rows(value2[0, 3:8], value2[1, 3:8])

    level = level1
    rows = jnp.stack([even, odd], axis=1).reshape(240, 128)
    spread = dot(rows, doubling(32, 0, 64)).reshape(10, 24, 128)
    plane[0:10, pl.ds(0, 24, stride=2)] = spread
    plane[0:10, pl.ds(1, 24, stride=2)] = spread
    left = iota((10, 24, 128), 2) < 64
    value1[1] = below1_ref[...] + jnp.where(left, plane[0:10, 0:24], plane[0:10, 24:48])
    level.clear_red((0, 9))
    level.half(0, 1, 8, 4)
    level.half(1, 1, 8, 4)
    level.half(0, 2, 6, 6)
    level.half(1, 2, 6, 6)
    even, odd = level.rows(value1[0, 2:8], value1[1, 2:8])
    rows = jnp.stack([even, odd], axis=1).reshape(12, 24, 128)[1:11]

    level = level0
    near = dot(rows[:, 8:24].reshape(160, 128), doubling(64)).reshape(10, 16, 128)
    far = dot(rows[:, 0:16].reshape(160, 128), doubling(64, 64)).reshape(10, 16, 128)
    for start, part in ((0, near), (32, far)):
        plane[0:10, pl.ds(start, 16, stride=2)] = part
        plane[0:10, pl.ds(start + 1, 16, stride=2)] = part
    value0[1] = plane[...]
    value0[1, 0:3, 8:56] = value0[1, 0:3, 8:56] + before_ref[...]
    value0[1, 3:7] = value0[1, 3:7] + below0_ref[...]
    value0[1, 7:10, 8:56] = value0[1, 7:10, 8:56] + after_ref[...]
    level.clear_red((0, 9))
    level.half(0, 1, 8, 4)
    level.half(1, 1, 8, 4)
    level.half(0, 2, 6, 3)
    level.half(1, 2, 6, 3)
    even, odd = level.rows(value0[0, 3:7, 16:48], value0[1, 3:7, 16:48])
    pressure_ref[...] = jnp.swapaxes(jnp.stack([even, odd], axis=1).reshape(8, 32, 128), 0, 1)

    def remaining(j):
        red, black = level.residual(1.0, 3 + j, 2)
        even, odd = level.rows(red, black)
        plane[pl.ds(2 * j, 4)] = jnp.stack([even, odd], axis=1).reshape(4, 64, 128)

    blocks(0, 4, 2, remaining)
    remain_ref[...] = jnp.swapaxes(plane[0:8, 16:48], 0, 1)


def pair(array_up, array_down, axis, group=1):
    groups = lax.axis_size(axis) // group
    up = [(i * group + j, (i + 2) * group - 1 - j) for i in range(groups - 1) for j in range(group)]
    down = [(j, i) for i, j in up]
    return lax.ppermute(array_up, axis, up), lax.ppermute(array_down, axis, down)


def shape(*sizes):
    return jax.ShapeDtypeStruct(sizes, F32)


def vmem(*sizes):
    return pltpu.VMEM(sizes, F32)


def params():
    return pltpu.CompilerParams(vmem_limit_bytes=24 * 1024 * 1024)


def body(right_side, labels):
    gz, xy = lax.axis_size("gz"), lax.axis_size("xy")
    density = jnp.where(labels == 1, gas_density, 1.0).astype(F32)
    before, after = pair(
        jnp.concatenate([right_side[-8:], density[-9:]], axis=0),
        jnp.concatenate([right_side[:8], density[:9]], axis=0),
        "gz",
    )
    wide_source, wide_density, low_rim, high_rim = pl.pallas_call(
        finest_rims,
        out_shape=[shape(8, 64, 128)] * 2 + [shape(10, 48, 128)] * 2,
        scratch_shapes=[vmem(64, 8, 128)] * 2,
        compiler_params=params(),
    )(right_side, labels, before, after)
    before, after = pair(high_rim, low_rim, "xy")
    finest = (wide_source, wide_density, before, after)
    at_group = lax.axis_index("xy") % GROUP
    place = jnp.stack([lax.axis_index("gz"), lax.axis_index("xy"), at_group]).astype(jnp.int32)
    smem, block = pl.BlockSpec(memory_space=pltpu.SMEM), pl.BlockSpec(memory_space=pltpu.VMEM)
    chunks, first_rows, last_rows, below0 = pl.pallas_call(
        finest_down,
        out_shape=[shape(GROUP, 64, 128), shape(3, 48, 128), shape(3, 48, 128), shape(4, 64, 128)],
        scratch_shapes=[vmem(20, 64, 128)] * 2 + [vmem(KEPT, 10, 64, 128), vmem(2, 10, 64, 128), vmem(8, 32, 128)],
        compiler_params=params(),
    )(*finest)

    teams = [[GROUP * i + j for j in range(GROUP)] for i in range(xy // GROUP)]
    chunks = lax.all_to_all(chunks, "xy", 0, 0, axis_index_groups=teams, tiled=True)
    window = chunks.reshape(4 * GROUP, 16, 128)
    before, after = pair(window[-13:], window[:13], "xy", GROUP)
    window = jnp.concatenate([before, window, after], axis=0)

    def faces(up):
        parts = []
        for rows, planes in FACES:
            part = window[rows.start : rows.stop, 16 - planes :] if up else window[rows.start : rows.stop, :planes]
            parts.append(part.reshape(-1, 128))
        return jnp.concatenate(parts, axis=0)

    before, after = pair(faces(True), faces(False), "gz")
    chunks, kept, below1 = pl.pallas_call(
        middle_down,
        out_shape=[shape(gz, 48, 128), shape(20, 48, 128), shape(10, 24, 128)],
        in_specs=[smem] + [block] * 3,
        scratch_shapes=[vmem(44, 48, 128)]
        + [vmem(44, 24, 128)] * 2
        + [vmem(KEPT, 22, 24, 128), vmem(2, 22, 24, 128), vmem(34, 32, 128)]
        + [vmem(20, 24, 128)] * 2
        + [vmem(KEPT, 10, 24, 128), vmem(2, 10, 24, 128)],
        compiler_params=params(),
    )(place, window, before, after)

    value_before, value_after = pair(last_rows, first_rows, "xy")
    column = lax.all_to_all(chunks, "gz", 0, 0, tiled=True)
    peers = [[GROUP * i + j for i in range(xy // GROUP)] for j in range(GROUP)]
    everywhere = lax.all_to_all(
        jnp.broadcast_to(column[:, 40:44].reshape(1, 4 * gz, 128), (xy // GROUP, 4 * gz, 128)),
        "xy", 0, 0, axis_index_groups=peers, tiled=True,
    )
    halo = jnp.pad(column[:, :40], ((1, 1), (0, 0), (0, 0)))
    halo = lax.dynamic_slice(halo, (lax.axis_index("gz"), 0, 0), (3, 40, 128)).reshape(3, 5, 8, 128)
    halo = jnp.swapaxes(halo, 0, 1).reshape(5, 24, 128)
    before, after = pair(halo, halo, "xy", GROUP)
    halo = jnp.concatenate([before, halo, after], axis=0)
    planes = 4 * gz
    return pl.pallas_call(
        partial(way_up, xy),
        out_shape=[shape(32, 8, 128)] * 2,
        in_specs=[smem] + [block] * 11,
        scratch_shapes=[vmem(planes + 4, 8, 128)] * 2
        + [vmem(KEPT, planes // 2 + 2, 8, 128), vmem(2, planes // 2 + 2, 8, 128), vmem(planes + 8, 8, 128)]
        + [vmem(22, 24, 128)] * 2
        + [vmem(KEPT, 11, 24, 128), vmem(2, 11, 24, 128)]
        + [vmem(20, 24, 128)] * 2
        + [vmem(KEPT, 10, 24, 128), vmem(2, 10, 24, 128)]
        + [vmem(20, 64, 128)] * 2
        + [vmem(KEPT, 10, 64, 128), vmem(2, 10, 64, 128), vmem(10, 64, 128)],
        compiler_params=params(),
    )(place, everywhere, halo, kept, below1, *finest, below0, value_before, value_after)


def solution(mesh):
    return jax.shard_map(
        body,
        mesh=mesh,
        in_specs=(P("gz", "xy", None), P("gz", "xy", None)),
        out_specs=(P("gz", "xy", None), P("gz", "xy", None)),
        check_vma=False,
    )
```

```python
from functools import partial

import jax
import jax.numpy as jnp
from jax import lax
from jax.experimental import pallas as pl
from jax.experimental.pallas import tpu as pltpu
from jax.sharding import PartitionSpec as P

gas_density = 0.001
least = 1e-4
F32 = jnp.float32
GROUP = 4
FACES = (
    (range(13, 29), 13),
    (range(9, 13), 12),
    (range(29, 33), 12),
    (range(5, 9), 8),
    (range(33, 37), 8),
    (range(1, 5), 4),
    (range(37, 41), 4),
)


def dot(a, b):
    return lax.dot_general(
        a, b, (((1,), (0,)), ((), ())), precision=lax.Precision.HIGHEST, preferred_element_type=F32
    )


def iota(shape, axis):
    return lax.broadcasted_iota(jnp.int32, shape, axis)


def halving(offset, weight, width=128):
    row, column = iota((128, 128), 0), iota((128, 128), 1)
    return jnp.where((row // 2 + offset == column) & (row < width), weight, 0.0).astype(F32)


def doubling(width, first=0, period=128):
    row, column = iota((128, 128), 0), iota((128, 128), 1)
    hit = ((column % period) // 2 + first == row) & (row < first + width)
    return jnp.where(hit, 1.0, 0.0).astype(F32)


def inverse(a):
    return pl.reciprocal(a, approx=True)


def blocks(lo, count, block, step):
    assert count % block == 0
    if count == block:
        step(lo)
    else:

        def turn(i, _):
            step(lo + i * block)
            return 0

        lax.fori_loop(0, count // block, turn, 0)


LOWER, LEFT, OUT, INNER, INVERSE, DIAGONAL, SOURCE = 0, 2, 4, 6, 7, 9, 11
KEPT = 13


class Level:
    def __init__(self, density, keep, value, width, cross=0, ends=False):
        self.density, self.keep, self.value = density, keep, value
        self.depth, self.width, self.cross, self.ends = value.shape[2], width, cross, ends
        self.row, self.lane = iota((1, 8, 128), 1), iota((1, 8, 128), 2)
        self.odd = (self.row + self.lane) % 2 == 1

    def choose(self, mask, a, b):
        if not isinstance(a, float):
            shape, a = a.shape, a.reshape(-1, 8, 128)
        if not isinstance(b, float):
            shape, b = b.shape, b.reshape(-1, 8, 128)
        return jnp.where(mask, a, b).reshape(shape)

    def low(self, a):
        turned = pltpu.roll(a, 1, 1)
        if self.cross:
            head = turned[:, :8]
            head = jnp.where(self.row == 0, pltpu.roll(head, self.cross, 2), head)
            turned = head if self.depth == 8 else jnp.concatenate([head, turned[:, 8:]], axis=1)
        return turned

    def high(self, a):
        turned = pltpu.roll(a, self.depth - 1, 1)
        if self.cross:
            tail = turned[:, -8:]
            tail = jnp.where(self.row == 7, pltpu.roll(tail, 128 - self.cross, 2), tail)
            turned = tail if self.depth == 8 else jnp.concatenate([turned[:, :-8], tail], axis=1)
        return turned

    def coefficients(self, source, factor, lo, count, block):
        first_x, last_x = self.lane % max(self.width, 1) == 0, self.lane % max(self.width, 1) == self.width - 1
        if self.ends:
            first, last = (self.row == 0) & (self.lane < self.width), (self.row == 7) & (self.lane >= 128 - self.width)

        def coupling(a, b):
            return 2.0 * inverse(jnp.maximum(a + b, least))

        def both(place, at, even, odd):
            self.keep[place, at] = self.choose(self.odd, odd, even)
            self.keep[place + 1, at] = self.choose(self.odd, even, odd)

        def step(j):
            at = pl.ds(j, block)
            shape = (block, 2, self.depth, 128)
            rows = self.density[pl.ds(2 * j, 2 * block)].reshape(shape)
            before = self.density[pl.ds(2 * j - 1, 2 * block)].reshape(shape)[:, 0]
            after = self.density[pl.ds(2 * j + 1, 2 * block)].reshape(shape)[:, 1]
            inner = coupling(rows[:, 0], rows[:, 1])
            out = (coupling(rows[:, 0], before), coupling(rows[:, 1], after))
            parts = []
            for k in range(2):
                d = rows[:, k]
                if self.width or self.ends:
                    edge = 2.0 * inverse(jnp.maximum(d, least))
                lower = coupling(d, self.low(d))
                upper = self.high(lower)
                if self.ends:
                    lower, upper = self.choose(first, edge, lower), self.choose(last, edge, upper)
                left = coupling(d, pltpu.roll(d, 1, 2))
                right = pltpu.roll(left, 127, 2)
                if self.width:
                    left, right = self.choose(first_x, edge, left), self.choose(last_x, edge, right)
                total = lower + upper + (out[0] + inner if k == 0 else inner + out[1]) + left + right
                if self.ends:
                    lower = self.choose(first, 0.0, lower)
                if self.width:
                    left = self.choose(first_x, 0.0, left)
                parts.append((lower, left, jnp.where(d > 0.0, inverse(total), 0.0), total))
            for place, even, odd in zip((LOWER, LEFT, INVERSE, DIAGONAL), *parts):
                both(place, at, even, odd)
            both(OUT, at, out[0], out[1])
            self.keep[INNER, at] = inner
            if source is not None:
                rows = factor * source[pl.ds(2 * j, 2 * block)].reshape(shape)
                both(SOURCE, at, rows[:, 0], rows[:, 1])

        blocks(lo, count, block, step)

    def gathered(self, colour, j, block):
        at, keep = pl.ds(j, block), self.keep
        other = self.value.at[1 - colour]
        w = other[at]
        before, after = other[pl.ds(j - 1, block)], other[pl.ds(j + 1, block)]
        side = self.choose(self.odd, before, after) if colour else self.choose(self.odd, after, before)
        total = keep[INNER, at] * w + keep[OUT + colour, at] * side
        total += keep[LOWER + colour, at] * self.low(w) + self.high(keep[LOWER + 1 - colour, at] * w)
        total += keep[LEFT + colour, at] * pltpu.roll(w, 1, 2) + pltpu.roll(keep[LEFT + 1 - colour, at] * w, 127, 2)
        return total

    def first(self, lo, count, block):
        def step(j):
            at = pl.ds(j, block)
            self.value[0, at] = self.keep[SOURCE, at] * self.keep[INVERSE, at]

        blocks(lo, count, block, step)

    def half(self, colour, lo, count, block):
        def step(j):
            at = pl.ds(j, block)
            total = self.keep[SOURCE + colour, at] + self.gathered(colour, j, block)
            self.value[colour, at] = total * self.keep[INVERSE + colour, at]

        blocks(lo, count, block, step)

    def residual(self, factor, j, block):
        at, out = pl.ds(j, block), []
        for colour in (0, 1):
            total = self.keep[DIAGONAL + colour, at] * self.value[colour, at] - self.gathered(colour, j, block)
            out.append((self.keep[SOURCE + colour, at] - total) * (1.0 / factor))
        return out

    def rows(self, red, black):
        return self.choose(self.odd, black, red), self.choose(self.odd, red, black)

    def clear_red(self, pairs):
        for j in pairs:
            self.value[0, j] = jnp.zeros((self.depth, 128), F32)

    def clear(self, pairs):
        for j in pairs:
            self.value[:, j] = jnp.zeros((2, self.depth, 128), F32)


def finest_rims(right_ref, labels_ref, before_ref, after_ref, s_ref, d_ref, low_ref, high_ref, source, density):
    for ref, near in ((source, 8), (density, 7)):
        ref[0:near] = jnp.zeros((near, 8, 128), F32)
        ref[64 - near : 64] = jnp.zeros((near, 8, 128), F32)
    source[8:16] = before_ref[0:8]
    source[48:56] = after_ref[0:8]
    source[16:48] = right_ref[...]
    density[7:16] = before_ref[8:17]
    density[48:57] = after_ref[8:17]
    density[16:48] = jnp.where(labels_ref[...] == 1, gas_density, 1.0)
    for start, wide, out in ((0, source, s_ref), (5, density, d_ref)):
        rows = jnp.swapaxes(wide[...], 0, 1)
        out[...] = rows
        low_ref[start : start + 5] = rows[0:5, 8:56]
        high_ref[start : start + 5] = rows[3:8, 8:56]


def finest_window(s_ref, d_ref, before_ref, after_ref, source, density):
    for ref in (source, density):
        for rows in (pl.ds(0, 6), pl.ds(14, 6)):
            ref[rows] = jnp.zeros((6, 64, 128), F32)
    source[1:6, 8:56] = before_ref[0:5]
    source[14:19, 8:56] = after_ref[0:5]
    density[1:6, 8:56] = before_ref[5:10]
    density[14:19, 8:56] = after_ref[5:10]
    source[6:14] = s_ref[...]
    density[6:14] = d_ref[...]


def finest_down(s_ref, d_ref, before_ref, after_ref, chunk_ref, low_ref, high_ref, below_ref,
                source, density, keep, value, plane):
    finest_window(s_ref, d_ref, before_ref, after_ref, source, density)
    level = Level(density, keep, value, 128)
    level.clear((0, 9))
    value[1, 1] = jnp.zeros((64, 128), F32)
    value[1, 8] = jnp.zeros((64, 128), F32)
    level.coefficients(source, 1.0, 1, 8, 2)
    level.first(1, 8, 4)
    level.half(1, 1, 8, 4)
    level.half(0, 2, 6, 3)
    level.half(1, 2, 6, 3)

    def pooling(j):
        red, black = level.residual(1.0, 3 + j, 2)
        plane[pl.ds(j, 2)] = (red + black)[:, 16:48]
        rows = density[pl.ds(6 + 2 * j, 4), 16:48].reshape(2, 2, 32, 128)
        plane[pl.ds(4 + j, 2)] = rows[:, 0] + rows[:, 1]

    blocks(0, 4, 2, pooling)
    pooled = plane[:, pl.ds(0, 16, stride=2)] + plane[:, pl.ds(1, 16, stride=2)]
    out = dot(pooled[:4].reshape(64, 128), halving(0, 0.125)) + dot(pooled[4:].reshape(64, 128), halving(64, 0.125))
    low_ref[...] = value[1, 3:6, 8:56]
    high_ref[...] = value[1, 4:7, 8:56]
    for peer in range(GROUP):
        chunk_ref[peer] = out
    below_ref[...] = value[1, 3:7]


def folded(ref, rows, source, density, start):
    block = ref[rows]
    near, far = block[:, :24], block[:, 24:]
    left = iota(near.shape, 2) < 64
    source[start] = jnp.where(left, near, pltpu.roll(far, 64, 2))
    density[start] = jnp.where(left, pltpu.roll(near, 64, 2), far)


def middle_down(place_ref, window_ref, before_ref, after_ref, chunk_ref, kept_ref, below_ref,
                window, source, density, keep, value, plane, source2, density2, keep2, value2):
    for near, ref in ((0, before_ref), (32, after_ref)):
        window[0:44, near : near + 16] = jnp.zeros((44, 16, 128), F32)
        start = 0
        for rows, planes in FACES:
            low = 16 - planes if near == 0 else 32
            for row in rows:
                window[row + 1, low : low + planes] = ref[start : start + planes]
                start += planes
    window[1:43, 16:32] = window_ref[...]
    for row in (0, 43):
        window[row] = jnp.zeros((48, 128), F32)
    blocks(0, 44, 11, lambda r: folded(window, pl.ds(r, 11), source, density, pl.ds(r, 11)))
    level = Level(density, keep, value, 64, 64)
    level.clear((0, 21))
    for j in (1, 20):
        value[1, j] = jnp.zeros((24, 128), F32)
    level.coefficients(source, 4.0, 1, 20, 5)
    level.first(1, 20, 10)
    level.half(1, 1, 20, 10)
    level.half(0, 2, 18, 9)
    level.half(1, 2, 18, 9)
    kept_ref[...] = window[pl.ds(6 + 4 * place_ref[2], 20)]
    below_ref[...] = value[1, pl.ds(3 + 2 * place_ref[2], 10)]

    def pooling(j):
        red, black = level.residual(4.0, 3 + j, 8)
        plane[pl.ds(j, 8), 0:24] = red + black

    blocks(0, 16, 8, pooling)
    rows = density[4:40].reshape(18, 2, 24, 128)
    plane[16:34, 0:24] = rows[:, 0] + rows[:, 1]
    pooled = plane[:, pl.ds(0, 16, stride=2)] + plane[:, pl.ds(1, 16, stride=2)]
    pooled = dot(pooled.reshape(34 * 16, 128), halving(0, 0.125)).reshape(34, 16, 128)
    lane = iota((34, 16, 128), 2)
    near, far = jnp.where(lane < 32, pooled, 0.0), jnp.where(lane < 32, pltpu.roll(pooled, 96, 2), 0.0)
    for ref, start, parts in ((source2, 2, slice(0, 16)), (density2, 1, slice(16, 34))):
        ref[start : start + parts.stop - parts.start, 0:12] = near[parts, 0:12]
        ref[start : start + parts.stop - parts.start, 12:24] = far[parts, 0:12]
    for row in (0, 19):
        density2[row] = jnp.zeros((24, 128), F32)
    below = Level(density2, keep2, value2, 0)
    below.clear((0, 9))
    for j in (1, 8):
        value2[1, j] = jnp.zeros((24, 128), F32)
    below.coefficients(source2, 16.0, 1, 8, 4)
    below.first(1, 8, 8)
    below.half(1, 1, 8, 8)
    below.half(0, 2, 6, 6)
    below.half(1, 2, 6, 6)
    red, black = below.residual(16.0, 3, 4)
    plane[0:4, 0:24] = red + black
    rows = density2[6:14].reshape(4, 2, 24, 128)
    plane[4:8, 0:24] = rows[:, 0] + rows[:, 1]
    rows = []
    for row in range(4):
        for part in (row, 4 + row):
            rows.append(plane[part, pl.ds(8, 4, stride=2)] + plane[part, pl.ds(9, 4, stride=2)])
    pooled = dot(jnp.concatenate(rows, axis=0), halving(0, 0.125, 32))
    for row in range(4):
        total = pooled[8 * row : 8 * row + 1]
        for i in range(1, 8):
            total = total + pltpu.roll(pooled[8 * row + i : 8 * row + i + 1], 16 * i, 1)
        chunk_ref[0, 40 + row : 41 + row] = total
    black = jnp.zeros((8, 128), F32)
    for j in range(4):
        total = black
        for k, ref in enumerate((source2, density2, source2, density2)):
            total = total + pltpu.roll(ref[6 + 2 * j + k // 2, 8:16], 32 * k, 1)
        chunk_ref[0, 8 * j : 8 * j + 8] = total
    for j in range(4):
        black = black + pltpu.roll(value2[1, 3 + j, 8:16], 32 * j, 1)
    chunk_ref[0, 32:40] = black
    chunk_ref[0, 44:48] = jnp.zeros((4, 128), F32)
    for peer in range(1, chunk_ref.shape[0]):
        chunk_ref[peer] = chunk_ref[0]


def coarsest(place_ref, gathered_ref, source, density, keep, value, wide, besides):
    planes = wide.shape[0] - 8
    groups = gathered_ref.shape[0]
    lane = iota((8, 128), 1)
    for row in (0, 1, planes + 2, planes + 3):
        density[row] = jnp.zeros((8, 128), F32)

    def spread(g):
        tiles = [
            jnp.concatenate([gathered_ref[2 * h + k, 4 * g : 4 * g + 4] for k in range(2)], axis=0)
            for h in range(groups // 2)
        ]
        tiles += [jnp.zeros((8, 128), F32)] * (8 - len(tiles))
        for step in (1, 2, 4):
            upper = (lane // 16) % (2 * step) >= step
            for i in range(8):
                if i % (2 * step) < step:
                    a, b = tiles[i], tiles[i + step]
                    tiles[i] = jnp.where(upper, pltpu.roll(b, 16 * step, 1), a)
                    tiles[i + step] = jnp.where(upper, b, pltpu.roll(a, 128 - 16 * step, 1))
        for z in range(4):
            source[2 + 4 * g + z] = tiles[z]
            density[2 + 4 * g + z] = tiles[4 + z]

    for g in range(planes // 4):
        spread(g)
    level = Level(density, keep, value, 16, 16, ends=True)
    pairs = planes // 2
    value[...] = jnp.zeros(value.shape, F32)
    level.coefficients(source, 64.0, 1, pairs, 4)

    for turns, beside in besides:

        def sweep(i, carry):
            beside(i)
            level.half(0, 1, pairs, pairs)
            level.half(1, 1, pairs, pairs)
            return carry

        lax.fori_loop(0, turns, sweep, 0)
    wide[0:4] = jnp.zeros((4, 8, 128), F32)
    wide[planes + 4 : planes + 8] = jnp.zeros((4, 8, 128), F32)
    even, odd = level.rows(value[0, 1 : pairs + 1], value[1, 1 : pairs + 1])
    for j in range(pairs):
        wide[4 + 2 * j] = even[j]
        wide[5 + 2 * j] = odd[j]
    return wide[pl.ds(4 * place_ref[0], 12)]


def way_up(devices, place_ref, gathered_ref, halo_ref, kept_ref, below1_ref,
           s_ref, d_ref, rim_before_ref, rim_after_ref, below0_ref, before_ref, after_ref,
           pressure_ref, remain_ref,
           source3, density3, keep3, value3, wide,
           source2, density2, keep2, value2, source1, density1, keep1, value1,
           source0, density0, keep0, value0, plane):
    at_y, at_group = place_ref[1], place_ref[2]
    level1 = Level(density1, keep1, value1, 64, 64)
    finest_window(s_ref, d_ref, rim_before_ref, rim_after_ref, source0, density0)
    level0 = Level(density0, keep0, value0, 128)
    lane = iota((24, 128), 1)
    for rows in (slice(0, 2), slice(20, 22)):
        density2[rows] = jnp.zeros((2, 24, 128), F32)
    for i in range(9):
        group, part = (at_group + i) // 4, (at_group + i) % 4
        block = halo_ref[5 * group + part]
        for k in range(2):
            row = 2 + 2 * i + k
            source2[row] = pltpu.roll(block, 64, 1) if k else block
            density2[row] = jnp.where(lane < 32, pltpu.roll(block, 96 - 64 * k, 1), 0.0)
        black = pltpu.roll(halo_ref[5 * group + 4], (128 - 32 * part) % 128, 1)
        value2[1, 1 + i] = jnp.where(lane < 32, black, 0.0)
    level = Level(density2, keep2, value2, 0)
    level.clear((0, 10))

    def finest(i):
        level0.coefficients(source0, 1.0, 1 + 2 * i, 2, 2)

    def folding(i):
        rows = pl.ds(5 * i, 5)
        folded(kept_ref, rows, source1, density1, rows)
        finest(i)

    near = coarsest(
        place_ref, gathered_ref, source3, density3, keep3, value3, wide,
        (
            (4, folding),
            (3, lambda i: level.coefficients(source2, 16.0, 1 + 3 * i, 3, 3)),
            (4, lambda i: level1.coefficients(source1, 4.0, 1 + 2 * i, 2, 2)),
            (1, lambda i: None),
        ),
    )
    row = iota((8, 128), 0)
    picked = []
    for i in range(9):
        y = at_y + i - 4
        inside = (y >= 0) & (y < devices)
        y = jnp.clip(y, 0, devices - 1)
        rows = jnp.sum(jnp.where(row == y % 8, near, 0.0), axis=1)
        rows = pltpu.roll(rows, (128 - 16 * (y // 8)) % 128, 1)
        picked.append(jnp.where(inside & (iota((12, 128), 1) < 16), rows, 0.0))
        picked.append(jnp.zeros((4, 128), F32))
    spread = dot(jnp.concatenate(picked, axis=0), doubling(16)).reshape(9, 16, 128)
    plane[0:9, pl.ds(0, 12, stride=2)] = spread[:, 0:12]
    plane[0:9, pl.ds(1, 12, stride=2)] = spread[:, 0:12]
    value2[1, 1:10] = value2[1, 1:10] + plane[0:9, 0:24]
    level.half(0, 1, 9, 9)
    level.half(1, 2, 7, 7)
    level.half(0, 2, 7, 7)
    level.half(1, 3, 5, 5)
    even, odd = level.rows(value2[0, 3:8], value2[1, 3:8])

    level = level1
    rows = jnp.stack([even, odd], axis=1).reshape(240, 128)
    spread = dot(rows, doubling(32, 0, 64)).reshape(10, 24, 128)
    plane[0:10, pl.ds(0, 24, stride=2)] = spread
    plane[0:10, pl.ds(1, 24, stride=2)] = spread
    left = iota((10, 24, 128), 2) < 64
    value1[1] = below1_ref[...] + jnp.where(left, plane[0:10, 0:24], plane[0:10, 24:48])
    level.clear_red((0, 9))
    level.half(0, 1, 8, 4)
    level.half(1, 1, 8, 4)
    level.half(0, 2, 6, 6)
    level.half(1, 2, 6, 6)
    even, odd = level.rows(value1[0, 2:8], value1[1, 2:8])
    rows = jnp.stack([even, odd], axis=1).reshape(12, 24, 128)[1:11]

    level = level0
    near = dot(rows[:, 8:24].reshape(160, 128), doubling(64)).reshape(10, 16, 128)
    far = dot(rows[:, 0:16].reshape(160, 128), doubling(64, 64)).reshape(10, 16, 128)
    for start, part in ((0, near), (32, far)):
        plane[0:10, pl.ds(start, 16, stride=2)] = part
        plane[0:10, pl.ds(start + 1, 16, stride=2)] = part
    value0[1] = plane[...]
    value0[1, 0:3, 8:56] = value0[1, 0:3, 8:56] + before_ref[...]
    value0[1, 3:7] = value0[1, 3:7] + below0_ref[...]
    value0[1, 7:10, 8:56] = value0[1, 7:10, 8:56] + after_ref[...]
    level.clear_red((0, 9))
    level.half(0, 1, 8, 4)
    level.half(1, 1, 8, 4)
    level.half(0, 2, 6, 3)
    level.half(1, 2, 6, 3)
    even, odd = level.rows(value0[0, 3:7, 16:48], value0[1, 3:7, 16:48])
    pressure_ref[...] = jnp.swapaxes(jnp.stack([even, odd], axis=1).reshape(8, 32, 128), 0, 1)

    def remaining(j):
        red, black = level.residual(1.0, 3 + j, 2)
        even, odd = level.rows(red, black)
        plane[pl.ds(2 * j, 4)] = jnp.stack([even, odd], axis=1).reshape(4, 64, 128)

    blocks(0, 4, 2, remaining)
    remain_ref[...] = jnp.swapaxes(plane[0:8, 16:48], 0, 1)


def pair(array_up, array_down, axis, group=1):
    groups = lax.axis_size(axis) // group
    up = [(i * group + j, (i + 2) * group - 1 - j) for i in range(groups - 1) for j in range(group)]
    down = [(j, i) for i, j in up]
    return lax.ppermute(array_up, axis, up), lax.ppermute(array_down, axis, down)


def shape(*sizes):
    return jax.ShapeDtypeStruct(sizes, F32)


def vmem(*sizes):
    return pltpu.VMEM(sizes, F32)


def params():
    return pltpu.CompilerParams(vmem_limit_bytes=24 * 1024 * 1024)


def body(right_side, labels):
    gz, xy = lax.axis_size("gz"), lax.axis_size("xy")
    density = jnp.where(labels == 1, gas_density, 1.0).astype(F32)
    before, after = pair(
        jnp.concatenate([right_side[-8:], density[-9:]], axis=0),
        jnp.concatenate([right_side[:8], density[:9]], axis=0),
        "gz",
    )
    wide_source, wide_density, low_rim, high_rim = pl.pallas_call(
        finest_rims,
        out_shape=[shape(8, 64, 128)] * 2 + [shape(10, 48, 128)] * 2,
        scratch_shapes=[vmem(64, 8, 128)] * 2,
        compiler_params=params(),
    )(right_side, labels, before, after)
    before, after = pair(high_rim, low_rim, "xy")
    finest = (wide_source, wide_density, before, after)
    at_group = lax.axis_index("xy") % GROUP
    place = jnp.stack([lax.axis_index("gz"), lax.axis_index("xy"), at_group]).astype(jnp.int32)
    smem, block = pl.BlockSpec(memory_space=pltpu.SMEM), pl.BlockSpec(memory_space=pltpu.VMEM)
    chunks, first_rows, last_rows, below0 = pl.pallas_call(
        finest_down,
        out_shape=[shape(GROUP, 64, 128), shape(3, 48, 128), shape(3, 48, 128), shape(4, 64, 128)],
        scratch_shapes=[vmem(20, 64, 128)] * 2 + [vmem(KEPT, 10, 64, 128), vmem(2, 10, 64, 128), vmem(8, 32, 128)],
        compiler_params=params(),
    )(*finest)

    teams = [[GROUP * i + j for j in range(GROUP)] for i in range(xy // GROUP)]
    chunks = lax.all_to_all(chunks, "xy", 0, 0, axis_index_groups=teams, tiled=True)
    window = chunks.reshape(4 * GROUP, 16, 128)
    before, after = pair(window[-13:], window[:13], "xy", GROUP)
    window = jnp.concatenate([before, window, after], axis=0)

    def faces(up):
        parts = []
        for rows, planes in FACES:
            part = window[rows.start : rows.stop, 16 - planes :] if up else window[rows.start : rows.stop, :planes]
            parts.append(part.reshape(-1, 128))
        return jnp.concatenate(parts, axis=0)

    before, after = pair(faces(True), faces(False), "gz")
    rims = pair(last_rows, first_rows, "xy")
    before, after, value_before, value_after = lax.optimization_barrier((before, after, *rims))
    chunks, kept, below1 = pl.pallas_call(
        middle_down,
        out_shape=[shape(gz, 48, 128), shape(20, 48, 128), shape(10, 24, 128)],
        in_specs=[smem] + [block] * 3,
        scratch_shapes=[vmem(44, 48, 128)]
        + [vmem(44, 24, 128)] * 2
        + [vmem(KEPT, 22, 24, 128), vmem(2, 22, 24, 128), vmem(34, 32, 128)]
        + [vmem(20, 24, 128)] * 2
        + [vmem(KEPT, 10, 24, 128), vmem(2, 10, 24, 128)],
        compiler_params=params(),
    )(place, window, before, after)

    column = lax.all_to_all(chunks, "gz", 0, 0, tiled=True)
    peers = [[GROUP * i + j for i in range(xy // GROUP)] for j in range(GROUP)]
    everywhere = lax.all_to_all(
        jnp.broadcast_to(column[:, 40:44].reshape(1, 4 * gz, 128), (xy // GROUP, 4 * gz, 128)),
        "xy", 0, 0, axis_index_groups=peers, tiled=True,
    )
    halo = jnp.pad(column[:, :40], ((1, 1), (0, 0), (0, 0)))
    halo = lax.dynamic_slice(halo, (lax.axis_index("gz"), 0, 0), (3, 40, 128)).reshape(3, 5, 8, 128)
    halo = jnp.swapaxes(halo, 0, 1).reshape(5, 24, 128)
    before, after = pair(halo, halo, "xy", GROUP)
    halo = jnp.concatenate([before, halo, after], axis=0)
    planes = 4 * gz
    return pl.pallas_call(
        partial(way_up, xy),
        out_shape=[shape(32, 8, 128)] * 2,
        in_specs=[smem] + [block] * 11,
        scratch_shapes=[vmem(planes + 4, 8, 128)] * 2
        + [vmem(KEPT, planes // 2 + 2, 8, 128), vmem(2, planes // 2 + 2, 8, 128), vmem(planes + 8, 8, 128)]
        + [vmem(22, 24, 128)] * 2
        + [vmem(KEPT, 11, 24, 128), vmem(2, 11, 24, 128)]
        + [vmem(20, 24, 128)] * 2
        + [vmem(KEPT, 10, 24, 128), vmem(2, 10, 24, 128)]
        + [vmem(20, 64, 128)] * 2
        + [vmem(KEPT, 10, 64, 128), vmem(2, 10, 64, 128), vmem(10, 64, 128)],
        compiler_params=params(),
    )(place, everywhere, halo, kept, below1, *finest, below0, value_before, value_after)


def solution(mesh):
    return jax.shard_map(
        body,
        mesh=mesh,
        in_specs=(P("gz", "xy", None), P("gz", "xy", None)),
        out_specs=(P("gz", "xy", None), P("gz", "xy", None)),
        check_vma=False,
    )
```

```python
from functools import partial

import jax
import jax.numpy as jnp
from jax import lax
from jax.experimental import pallas as pl
from jax.experimental.pallas import tpu as pltpu
from jax.sharding import PartitionSpec as P

gas_density = 0.001
least = 1e-4
F32 = jnp.float32
GROUP = 4
FACES = (
    (range(13, 29), 13),
    (range(9, 13), 12),
    (range(29, 33), 12),
    (range(5, 9), 8),
    (range(33, 37), 8),
    (range(1, 5), 4),
    (range(37, 41), 4),
)


def dot(a, b):
    return lax.dot_general(
        a, b, (((1,), (0,)), ((), ())), precision=lax.Precision.HIGHEST, preferred_element_type=F32
    )


def iota(shape, axis):
    return lax.broadcasted_iota(jnp.int32, shape, axis)


def halving(offset, weight, width=128):
    row, column = iota((128, 128), 0), iota((128, 128), 1)
    return jnp.where((row // 2 + offset == column) & (row < width), weight, 0.0).astype(F32)


def doubling(width, first=0, period=128):
    row, column = iota((128, 128), 0), iota((128, 128), 1)
    hit = ((column % period) // 2 + first == row) & (row < first + width)
    return jnp.where(hit, 1.0, 0.0).astype(F32)


def inverse(a):
    return pl.reciprocal(a, approx=True)


def blocks(lo, count, block, step):
    assert count % block == 0
    if count == block:
        step(lo)
    else:

        def turn(i, _):
            step(lo + i * block)
            return 0

        lax.fori_loop(0, count // block, turn, 0)


LOWER, LEFT, OUT, INNER, INVERSE, DIAGONAL, SOURCE = 0, 2, 4, 6, 7, 9, 11
KEPT = 13


class Level:
    def __init__(self, density, keep, value, width, cross=0, ends=False):
        self.density, self.keep, self.value = density, keep, value
        self.depth, self.width, self.cross, self.ends = value.shape[2], width, cross, ends
        self.row, self.lane = iota((1, 8, 128), 1), iota((1, 8, 128), 2)
        self.odd = (self.row + self.lane) % 2 == 1

    def choose(self, mask, a, b):
        if not isinstance(a, float):
            shape, a = a.shape, a.reshape(-1, 8, 128)
        if not isinstance(b, float):
            shape, b = b.shape, b.reshape(-1, 8, 128)
        return jnp.where(mask, a, b).reshape(shape)

    def low(self, a):
        turned = pltpu.roll(a, 1, 1)
        if self.cross:
            head = turned[:, :8]
            head = jnp.where(self.row == 0, pltpu.roll(head, self.cross, 2), head)
            turned = head if self.depth == 8 else jnp.concatenate([head, turned[:, 8:]], axis=1)
        return turned

    def high(self, a):
        turned = pltpu.roll(a, self.depth - 1, 1)
        if self.cross:
            tail = turned[:, -8:]
            tail = jnp.where(self.row == 7, pltpu.roll(tail, 128 - self.cross, 2), tail)
            turned = tail if self.depth == 8 else jnp.concatenate([turned[:, :-8], tail], axis=1)
        return turned

    def coefficients(self, source, factor, lo, count, block):
        first_x, last_x = self.lane % max(self.width, 1) == 0, self.lane % max(self.width, 1) == self.width - 1
        if self.ends:
            first, last = (self.row == 0) & (self.lane < self.width), (self.row == 7) & (self.lane >= 128 - self.width)

        def coupling(a, b):
            return 2.0 * inverse(jnp.maximum(a + b, least))

        def both(place, at, even, odd):
            self.keep[place, at] = self.choose(self.odd, odd, even)
            self.keep[place + 1, at] = self.choose(self.odd, even, odd)

        def step(j):
            at = pl.ds(j, block)
            shape = (block, 2, self.depth, 128)
            rows = self.density[pl.ds(2 * j, 2 * block)].reshape(shape)
            before = self.density[pl.ds(2 * j - 1, 2 * block)].reshape(shape)[:, 0]
            after = self.density[pl.ds(2 * j + 1, 2 * block)].reshape(shape)[:, 1]
            inner = coupling(rows[:, 0], rows[:, 1])
            out = (coupling(rows[:, 0], before), coupling(rows[:, 1], after))
            parts = []
            for k in range(2):
                d = rows[:, k]
                if self.width or self.ends:
                    edge = 2.0 * inverse(jnp.maximum(d, least))
                lower = coupling(d, self.low(d))
                upper = self.high(lower)
                if self.ends:
                    lower, upper = self.choose(first, edge, lower), self.choose(last, edge, upper)
                left = coupling(d, pltpu.roll(d, 1, 2))
                right = pltpu.roll(left, 127, 2)
                if self.width:
                    left, right = self.choose(first_x, edge, left), self.choose(last_x, edge, right)
                total = lower + upper + (out[0] + inner if k == 0 else inner + out[1]) + left + right
                if self.ends:
                    lower = self.choose(first, 0.0, lower)
                if self.width:
                    left = self.choose(first_x, 0.0, left)
                parts.append((lower, left, jnp.where(d > 0.0, inverse(total), 0.0), total))
            for place, even, odd in zip((LOWER, LEFT, INVERSE, DIAGONAL), *parts):
                both(place, at, even, odd)
            both(OUT, at, out[0], out[1])
            self.keep[INNER, at] = inner
            if source is not None:
                rows = factor * source[pl.ds(2 * j, 2 * block)].reshape(shape)
                both(SOURCE, at, rows[:, 0], rows[:, 1])

        blocks(lo, count, block, step)

    def gathered(self, colour, j, block):
        at, keep = pl.ds(j, block), self.keep
        other = self.value.at[1 - colour]
        w = other[at]
        before, after = other[pl.ds(j - 1, block)], other[pl.ds(j + 1, block)]
        side = self.choose(self.odd, before, after) if colour else self.choose(self.odd, after, before)
        total = keep[INNER, at] * w + keep[OUT + colour, at] * side
        total += keep[LOWER + colour, at] * self.low(w) + self.high(keep[LOWER + 1 - colour, at] * w)
        total += keep[LEFT + colour, at] * pltpu.roll(w, 1, 2) + pltpu.roll(keep[LEFT + 1 - colour, at] * w, 127, 2)
        return total

    def first(self, lo, count, block):
        def step(j):
            at = pl.ds(j, block)
            self.value[0, at] = self.keep[SOURCE, at] * self.keep[INVERSE, at]

        blocks(lo, count, block, step)

    def half(self, colour, lo, count, block):
        def step(j):
            at = pl.ds(j, block)
            total = self.keep[SOURCE + colour, at] + self.gathered(colour, j, block)
            self.value[colour, at] = total * self.keep[INVERSE + colour, at]

        blocks(lo, count, block, step)

    def residual(self, factor, j, block):
        at, out = pl.ds(j, block), []
        for colour in (0, 1):
            total = self.keep[DIAGONAL + colour, at] * self.value[colour, at] - self.gathered(colour, j, block)
            out.append((self.keep[SOURCE + colour, at] - total) * (1.0 / factor))
        return out

    def rows(self, red, black):
        return self.choose(self.odd, black, red), self.choose(self.odd, red, black)

    def clear_red(self, pairs):
        for j in pairs:
            self.value[0, j] = jnp.zeros((self.depth, 128), F32)

    def clear(self, pairs):
        for j in pairs:
            self.value[:, j] = jnp.zeros((2, self.depth, 128), F32)


def finest_rims(right_ref, labels_ref, before_ref, after_ref, s_ref, d_ref, low_ref, high_ref, source, density):
    for ref, near in ((source, 8), (density, 7)):
        ref[0:near] = jnp.zeros((near, 8, 128), F32)
        ref[64 - near : 64] = jnp.zeros((near, 8, 128), F32)
    source[8:16] = before_ref[0:8]
    source[48:56] = after_ref[0:8]
    source[16:48] = right_ref[...]
    density[7:16] = before_ref[8:17]
    density[48:57] = after_ref[8:17]
    density[16:48] = jnp.where(labels_ref[...] == 1, gas_density, 1.0)
    for start, wide, out in ((0, source, s_ref), (5, density, d_ref)):
        rows = jnp.swapaxes(wide[...], 0, 1)
        out[...] = rows
        low_ref[start : start + 5] = rows[0:5, 8:56]
        high_ref[start : start + 5] = rows[3:8, 8:56]


def finest_window(s_ref, d_ref, before_ref, after_ref, source, density):
    for ref in (source, density):
        for rows in (pl.ds(0, 6), pl.ds(14, 6)):
            ref[rows] = jnp.zeros((6, 64, 128), F32)
    source[1:6, 8:56] = before_ref[0:5]
    source[14:19, 8:56] = after_ref[0:5]
    density[1:6, 8:56] = before_ref[5:10]
    density[14:19, 8:56] = after_ref[5:10]
    source[6:14] = s_ref[...]
    density[6:14] = d_ref[...]


def finest_down(s_ref, d_ref, before_ref, after_ref, chunk_ref, low_ref, high_ref, below_ref,
                source, density, keep, value, plane):
    finest_window(s_ref, d_ref, before_ref, after_ref, source, density)
    level = Level(density, keep, value, 128)
    level.clear((0, 9))
    value[1, 1] = jnp.zeros((64, 128), F32)
    value[1, 8] = jnp.zeros((64, 128), F32)
    level.coefficients(source, 1.0, 1, 8, 2)
    level.first(1, 8, 4)
    level.half(1, 1, 8, 4)
    level.half(0, 2, 6, 3)
    level.half(1, 2, 6, 3)

    def pooling(j):
        red, black = level.residual(1.0, 3 + j, 2)
        plane[pl.ds(j, 2)] = (red + black)[:, 16:48]
        rows = density[pl.ds(6 + 2 * j, 4), 16:48].reshape(2, 2, 32, 128)
        plane[pl.ds(4 + j, 2)] = rows[:, 0] + rows[:, 1]

    blocks(0, 4, 2, pooling)
    pooled = plane[:, pl.ds(0, 16, stride=2)] + plane[:, pl.ds(1, 16, stride=2)]
    out = dot(pooled[:4].reshape(64, 128), halving(0, 0.125)) + dot(pooled[4:].reshape(64, 128), halving(64, 0.125))
    low_ref[...] = value[1, 3:6, 8:56]
    high_ref[...] = value[1, 4:7, 8:56]
    for peer in range(GROUP):
        chunk_ref[peer] = out
    below_ref[...] = value[1, 3:7]


def folded(ref, rows, source, density, start):
    block = ref[rows]
    near, far = block[:, :24], block[:, 24:]
    left = iota(near.shape, 2) < 64
    source[start] = jnp.where(left, near, pltpu.roll(far, 64, 2))
    density[start] = jnp.where(left, pltpu.roll(near, 64, 2), far)


def middle_down(place_ref, window_ref, before_ref, after_ref, chunk_ref, kept_ref, below_ref,
                window, source, density, keep, value, plane, source2, density2, keep2, value2):
    for near, ref in ((0, before_ref), (32, after_ref)):
        window[0:44, near : near + 16] = jnp.zeros((44, 16, 128), F32)
        start = 0
        for rows, planes in FACES:
            low = 16 - planes if near == 0 else 32
            for row in rows:
                window[row + 1, low : low + planes] = ref[start : start + planes]
                start += planes
    window[1:43, 16:32] = window_ref[...]
    for row in (0, 43):
        window[row] = jnp.zeros((48, 128), F32)
    blocks(0, 44, 11, lambda r: folded(window, pl.ds(r, 11), source, density, pl.ds(r, 11)))
    level = Level(density, keep, value, 64, 64)
    level.clear((0, 21))
    for j in (1, 20):
        value[1, j] = jnp.zeros((24, 128), F32)
    level.coefficients(source, 4.0, 1, 20, 5)
    level.first(1, 20, 10)
    level.half(1, 1, 20, 10)
    level.half(0, 2, 18, 9)
    level.half(1, 2, 18, 9)
    kept_ref[...] = window[pl.ds(6 + 4 * place_ref[2], 20)]
    below_ref[...] = value[1, pl.ds(3 + 2 * place_ref[2], 10)]

    def pooling(j):
        red, black = level.residual(4.0, 3 + j, 8)
        plane[pl.ds(j, 8), 0:24] = red + black

    blocks(0, 16, 8, pooling)
    rows = density[4:40].reshape(18, 2, 24, 128)
    plane[16:34, 0:24] = rows[:, 0] + rows[:, 1]
    pooled = plane[:, pl.ds(0, 16, stride=2)] + plane[:, pl.ds(1, 16, stride=2)]
    pooled = dot(pooled.reshape(34 * 16, 128), halving(0, 0.125)).reshape(34, 16, 128)
    lane = iota((34, 16, 128), 2)
    near, far = jnp.where(lane < 32, pooled, 0.0), jnp.where(lane < 32, pltpu.roll(pooled, 96, 2), 0.0)
    for ref, start, parts in ((source2, 2, slice(0, 16)), (density2, 1, slice(16, 34))):
        ref[start : start + parts.stop - parts.start, 0:12] = near[parts, 0:12]
        ref[start : start + parts.stop - parts.start, 12:24] = far[parts, 0:12]
    for row in (0, 19):
        density2[row] = jnp.zeros((24, 128), F32)
    below = Level(density2, keep2, value2, 0)
    below.clear((0, 9))
    for j in (1, 8):
        value2[1, j] = jnp.zeros((24, 128), F32)
    below.coefficients(source2, 16.0, 1, 8, 4)
    below.first(1, 8, 8)
    below.half(1, 1, 8, 8)
    below.half(0, 2, 6, 6)
    below.half(1, 2, 6, 6)
    red, black = below.residual(16.0, 3, 4)
    plane[0:4, 0:24] = red + black
    rows = density2[6:14].reshape(4, 2, 24, 128)
    plane[4:8, 0:24] = rows[:, 0] + rows[:, 1]
    rows = []
    for row in range(4):
        for part in (row, 4 + row):
            rows.append(plane[part, pl.ds(8, 4, stride=2)] + plane[part, pl.ds(9, 4, stride=2)])
    pooled = dot(jnp.concatenate(rows, axis=0), halving(0, 0.125, 32))
    for row in range(4):
        total = pooled[8 * row : 8 * row + 1]
        for i in range(1, 8):
            total = total + pltpu.roll(pooled[8 * row + i : 8 * row + i + 1], 16 * i, 1)
        chunk_ref[0, 40 + row : 41 + row] = total
    black = jnp.zeros((8, 128), F32)
    for j in range(4):
        total = black
        for k, ref in enumerate((source2, density2, source2, density2)):
            total = total + pltpu.roll(ref[6 + 2 * j + k // 2, 8:16], 32 * k, 1)
        chunk_ref[0, 8 * j : 8 * j + 8] = total
    for j in range(4):
        black = black + pltpu.roll(value2[1, 3 + j, 8:16], 32 * j, 1)
    chunk_ref[0, 32:40] = black
    chunk_ref[0, 44:48] = jnp.zeros((4, 128), F32)
    for peer in range(1, chunk_ref.shape[0]):
        chunk_ref[peer] = chunk_ref[0]


def coarsest(place_ref, gathered_ref, source, density, keep, value, wide, besides):
    planes = wide.shape[0] - 8
    groups = gathered_ref.shape[0]
    lane = iota((8, 128), 1)
    for row in (0, 1, planes + 2, planes + 3):
        density[row] = jnp.zeros((8, 128), F32)

    def spread(g):
        tiles = [
            jnp.concatenate([gathered_ref[2 * h + k, 4 * g : 4 * g + 4] for k in range(2)], axis=0)
            for h in range(groups // 2)
        ]
        tiles += [jnp.zeros((8, 128), F32)] * (8 - len(tiles))
        for step in (1, 2, 4):
            upper = (lane // 16) % (2 * step) >= step
            for i in range(8):
                if i % (2 * step) < step:
                    a, b = tiles[i], tiles[i + step]
                    tiles[i] = jnp.where(upper, pltpu.roll(b, 16 * step, 1), a)
                    tiles[i + step] = jnp.where(upper, b, pltpu.roll(a, 128 - 16 * step, 1))
        for z in range(4):
            source[2 + 4 * g + z] = tiles[z]
            density[2 + 4 * g + z] = tiles[4 + z]

    for g in range(planes // 4):
        spread(g)
    level = Level(density, keep, value, 16, 16, ends=True)
    pairs = planes // 2
    value[...] = jnp.zeros(value.shape, F32)
    level.coefficients(source, 64.0, 1, pairs, 4)

    for turns, beside in besides:

        def sweep(i, carry):
            beside(i)
            level.half(0, 1, pairs, pairs)
            level.half(1, 1, pairs, pairs)
            return carry

        lax.fori_loop(0, turns, sweep, 0)
    wide[0:4] = jnp.zeros((4, 8, 128), F32)
    wide[planes + 4 : planes + 8] = jnp.zeros((4, 8, 128), F32)
    even, odd = level.rows(value[0, 1 : pairs + 1], value[1, 1 : pairs + 1])
    for j in range(pairs):
        wide[4 + 2 * j] = even[j]
        wide[5 + 2 * j] = odd[j]
    return wide[pl.ds(4 * place_ref[0], 12)]


def solve(place_ref, gathered_ref, kept_ref, s_ref, d_ref, rim_before_ref, rim_after_ref,
          near_ref, keep1, keep0,
          source3, density3, keep3, value3, wide, source1, density1, value1, source0, density0, value0):
    level1 = Level(density1, keep1, value1, 64, 64)
    finest_window(s_ref, d_ref, rim_before_ref, rim_after_ref, source0, density0)
    level0 = Level(density0, keep0, value0, 128)

    def finest(i):
        rows = pl.ds(5 * i, 5)
        folded(kept_ref, rows, source1, density1, rows)
        level0.coefficients(source0, 1.0, 1 + 2 * i, 2, 2)

    near_ref[...] = coarsest(
        place_ref, gathered_ref, source3, density3, keep3, value3, wide,
        (
            (4, finest),
            (4, lambda i: level1.coefficients(source1, 4.0, 1 + 2 * i, 2, 2)),
            (4, lambda i: None),
        ),
    )


def way_up(devices, place_ref, near_ref, halo_ref, keep1, keep0, below1_ref, below0_ref, before_ref, after_ref,
           pressure_ref, remain_ref,
           source2, density2, keep2, value2, value1, value0, plane):
    at_y, at_group = place_ref[1], place_ref[2]
    level1 = Level(None, keep1, value1, 64, 64)
    level0 = Level(None, keep0, value0, 128)
    lane = iota((24, 128), 1)
    for rows in (slice(0, 2), slice(20, 22)):
        density2[rows] = jnp.zeros((2, 24, 128), F32)
    for i in range(9):
        group, part = (at_group + i) // 4, (at_group + i) % 4
        block = halo_ref[5 * group + part]
        for k in range(2):
            row = 2 + 2 * i + k
            source2[row] = pltpu.roll(block, 64, 1) if k else block
            density2[row] = jnp.where(lane < 32, pltpu.roll(block, 96 - 64 * k, 1), 0.0)
        black = pltpu.roll(halo_ref[5 * group + 4], (128 - 32 * part) % 128, 1)
        value2[1, 1 + i] = jnp.where(lane < 32, black, 0.0)
    level = Level(density2, keep2, value2, 0)
    level.clear((0, 10))
    level.coefficients(source2, 16.0, 1, 9, 3)
    near = near_ref[...]
    row = iota((8, 128), 0)
    picked = []
    for i in range(9):
        y = at_y + i - 4
        inside = (y >= 0) & (y < devices)
        y = jnp.clip(y, 0, devices - 1)
        rows = jnp.sum(jnp.where(row == y % 8, near, 0.0), axis=1)
        rows = pltpu.roll(rows, (128 - 16 * (y // 8)) % 128, 1)
        picked.append(jnp.where(inside & (iota((12, 128), 1) < 16), rows, 0.0))
        picked.append(jnp.zeros((4, 128), F32))
    spread = dot(jnp.concatenate(picked, axis=0), doubling(16)).reshape(9, 16, 128)
    plane[0:9, pl.ds(0, 12, stride=2)] = spread[:, 0:12]
    plane[0:9, pl.ds(1, 12, stride=2)] = spread[:, 0:12]
    value2[1, 1:10] = value2[1, 1:10] + plane[0:9, 0:24]
    level.half(0, 1, 9, 9)
    level.half(1, 2, 7, 7)
    level.half(0, 2, 7, 7)
    level.half(1, 3, 5, 5)
    even, odd = level.rows(value2[0, 3:8], value2[1, 3:8])

    level = level1
    rows = jnp.stack([even, odd], axis=1).reshape(240, 128)
    spread = dot(rows, doubling(32, 0, 64)).reshape(10, 24, 128)
    plane[0:10, pl.ds(0, 24, stride=2)] = spread
    plane[0:10, pl.ds(1, 24, stride=2)] = spread
    left = iota((10, 24, 128), 2) < 64
    value1[1] = below1_ref[...] + jnp.where(left, plane[0:10, 0:24], plane[0:10, 24:48])
    level.clear_red((0, 9))
    level.half(0, 1, 8, 4)
    level.half(1, 1, 8, 4)
    level.half(0, 2, 6, 6)
    level.half(1, 2, 6, 6)
    even, odd = level.rows(value1[0, 2:8], value1[1, 2:8])
    rows = jnp.stack([even, odd], axis=1).reshape(12, 24, 128)[1:11]

    level = level0
    near = dot(rows[:, 8:24].reshape(160, 128), doubling(64)).reshape(10, 16, 128)
    far = dot(rows[:, 0:16].reshape(160, 128), doubling(64, 64)).reshape(10, 16, 128)
    for start, part in ((0, near), (32, far)):
        plane[0:10, pl.ds(start, 16, stride=2)] = part
        plane[0:10, pl.ds(start + 1, 16, stride=2)] = part
    value0[1] = plane[...]
    value0[1, 0:3, 8:56] = value0[1, 0:3, 8:56] + before_ref[...]
    value0[1, 3:7] = value0[1, 3:7] + below0_ref[...]
    value0[1, 7:10, 8:56] = value0[1, 7:10, 8:56] + after_ref[...]
    level.clear_red((0, 9))
    level.half(0, 1, 8, 4)
    level.half(1, 1, 8, 4)
    level.half(0, 2, 6, 3)
    level.half(1, 2, 6, 3)
    even, odd = level.rows(value0[0, 3:7, 16:48], value0[1, 3:7, 16:48])
    pressure_ref[...] = jnp.swapaxes(jnp.stack([even, odd], axis=1).reshape(8, 32, 128), 0, 1)

    def remaining(j):
        red, black = level.residual(1.0, 3 + j, 2)
        even, odd = level.rows(red, black)
        plane[pl.ds(2 * j, 4)] = jnp.stack([even, odd], axis=1).reshape(4, 64, 128)

    blocks(0, 4, 2, remaining)
    remain_ref[...] = jnp.swapaxes(plane[0:8, 16:48], 0, 1)


def pair(array_up, array_down, axis, group=1):
    groups = lax.axis_size(axis) // group
    up = [(i * group + j, (i + 2) * group - 1 - j) for i in range(groups - 1) for j in range(group)]
    down = [(j, i) for i, j in up]
    return lax.ppermute(array_up, axis, up), lax.ppermute(array_down, axis, down)


def shape(*sizes):
    return jax.ShapeDtypeStruct(sizes, F32)


def vmem(*sizes):
    return pltpu.VMEM(sizes, F32)


def params():
    return pltpu.CompilerParams(vmem_limit_bytes=24 * 1024 * 1024)


def body(right_side, labels):
    gz, xy = lax.axis_size("gz"), lax.axis_size("xy")
    density = jnp.where(labels == 1, gas_density, 1.0).astype(F32)
    before, after = pair(
        jnp.concatenate([right_side[-8:], density[-9:]], axis=0),
        jnp.concatenate([right_side[:8], density[:9]], axis=0),
        "gz",
    )
    wide_source, wide_density, low_rim, high_rim = pl.pallas_call(
        finest_rims,
        out_shape=[shape(8, 64, 128)] * 2 + [shape(10, 48, 128)] * 2,
        scratch_shapes=[vmem(64, 8, 128)] * 2,
        compiler_params=params(),
    )(right_side, labels, before, after)
    before, after = pair(high_rim, low_rim, "xy")
    finest = (wide_source, wide_density, before, after)
    at_group = lax.axis_index("xy") % GROUP
    place = jnp.stack([lax.axis_index("gz"), lax.axis_index("xy"), at_group]).astype(jnp.int32)
    smem, block = pl.BlockSpec(memory_space=pltpu.SMEM), pl.BlockSpec(memory_space=pltpu.VMEM)
    chunks, first_rows, last_rows, below0 = pl.pallas_call(
        finest_down,
        out_shape=[shape(GROUP, 64, 128), shape(3, 48, 128), shape(3, 48, 128), shape(4, 64, 128)],
        scratch_shapes=[vmem(20, 64, 128)] * 2 + [vmem(KEPT, 10, 64, 128), vmem(2, 10, 64, 128), vmem(8, 32, 128)],
        compiler_params=params(),
    )(*finest)

    teams = [[GROUP * i + j for j in range(GROUP)] for i in range(xy // GROUP)]
    chunks = lax.all_to_all(chunks, "xy", 0, 0, axis_index_groups=teams, tiled=True)
    window = chunks.reshape(4 * GROUP, 16, 128)
    before, after = pair(window[-13:], window[:13], "xy", GROUP)
    window = jnp.concatenate([before, window, after], axis=0)

    def faces(up):
        parts = []
        for rows, planes in FACES:
            part = window[rows.start : rows.stop, 16 - planes :] if up else window[rows.start : rows.stop, :planes]
            parts.append(part.reshape(-1, 128))
        return jnp.concatenate(parts, axis=0)

    before, after = pair(faces(True), faces(False), "gz")
    rims = pair(last_rows, first_rows, "xy")
    before, after, value_before, value_after = lax.optimization_barrier((before, after, *rims))
    chunks, kept, below1 = pl.pallas_call(
        middle_down,
        out_shape=[shape(gz, 48, 128), shape(20, 48, 128), shape(10, 24, 128)],
        in_specs=[smem] + [block] * 3,
        scratch_shapes=[vmem(44, 48, 128)]
        + [vmem(44, 24, 128)] * 2
        + [vmem(KEPT, 22, 24, 128), vmem(2, 22, 24, 128), vmem(34, 32, 128)]
        + [vmem(20, 24, 128)] * 2
        + [vmem(KEPT, 10, 24, 128), vmem(2, 10, 24, 128)],
        compiler_params=params(),
    )(place, window, before, after)

    column = lax.all_to_all(chunks, "gz", 0, 0, tiled=True)
    peers = [[GROUP * i + j for i in range(xy // GROUP)] for j in range(GROUP)]
    everywhere = lax.all_to_all(
        jnp.broadcast_to(column[:, 40:44].reshape(1, 4 * gz, 128), (xy // GROUP, 4 * gz, 128)),
        "xy", 0, 0, axis_index_groups=peers, tiled=True,
    )
    halo = jnp.pad(column[:, :40], ((1, 1), (0, 0), (0, 0)))
    halo = lax.dynamic_slice(halo, (lax.axis_index("gz"), 0, 0), (3, 40, 128)).reshape(3, 5, 8, 128)
    halo = jnp.swapaxes(halo, 0, 1).reshape(5, 24, 128)
    before, after = pair(halo, halo, "xy", GROUP)
    halo = jnp.concatenate([before, halo, after], axis=0)
    planes = 4 * gz
    near, keep1, keep0 = pl.pallas_call(
        solve,
        out_shape=[shape(12, 8, 128), shape(KEPT, 10, 24, 128), shape(KEPT, 10, 64, 128)],
        in_specs=[smem] + [block] * 6,
        scratch_shapes=[vmem(planes + 4, 8, 128)] * 2
        + [vmem(KEPT, planes // 2 + 2, 8, 128), vmem(2, planes // 2 + 2, 8, 128), vmem(planes + 8, 8, 128)]
        + [vmem(20, 24, 128)] * 2
        + [vmem(2, 10, 24, 128)]
        + [vmem(20, 64, 128)] * 2
        + [vmem(2, 10, 64, 128)],
        compiler_params=params(),
        cost_estimate=pl.CostEstimate(flops=100_000_000, bytes_accessed=16_000_000, transcendentals=0),
    )(place, everywhere, kept, *finest)
    return pl.pallas_call(
        partial(way_up, xy),
        out_shape=[shape(32, 8, 128)] * 2,
        in_specs=[smem] + [block] * 8,
        scratch_shapes=[vmem(22, 24, 128)] * 2
        + [vmem(KEPT, 11, 24, 128), vmem(2, 11, 24, 128)]
        + [vmem(2, 10, 24, 128), vmem(2, 10, 64, 128), vmem(10, 64, 128)],
        compiler_params=params(),
    )(place, near, halo, keep1, keep0, below1, below0, value_before, value_after)


def solution(mesh):
    return jax.shard_map(
        body,
        mesh=mesh,
        in_specs=(P("gz", "xy", None), P("gz", "xy", None)),
        out_specs=(P("gz", "xy", None), P("gz", "xy", None)),
        check_vma=False,
    )
```

```python
from functools import partial

import jax
import jax.numpy as jnp
from jax import lax
from jax.experimental import pallas as pl
from jax.experimental.pallas import tpu as pltpu
from jax.sharding import PartitionSpec as P

gas_density = 0.001
least = 1e-4
F32 = jnp.float32
GROUP = 4
FACES = (
    (range(13, 29), 13),
    (range(9, 13), 12),
    (range(29, 33), 12),
    (range(5, 9), 8),
    (range(33, 37), 8),
    (range(1, 5), 4),
    (range(37, 41), 4),
)


def dot(a, b):
    return lax.dot_general(
        a, b, (((1,), (0,)), ((), ())), precision=lax.Precision.HIGHEST, preferred_element_type=F32
    )


def iota(shape, axis):
    return lax.broadcasted_iota(jnp.int32, shape, axis)


def halving(offset, weight, width=128):
    row, column = iota((128, 128), 0), iota((128, 128), 1)
    return jnp.where((row // 2 + offset == column) & (row < width), weight, 0.0).astype(F32)


def doubling(width, first=0, period=128):
    row, column = iota((128, 128), 0), iota((128, 128), 1)
    hit = ((column % period) // 2 + first == row) & (row < first + width)
    return jnp.where(hit, 1.0, 0.0).astype(F32)


def inverse(a):
    return pl.reciprocal(a, approx=True)


def blocks(lo, count, block, step):
    assert count % block == 0
    if count == block:
        step(lo)
    else:

        def turn(i, _):
            step(lo + i * block)
            return 0

        lax.fori_loop(0, count // block, turn, 0)


LOWER, LEFT, OUT, INNER, INVERSE, DIAGONAL, SOURCE = 0, 2, 4, 6, 7, 9, 11
KEPT = 13


class Level:
    def __init__(self, density, keep, value, width, cross=0, ends=False):
        self.density, self.keep, self.value = density, keep, value
        self.depth, self.width, self.cross, self.ends = value.shape[2], width, cross, ends
        self.row, self.lane = iota((1, 8, 128), 1), iota((1, 8, 128), 2)
        self.odd = (self.row + self.lane) % 2 == 1

    def choose(self, mask, a, b):
        if not isinstance(a, float):
            shape, a = a.shape, a.reshape(-1, 8, 128)
        if not isinstance(b, float):
            shape, b = b.shape, b.reshape(-1, 8, 128)
        return jnp.where(mask, a, b).reshape(shape)

    def low(self, a):
        turned = pltpu.roll(a, 1, 1)
        if self.cross:
            head = turned[:, :8]
            head = jnp.where(self.row == 0, pltpu.roll(head, self.cross, 2), head)
            turned = head if self.depth == 8 else jnp.concatenate([head, turned[:, 8:]], axis=1)
        return turned

    def high(self, a):
        turned = pltpu.roll(a, self.depth - 1, 1)
        if self.cross:
            tail = turned[:, -8:]
            tail = jnp.where(self.row == 7, pltpu.roll(tail, 128 - self.cross, 2), tail)
            turned = tail if self.depth == 8 else jnp.concatenate([turned[:, :-8], tail], axis=1)
        return turned

    def coefficients(self, source, factor, lo, count, block):
        first_x, last_x = self.lane % max(self.width, 1) == 0, self.lane % max(self.width, 1) == self.width - 1
        if self.ends:
            first, last = (self.row == 0) & (self.lane < self.width), (self.row == 7) & (self.lane >= 128 - self.width)

        def coupling(a, b):
            return 2.0 * inverse(jnp.maximum(a + b, least))

        def both(place, at, even, odd):
            self.keep[place, at] = self.choose(self.odd, odd, even)
            self.keep[place + 1, at] = self.choose(self.odd, even, odd)

        def step(j):
            at = pl.ds(j, block)
            shape = (block, 2, self.depth, 128)
            rows = self.density[pl.ds(2 * j, 2 * block)].reshape(shape)
            before = self.density[pl.ds(2 * j - 1, 2 * block)].reshape(shape)[:, 0]
            after = self.density[pl.ds(2 * j + 1, 2 * block)].reshape(shape)[:, 1]
            inner = coupling(rows[:, 0], rows[:, 1])
            out = (coupling(rows[:, 0], before), coupling(rows[:, 1], after))
            parts = []
            for k in range(2):
                d = rows[:, k]
                if self.width or self.ends:
                    edge = 2.0 * inverse(jnp.maximum(d, least))
                lower = coupling(d, self.low(d))
                upper = self.high(lower)
                if self.ends:
                    lower, upper = self.choose(first, edge, lower), self.choose(last, edge, upper)
                left = coupling(d, pltpu.roll(d, 1, 2))
                right = pltpu.roll(left, 127, 2)
                if self.width:
                    left, right = self.choose(first_x, edge, left), self.choose(last_x, edge, right)
                total = lower + upper + (out[0] + inner if k == 0 else inner + out[1]) + left + right
                if self.ends:
                    lower = self.choose(first, 0.0, lower)
                if self.width:
                    left = self.choose(first_x, 0.0, left)
                parts.append((lower, left, jnp.where(d > 0.0, inverse(total), 0.0), total))
            for place, even, odd in zip((LOWER, LEFT, INVERSE, DIAGONAL), *parts):
                both(place, at, even, odd)
            both(OUT, at, out[0], out[1])
            self.keep[INNER, at] = inner
            if source is not None:
                rows = factor * source[pl.ds(2 * j, 2 * block)].reshape(shape)
                both(SOURCE, at, rows[:, 0], rows[:, 1])

        blocks(lo, count, block, step)

    def gathered(self, colour, j, block):
        at, keep = pl.ds(j, block), self.keep
        other = self.value.at[1 - colour]
        w = other[at]
        before, after = other[pl.ds(j - 1, block)], other[pl.ds(j + 1, block)]
        side = self.choose(self.odd, before, after) if colour else self.choose(self.odd, after, before)
        total = keep[INNER, at] * w + keep[OUT + colour, at] * side
        total += keep[LOWER + colour, at] * self.low(w) + self.high(keep[LOWER + 1 - colour, at] * w)
        total += keep[LEFT + colour, at] * pltpu.roll(w, 1, 2) + pltpu.roll(keep[LEFT + 1 - colour, at] * w, 127, 2)
        return total

    def first(self, lo, count, block):
        def step(j):
            at = pl.ds(j, block)
            self.value[0, at] = self.keep[SOURCE, at] * self.keep[INVERSE, at]

        blocks(lo, count, block, step)

    def half(self, colour, lo, count, block):
        def step(j):
            at = pl.ds(j, block)
            total = self.keep[SOURCE + colour, at] + self.gathered(colour, j, block)
            self.value[colour, at] = total * self.keep[INVERSE + colour, at]

        blocks(lo, count, block, step)

    def residual(self, factor, j, block):
        at, out = pl.ds(j, block), []
        for colour in (0, 1):
            total = self.keep[DIAGONAL + colour, at] * self.value[colour, at] - self.gathered(colour, j, block)
            out.append((self.keep[SOURCE + colour, at] - total) * (1.0 / factor))
        return out

    def rows(self, red, black):
        return self.choose(self.odd, black, red), self.choose(self.odd, red, black)

    def clear_red(self, pairs):
        for j in pairs:
            self.value[0, j] = jnp.zeros((self.depth, 128), F32)

    def clear(self, pairs):
        for j in pairs:
            self.value[:, j] = jnp.zeros((2, self.depth, 128), F32)


def finest_rims(right_ref, labels_ref, before_ref, after_ref, s_ref, d_ref, low_ref, high_ref, source, density):
    for ref, near in ((source, 8), (density, 7)):
        ref[0:near] = jnp.zeros((near, 8, 128), F32)
        ref[64 - near : 64] = jnp.zeros((near, 8, 128), F32)
    source[8:16] = before_ref[0:8]
    source[48:56] = after_ref[0:8]
    source[16:48] = right_ref[...]
    density[7:16] = before_ref[8:17]
    density[48:57] = after_ref[8:17]
    density[16:48] = jnp.where(labels_ref[...] == 1, gas_density, 1.0)
    for start, wide, out in ((0, source, s_ref), (5, density, d_ref)):
        rows = jnp.swapaxes(wide[...], 0, 1)
        out[...] = rows
        low_ref[start : start + 5] = rows[0:5, 8:56]
        high_ref[start : start + 5] = rows[3:8, 8:56]


def finest_window(s_ref, d_ref, before_ref, after_ref, source, density):
    for ref in (source, density):
        for rows in (pl.ds(0, 6), pl.ds(14, 6)):
            ref[rows] = jnp.zeros((6, 64, 128), F32)
    source[1:6, 8:56] = before_ref[0:5]
    source[14:19, 8:56] = after_ref[0:5]
    density[1:6, 8:56] = before_ref[5:10]
    density[14:19, 8:56] = after_ref[5:10]
    source[6:14] = s_ref[...]
    density[6:14] = d_ref[...]


def finest_down(s_ref, d_ref, before_ref, after_ref, chunk_ref, low_ref, high_ref, below_ref,
                source, density, keep, value, plane):
    finest_window(s_ref, d_ref, before_ref, after_ref, source, density)
    level = Level(density, keep, value, 128)
    level.clear((0, 9))
    value[1, 1] = jnp.zeros((64, 128), F32)
    value[1, 8] = jnp.zeros((64, 128), F32)
    level.coefficients(source, 1.0, 1, 8, 2)
    level.first(1, 8, 4)
    level.half(1, 1, 8, 4)
    level.half(0, 2, 6, 3)
    level.half(1, 2, 6, 3)

    def pooling(j):
        red, black = level.residual(1.0, 3 + j, 2)
        plane[pl.ds(j, 2)] = (red + black)[:, 16:48]
        rows = density[pl.ds(6 + 2 * j, 4), 16:48].reshape(2, 2, 32, 128)
        plane[pl.ds(4 + j, 2)] = rows[:, 0] + rows[:, 1]

    blocks(0, 4, 2, pooling)
    pooled = plane[:, pl.ds(0, 16, stride=2)] + plane[:, pl.ds(1, 16, stride=2)]
    out = dot(pooled[:4].reshape(64, 128), halving(0, 0.125)) + dot(pooled[4:].reshape(64, 128), halving(64, 0.125))
    low_ref[...] = value[1, 3:6, 8:56]
    high_ref[...] = value[1, 4:7, 8:56]
    for peer in range(GROUP):
        chunk_ref[peer] = out
    below_ref[...] = value[1, 3:7]


def folded(ref, rows, source, density, start):
    block = ref[rows]
    near, far = block[:, :24], block[:, 24:]
    left = iota(near.shape, 2) < 64
    source[start] = jnp.where(left, near, pltpu.roll(far, 64, 2))
    density[start] = jnp.where(left, pltpu.roll(near, 64, 2), far)


def middle_down(place_ref, window_ref, before_ref, after_ref, chunk_ref, halo_ref, kept_ref, below_ref,
                window, source, density, keep, value, plane, source2, density2, keep2, value2):
    for near, ref in ((0, before_ref), (32, after_ref)):
        window[0:44, near : near + 16] = jnp.zeros((44, 16, 128), F32)
        start = 0
        for rows, planes in FACES:
            low = 16 - planes if near == 0 else 32
            for row in rows:
                window[row + 1, low : low + planes] = ref[start : start + planes]
                start += planes
    window[1:43, 16:32] = window_ref[...]
    for row in (0, 43):
        window[row] = jnp.zeros((48, 128), F32)
    blocks(0, 44, 11, lambda r: folded(window, pl.ds(r, 11), source, density, pl.ds(r, 11)))
    level = Level(density, keep, value, 64, 64)
    level.clear((0, 21))
    for j in (1, 20):
        value[1, j] = jnp.zeros((24, 128), F32)
    level.coefficients(source, 4.0, 1, 20, 5)
    level.first(1, 20, 10)
    level.half(1, 1, 20, 10)
    level.half(0, 2, 18, 9)
    level.half(1, 2, 18, 9)
    kept_ref[...] = window[pl.ds(6 + 4 * place_ref[2], 20)]
    below_ref[...] = value[1, pl.ds(3 + 2 * place_ref[2], 10)]

    def pooling(j):
        red, black = level.residual(4.0, 3 + j, 8)
        plane[pl.ds(j, 8), 0:24] = red + black

    blocks(0, 16, 8, pooling)
    rows = density[4:40].reshape(18, 2, 24, 128)
    plane[16:34, 0:24] = rows[:, 0] + rows[:, 1]
    pooled = plane[:, pl.ds(0, 16, stride=2)] + plane[:, pl.ds(1, 16, stride=2)]
    pooled = dot(pooled.reshape(34 * 16, 128), halving(0, 0.125)).reshape(34, 16, 128)
    lane = iota((34, 16, 128), 2)
    near, far = jnp.where(lane < 32, pooled, 0.0), jnp.where(lane < 32, pltpu.roll(pooled, 96, 2), 0.0)
    for ref, start, parts in ((source2, 2, slice(0, 16)), (density2, 1, slice(16, 34))):
        ref[start : start + parts.stop - parts.start, 0:12] = near[parts, 0:12]
        ref[start : start + parts.stop - parts.start, 12:24] = far[parts, 0:12]
    for row in (0, 19):
        density2[row] = jnp.zeros((24, 128), F32)
    below = Level(density2, keep2, value2, 0)
    below.clear((0, 9))
    for j in (1, 8):
        value2[1, j] = jnp.zeros((24, 128), F32)
    below.coefficients(source2, 16.0, 1, 8, 4)
    below.first(1, 8, 8)
    below.half(1, 1, 8, 8)
    below.half(0, 2, 6, 6)
    below.half(1, 2, 6, 6)
    red, black = below.residual(16.0, 3, 4)
    plane[0:4, 0:24] = red + black
    rows = density2[6:14].reshape(4, 2, 24, 128)
    plane[4:8, 0:24] = rows[:, 0] + rows[:, 1]
    rows = []
    for row in range(4):
        for part in (row, 4 + row):
            rows.append(plane[part, pl.ds(8, 4, stride=2)] + plane[part, pl.ds(9, 4, stride=2)])
    pooled = dot(jnp.concatenate(rows, axis=0), halving(0, 0.125, 32))
    for row in range(4):
        total = pooled[8 * row : 8 * row + 1]
        for i in range(1, 8):
            total = total + pltpu.roll(pooled[8 * row + i : 8 * row + i + 1], 16 * i, 1)
        chunk_ref[0, row : row + 1] = total
    black = jnp.zeros((8, 128), F32)
    for j in range(4):
        total = black
        for k, ref in enumerate((source2, density2, source2, density2)):
            total = total + pltpu.roll(ref[6 + 2 * j + k // 2, 8:16], 32 * k, 1)
        halo_ref[8 * j : 8 * j + 8] = total
    for j in range(4):
        black = black + pltpu.roll(value2[1, 3 + j, 8:16], 32 * j, 1)
    halo_ref[32:40] = black
    chunk_ref[0, 4:8] = jnp.zeros((4, 128), F32)
    for peer in range(1, chunk_ref.shape[0]):
        chunk_ref[peer] = chunk_ref[0]


def coarsest(place_ref, gathered_ref, source, density, keep, value, wide, besides):
    planes = wide.shape[0] - 8
    lane = iota((8, 128), 1)
    for row in (0, 1, planes + 2, planes + 3):
        density[row] = jnp.zeros((8, 128), F32)

    def spread(g):
        tiles = [gathered_ref[g, 8 * h : 8 * h + 8] for h in range(gathered_ref.shape[1] // 8)]
        tiles += [jnp.zeros((8, 128), F32)] * (8 - len(tiles))
        for step in (1, 2, 4):
            upper = (lane // 16) % (2 * step) >= step
            for i in range(8):
                if i % (2 * step) < step:
                    a, b = tiles[i], tiles[i + step]
                    tiles[i] = jnp.where(upper, pltpu.roll(b, 16 * step, 1), a)
                    tiles[i + step] = jnp.where(upper, b, pltpu.roll(a, 128 - 16 * step, 1))
        for z in range(4):
            source[2 + 4 * g + z] = tiles[z]
            density[2 + 4 * g + z] = tiles[4 + z]

    for g in range(planes // 4):
        spread(g)
    level = Level(density, keep, value, 16, 16, ends=True)
    pairs = planes // 2
    value[...] = jnp.zeros(value.shape, F32)
    level.coefficients(source, 64.0, 1, pairs, 4)

    for turns, beside in besides:

        def sweep(i, carry):
            beside(i)
            level.half(0, 1, pairs, pairs)
            level.half(1, 1, pairs, pairs)
            return carry

        lax.fori_loop(0, turns, sweep, 0)
    wide[0:4] = jnp.zeros((4, 8, 128), F32)
    wide[planes + 4 : planes + 8] = jnp.zeros((4, 8, 128), F32)
    even, odd = level.rows(value[0, 1 : pairs + 1], value[1, 1 : pairs + 1])
    for j in range(pairs):
        wide[4 + 2 * j] = even[j]
        wide[5 + 2 * j] = odd[j]
    return wide[pl.ds(4 * place_ref[0], 12)]


def way_up(devices, place_ref, gathered_ref, halo_ref, kept_ref, below1_ref,
           s_ref, d_ref, rim_before_ref, rim_after_ref, below0_ref, before_ref, after_ref,
           pressure_ref, remain_ref,
           source3, density3, keep3, value3, wide,
           source2, density2, keep2, value2, source1, density1, keep1, value1,
           source0, density0, keep0, value0, plane):
    at_y, at_group = place_ref[1], place_ref[2]
    level1 = Level(density1, keep1, value1, 64, 64)
    finest_window(s_ref, d_ref, rim_before_ref, rim_after_ref, source0, density0)
    level0 = Level(density0, keep0, value0, 128)
    lane = iota((24, 128), 1)
    for rows in (slice(0, 2), slice(20, 22)):
        density2[rows] = jnp.zeros((2, 24, 128), F32)
    for i in range(9):
        group, part = (at_group + i) // 4, (at_group + i) % 4
        block = halo_ref[5 * group + part]
        for k in range(2):
            row = 2 + 2 * i + k
            source2[row] = pltpu.roll(block, 64, 1) if k else block
            density2[row] = jnp.where(lane < 32, pltpu.roll(block, 96 - 64 * k, 1), 0.0)
        black = pltpu.roll(halo_ref[5 * group + 4], (128 - 32 * part) % 128, 1)
        value2[1, 1 + i] = jnp.where(lane < 32, black, 0.0)
    level = Level(density2, keep2, value2, 0)
    level.clear((0, 10))

    def finest(i):
        level0.coefficients(source0, 1.0, 1 + 2 * i, 2, 2)

    def folding(i):
        rows = pl.ds(5 * i, 5)
        folded(kept_ref, rows, source1, density1, rows)
        finest(i)

    near = coarsest(
        place_ref, gathered_ref, source3, density3, keep3, value3, wide,
        (
            (4, folding),
            (3, lambda i: level.coefficients(source2, 16.0, 1 + 3 * i, 3, 3)),
            (4, lambda i: level1.coefficients(source1, 4.0, 1 + 2 * i, 2, 2)),
            (1, lambda i: None),
        ),
    )
    row = iota((8, 128), 0)
    picked = []
    for i in range(9):
        y = at_y + i - 4
        inside = (y >= 0) & (y < devices)
        y = jnp.clip(y, 0, devices - 1)
        rows = jnp.sum(jnp.where(row == y % 8, near, 0.0), axis=1)
        rows = pltpu.roll(rows, (128 - 16 * (y // 8)) % 128, 1)
        picked.append(jnp.where(inside & (iota((12, 128), 1) < 16), rows, 0.0))
        picked.append(jnp.zeros((4, 128), F32))
    spread = dot(jnp.concatenate(picked, axis=0), doubling(16)).reshape(9, 16, 128)
    plane[0:9, pl.ds(0, 12, stride=2)] = spread[:, 0:12]
    plane[0:9, pl.ds(1, 12, stride=2)] = spread[:, 0:12]
    value2[1, 1:10] = value2[1, 1:10] + plane[0:9, 0:24]
    level.half(0, 1, 9, 9)
    level.half(1, 2, 7, 7)
    level.half(0, 2, 7, 7)
    level.half(1, 3, 5, 5)
    even, odd = level.rows(value2[0, 3:8], value2[1, 3:8])

    level = level1
    rows = jnp.stack([even, odd], axis=1).reshape(240, 128)
    spread = dot(rows, doubling(32, 0, 64)).reshape(10, 24, 128)
    plane[0:10, pl.ds(0, 24, stride=2)] = spread
    plane[0:10, pl.ds(1, 24, stride=2)] = spread
    left = iota((10, 24, 128), 2) < 64
    value1[1] = below1_ref[...] + jnp.where(left, plane[0:10, 0:24], plane[0:10, 24:48])
    level.clear_red((0, 9))
    level.half(0, 1, 8, 4)
    level.half(1, 1, 8, 4)
    level.half(0, 2, 6, 6)
    level.half(1, 2, 6, 6)
    even, odd = level.rows(value1[0, 2:8], value1[1, 2:8])
    rows = jnp.stack([even, odd], axis=1).reshape(12, 24, 128)[1:11]

    level = level0
    near = dot(rows[:, 8:24].reshape(160, 128), doubling(64)).reshape(10, 16, 128)
    far = dot(rows[:, 0:16].reshape(160, 128), doubling(64, 64)).reshape(10, 16, 128)
    for start, part in ((0, near), (32, far)):
        plane[0:10, pl.ds(start, 16, stride=2)] = part
        plane[0:10, pl.ds(start + 1, 16, stride=2)] = part
    value0[1] = plane[...]
    value0[1, 0:3, 8:56] = value0[1, 0:3, 8:56] + before_ref[...]
    value0[1, 3:7] = value0[1, 3:7] + below0_ref[...]
    value0[1, 7:10, 8:56] = value0[1, 7:10, 8:56] + after_ref[...]
    level.clear_red((0, 9))
    level.half(0, 1, 8, 4)
    level.half(1, 1, 8, 4)
    level.half(0, 2, 6, 3)
    level.half(1, 2, 6, 3)
    even, odd = level.rows(value0[0, 3:7, 16:48], value0[1, 3:7, 16:48])
    pressure_ref[...] = jnp.swapaxes(jnp.stack([even, odd], axis=1).reshape(8, 32, 128), 0, 1)

    def remaining(j):
        red, black = level.residual(1.0, 3 + j, 2)
        even, odd = level.rows(red, black)
        plane[pl.ds(2 * j, 4)] = jnp.stack([even, odd], axis=1).reshape(4, 64, 128)

    blocks(0, 4, 2, remaining)
    remain_ref[...] = jnp.swapaxes(plane[0:8, 16:48], 0, 1)


def pair(array_up, array_down, axis, group=1):
    groups = lax.axis_size(axis) // group
    up = [(i * group + j, (i + 2) * group - 1 - j) for i in range(groups - 1) for j in range(group)]
    down = [(j, i) for i, j in up]
    return lax.ppermute(array_up, axis, up), lax.ppermute(array_down, axis, down)


def shape(*sizes):
    return jax.ShapeDtypeStruct(sizes, F32)


def vmem(*sizes):
    return pltpu.VMEM(sizes, F32)


def params():
    return pltpu.CompilerParams(vmem_limit_bytes=24 * 1024 * 1024)


def body(right_side, labels):
    gz, xy = lax.axis_size("gz"), lax.axis_size("xy")
    density = jnp.where(labels == 1, gas_density, 1.0).astype(F32)
    before, after = pair(
        jnp.concatenate([right_side[-8:], density[-9:]], axis=0),
        jnp.concatenate([right_side[:8], density[:9]], axis=0),
        "gz",
    )
    wide_source, wide_density, low_rim, high_rim = pl.pallas_call(
        finest_rims,
        out_shape=[shape(8, 64, 128)] * 2 + [shape(10, 48, 128)] * 2,
        scratch_shapes=[vmem(64, 8, 128)] * 2,
        compiler_params=params(),
    )(right_side, labels, before, after)
    before, after = pair(high_rim, low_rim, "xy")
    finest = (wide_source, wide_density, before, after)
    at_group = lax.axis_index("xy") % GROUP
    place = jnp.stack([lax.axis_index("gz"), lax.axis_index("xy"), at_group]).astype(jnp.int32)
    smem, block = pl.BlockSpec(memory_space=pltpu.SMEM), pl.BlockSpec(memory_space=pltpu.VMEM)
    chunks, first_rows, last_rows, below0 = pl.pallas_call(
        finest_down,
        out_shape=[shape(GROUP, 64, 128), shape(3, 48, 128), shape(3, 48, 128), shape(4, 64, 128)],
        scratch_shapes=[vmem(20, 64, 128)] * 2 + [vmem(KEPT, 10, 64, 128), vmem(2, 10, 64, 128), vmem(8, 32, 128)],
        compiler_params=params(),
    )(*finest)

    teams = [[GROUP * i + j for j in range(GROUP)] for i in range(xy // GROUP)]
    chunks = lax.all_to_all(chunks, "xy", 0, 0, axis_index_groups=teams, tiled=True)
    window = chunks.reshape(4 * GROUP, 16, 128)
    before, after = pair(window[-13:], window[:13], "xy", GROUP)
    window = jnp.concatenate([before, window, after], axis=0)

    def faces(up):
        parts = []
        for rows, planes in FACES:
            part = window[rows.start : rows.stop, 16 - planes :] if up else window[rows.start : rows.stop, :planes]
            parts.append(part.reshape(-1, 128))
        return jnp.concatenate(parts, axis=0)

    before, after = pair(faces(True), faces(False), "gz")
    rims = pair(last_rows, first_rows, "xy")
    before, after, value_before, value_after = lax.optimization_barrier((before, after, *rims))
    chunks, halo, kept, below1 = pl.pallas_call(
        middle_down,
        out_shape=[shape(xy // GROUP, 8, 128), shape(40, 128), shape(20, 48, 128), shape(10, 24, 128)],
        in_specs=[smem] + [block] * 3,
        scratch_shapes=[vmem(44, 48, 128)]
        + [vmem(44, 24, 128)] * 2
        + [vmem(KEPT, 22, 24, 128), vmem(2, 22, 24, 128), vmem(34, 32, 128)]
        + [vmem(20, 24, 128)] * 2
        + [vmem(KEPT, 10, 24, 128), vmem(2, 10, 24, 128)],
        compiler_params=params(),
    )(place, window, before, after)

    peers = [[GROUP * i + j for i in range(xy // GROUP)] for j in range(GROUP)]
    chunks = lax.all_to_all(chunks, "xy", 0, 0, axis_index_groups=peers, tiled=True)
    before, after = pair(halo, halo, "xy", GROUP)
    halo = jnp.concatenate([before, halo, after], axis=0)
    layer = chunks[:, :4].reshape(1, xy, 128)
    everywhere = lax.all_to_all(jnp.broadcast_to(layer, (gz, xy, 128)), "gz", 0, 0, tiled=True)
    before, after = pair(halo, halo, "gz")
    halo = jnp.concatenate([part.reshape(15, 8, 128) for part in (before, halo, after)], axis=1)
    planes = 4 * gz
    return pl.pallas_call(
        partial(way_up, xy),
        out_shape=[shape(32, 8, 128)] * 2,
        in_specs=[smem] + [block] * 11,
        scratch_shapes=[vmem(planes + 4, 8, 128)] * 2
        + [vmem(KEPT, planes // 2 + 2, 8, 128), vmem(2, planes // 2 + 2, 8, 128), vmem(planes + 8, 8, 128)]
        + [vmem(22, 24, 128)] * 2
        + [vmem(KEPT, 11, 24, 128), vmem(2, 11, 24, 128)]
        + [vmem(20, 24, 128)] * 2
        + [vmem(KEPT, 10, 24, 128), vmem(2, 10, 24, 128)]
        + [vmem(20, 64, 128)] * 2
        + [vmem(KEPT, 10, 64, 128), vmem(2, 10, 64, 128), vmem(10, 64, 128)],
        compiler_params=params(),
    )(place, everywhere, halo, kept, below1, *finest, below0, value_before, value_after)


def solution(mesh):
    return jax.shard_map(
        body,
        mesh=mesh,
        in_specs=(P("gz", "xy", None), P("gz", "xy", None)),
        out_specs=(P("gz", "xy", None), P("gz", "xy", None)),
        check_vma=False,
    )
```

```python
from functools import partial

import jax
import jax.numpy as jnp
from jax import lax
from jax.experimental import pallas as pl
from jax.experimental.pallas import tpu as pltpu
from jax.sharding import PartitionSpec as P

gas_density = 0.001
least = 1e-4
F32 = jnp.float32
GROUP = 4
FACES = (
    (range(13, 29), 13),
    (range(9, 13), 12),
    (range(29, 33), 12),
    (range(5, 9), 8),
    (range(33, 37), 8),
    (range(1, 5), 4),
    (range(37, 41), 4),
)


def dot(a, b):
    return lax.dot_general(
        a, b, (((1,), (0,)), ((), ())), precision=lax.Precision.HIGHEST, preferred_element_type=F32
    )


def iota(shape, axis):
    return lax.broadcasted_iota(jnp.int32, shape, axis)


def halving(offset, weight, width=128):
    row, column = iota((128, 128), 0), iota((128, 128), 1)
    return jnp.where((row // 2 + offset == column) & (row < width), weight, 0.0).astype(F32)


def doubling(width, first=0, period=128):
    row, column = iota((128, 128), 0), iota((128, 128), 1)
    hit = ((column % period) // 2 + first == row) & (row < first + width)
    return jnp.where(hit, 1.0, 0.0).astype(F32)


def inverse(a):
    return pl.reciprocal(a, approx=True)


def blocks(lo, count, block, step):
    assert count % block == 0
    if count == block:
        step(lo)
    else:

        def turn(i, _):
            step(lo + i * block)
            return 0

        lax.fori_loop(0, count // block, turn, 0)


LOWER, LEFT, OUT, INNER, INVERSE, DIAGONAL, SOURCE = 0, 2, 4, 6, 7, 9, 11
KEPT = 13


class Level:
    def __init__(self, density, keep, value, width, cross=0, ends=False):
        self.density, self.keep, self.value = density, keep, value
        self.depth, self.width, self.cross, self.ends = value.shape[2], width, cross, ends
        self.row, self.lane = iota((1, 8, 128), 1), iota((1, 8, 128), 2)
        self.odd = (self.row + self.lane) % 2 == 1

    def choose(self, mask, a, b):
        if not isinstance(a, float):
            shape, a = a.shape, a.reshape(-1, 8, 128)
        if not isinstance(b, float):
            shape, b = b.shape, b.reshape(-1, 8, 128)
        return jnp.where(mask, a, b).reshape(shape)

    def low(self, a):
        turned = pltpu.roll(a, 1, 1)
        if self.cross:
            head = turned[:, :8]
            head = jnp.where(self.row == 0, pltpu.roll(head, self.cross, 2), head)
            turned = head if self.depth == 8 else jnp.concatenate([head, turned[:, 8:]], axis=1)
        return turned

    def high(self, a):
        turned = pltpu.roll(a, self.depth - 1, 1)
        if self.cross:
            tail = turned[:, -8:]
            tail = jnp.where(self.row == 7, pltpu.roll(tail, 128 - self.cross, 2), tail)
            turned = tail if self.depth == 8 else jnp.concatenate([turned[:, :-8], tail], axis=1)
        return turned

    def coefficients(self, source, factor, lo, count, block):
        first_x, last_x = self.lane % max(self.width, 1) == 0, self.lane % max(self.width, 1) == self.width - 1
        if self.ends:
            first, last = (self.row == 0) & (self.lane < self.width), (self.row == 7) & (self.lane >= 128 - self.width)

        def coupling(a, b):
            return 2.0 * inverse(jnp.maximum(a + b, least))

        def both(place, at, even, odd):
            self.keep[place, at] = self.choose(self.odd, odd, even)
            self.keep[place + 1, at] = self.choose(self.odd, even, odd)

        def step(j):
            at = pl.ds(j, block)
            shape = (block, 2, self.depth, 128)
            rows = self.density[pl.ds(2 * j, 2 * block)].reshape(shape)
            before = self.density[pl.ds(2 * j - 1, 2 * block)].reshape(shape)[:, 0]
            after = self.density[pl.ds(2 * j + 1, 2 * block)].reshape(shape)[:, 1]
            inner = coupling(rows[:, 0], rows[:, 1])
            out = (coupling(rows[:, 0], before), coupling(rows[:, 1], after))
            parts = []
            for k in range(2):
                d = rows[:, k]
                if self.width or self.ends:
                    edge = 2.0 * inverse(jnp.maximum(d, least))
                lower = coupling(d, self.low(d))
                upper = self.high(lower)
                if self.ends:
                    lower, upper = self.choose(first, edge, lower), self.choose(last, edge, upper)
                left = coupling(d, pltpu.roll(d, 1, 2))
                right = pltpu.roll(left, 127, 2)
                if self.width:
                    left, right = self.choose(first_x, edge, left), self.choose(last_x, edge, right)
                total = lower + upper + (out[0] + inner if k == 0 else inner + out[1]) + left + right
                if self.ends:
                    lower = self.choose(first, 0.0, lower)
                if self.width:
                    left = self.choose(first_x, 0.0, left)
                parts.append((lower, left, jnp.where(d > 0.0, inverse(total), 0.0), total))
            for place, even, odd in zip((LOWER, LEFT, INVERSE, DIAGONAL), *parts):
                both(place, at, even, odd)
            both(OUT, at, out[0], out[1])
            self.keep[INNER, at] = inner
            if source is not None:
                rows = factor * source[pl.ds(2 * j, 2 * block)].reshape(shape)
                both(SOURCE, at, rows[:, 0], rows[:, 1])

        blocks(lo, count, block, step)

    def gathered(self, colour, j, block):
        at, keep = pl.ds(j, block), self.keep
        other = self.value.at[1 - colour]
        w = other[at]
        before, after = other[pl.ds(j - 1, block)], other[pl.ds(j + 1, block)]
        side = self.choose(self.odd, before, after) if colour else self.choose(self.odd, after, before)
        total = keep[INNER, at] * w + keep[OUT + colour, at] * side
        total += keep[LOWER + colour, at] * self.low(w) + self.high(keep[LOWER + 1 - colour, at] * w)
        total += keep[LEFT + colour, at] * pltpu.roll(w, 1, 2) + pltpu.roll(keep[LEFT + 1 - colour, at] * w, 127, 2)
        return total

    def first(self, lo, count, block):
        def step(j):
            at = pl.ds(j, block)
            self.value[0, at] = self.keep[SOURCE, at] * self.keep[INVERSE, at]

        blocks(lo, count, block, step)

    def half(self, colour, lo, count, block):
        def step(j):
            at = pl.ds(j, block)
            total = self.keep[SOURCE + colour, at] + self.gathered(colour, j, block)
            self.value[colour, at] = total * self.keep[INVERSE + colour, at]

        blocks(lo, count, block, step)

    def residual(self, factor, j, block):
        at, out = pl.ds(j, block), []
        for colour in (0, 1):
            total = self.keep[DIAGONAL + colour, at] * self.value[colour, at] - self.gathered(colour, j, block)
            out.append((self.keep[SOURCE + colour, at] - total) * (1.0 / factor))
        return out

    def rows(self, red, black):
        return self.choose(self.odd, black, red), self.choose(self.odd, red, black)

    def clear_red(self, pairs):
        for j in pairs:
            self.value[0, j] = jnp.zeros((self.depth, 128), F32)

    def clear(self, pairs):
        for j in pairs:
            self.value[:, j] = jnp.zeros((2, self.depth, 128), F32)


def finest_rims(right_ref, labels_ref, before_ref, after_ref, s_ref, d_ref, low_ref, high_ref, source, density):
    for ref, near in ((source, 8), (density, 7)):
        ref[0:near] = jnp.zeros((near, 8, 128), F32)
        ref[64 - near : 64] = jnp.zeros((near, 8, 128), F32)
    source[8:16] = before_ref[0:8]
    source[48:56] = after_ref[0:8]
    source[16:48] = right_ref[...]
    density[7:16] = before_ref[8:17]
    density[48:57] = after_ref[8:17]
    density[16:48] = jnp.where(labels_ref[...] == 1, gas_density, 1.0)
    for start, wide, out in ((0, source, s_ref), (5, density, d_ref)):
        rows = jnp.swapaxes(wide[...], 0, 1)
        out[...] = rows
        low_ref[start : start + 5] = rows[0:5, 8:56]
        high_ref[start : start + 5] = rows[3:8, 8:56]


def finest_window(s_ref, d_ref, before_ref, after_ref, source, density):
    for ref in (source, density):
        for rows in (pl.ds(0, 6), pl.ds(14, 6)):
            ref[rows] = jnp.zeros((6, 64, 128), F32)
    source[1:6, 8:56] = before_ref[0:5]
    source[14:19, 8:56] = after_ref[0:5]
    density[1:6, 8:56] = before_ref[5:10]
    density[14:19, 8:56] = after_ref[5:10]
    source[6:14] = s_ref[...]
    density[6:14] = d_ref[...]


def finest_down(s_ref, d_ref, before_ref, after_ref, chunk_ref, low_ref, high_ref, below_ref,
                source, density, keep, value, plane):
    finest_window(s_ref, d_ref, before_ref, after_ref, source, density)
    level = Level(density, keep, value, 128)
    level.clear((0, 9))
    value[1, 1] = jnp.zeros((64, 128), F32)
    value[1, 8] = jnp.zeros((64, 128), F32)
    level.coefficients(source, 1.0, 1, 8, 2)
    level.first(1, 8, 4)
    level.half(1, 1, 8, 4)
    level.half(0, 2, 6, 3)
    level.half(1, 2, 6, 3)

    def pooling(j):
        red, black = level.residual(1.0, 3 + j, 2)
        plane[pl.ds(j, 2)] = (red + black)[:, 16:48]
        rows = density[pl.ds(6 + 2 * j, 4), 16:48].reshape(2, 2, 32, 128)
        plane[pl.ds(4 + j, 2)] = rows[:, 0] + rows[:, 1]

    blocks(0, 4, 2, pooling)
    pooled = plane[:, pl.ds(0, 16, stride=2)] + plane[:, pl.ds(1, 16, stride=2)]
    out = dot(pooled[:4].reshape(64, 128), halving(0, 0.125)) + dot(pooled[4:].reshape(64, 128), halving(64, 0.125))
    low_ref[...] = value[1, 3:6, 8:56]
    high_ref[...] = value[1, 4:7, 8:56]
    for peer in range(GROUP):
        chunk_ref[peer] = out
    below_ref[...] = value[1, 3:7]


def folded(ref, rows, source, density, start):
    block = ref[rows]
    near, far = block[:, :24], block[:, 24:]
    left = iota(near.shape, 2) < 64
    source[start] = jnp.where(left, near, pltpu.roll(far, 64, 2))
    density[start] = jnp.where(left, pltpu.roll(near, 64, 2), far)


def middle_down(place_ref, window_ref, before_ref, after_ref, chunk_ref, halo_ref, kept_ref, below_ref,
                window, source, density, keep, value, plane, source2, density2, keep2, value2):
    for near, ref in ((0, before_ref), (32, after_ref)):
        window[0:44, near : near + 16] = jnp.zeros((44, 16, 128), F32)
        start = 0
        for rows, planes in FACES:
            low = 16 - planes if near == 0 else 32
            for row in rows:
                window[row + 1, low : low + planes] = ref[start : start + planes]
                start += planes
    window[1:43, 16:32] = window_ref[...]
    for row in (0, 43):
        window[row] = jnp.zeros((48, 128), F32)
    blocks(0, 44, 11, lambda r: folded(window, pl.ds(r, 11), source, density, pl.ds(r, 11)))
    level = Level(density, keep, value, 64, 64)
    level.clear((0, 21))
    for j in (1, 20):
        value[1, j] = jnp.zeros((24, 128), F32)
    level.coefficients(source, 4.0, 1, 20, 5)
    level.first(1, 20, 10)
    level.half(1, 1, 20, 10)
    level.half(0, 2, 18, 9)
    level.half(1, 2, 18, 9)
    kept_ref[...] = window[pl.ds(6 + 4 * place_ref[2], 20)]
    below_ref[...] = value[1, pl.ds(3 + 2 * place_ref[2], 10)]

    def pooling(j):
        red, black = level.residual(4.0, 3 + j, 8)
        plane[pl.ds(j, 8), 0:24] = red + black

    blocks(0, 16, 8, pooling)
    rows = density[4:40].reshape(18, 2, 24, 128)
    plane[16:34, 0:24] = rows[:, 0] + rows[:, 1]
    pooled = plane[:, pl.ds(0, 16, stride=2)] + plane[:, pl.ds(1, 16, stride=2)]
    pooled = dot(pooled.reshape(34 * 16, 128), halving(0, 0.125)).reshape(34, 16, 128)
    lane = iota((34, 16, 128), 2)
    near, far = jnp.where(lane < 32, pooled, 0.0), jnp.where(lane < 32, pltpu.roll(pooled, 96, 2), 0.0)
    for ref, start, parts in ((source2, 2, slice(0, 16)), (density2, 1, slice(16, 34))):
        ref[start : start + parts.stop - parts.start, 0:12] = near[parts, 0:12]
        ref[start : start + parts.stop - parts.start, 12:24] = far[parts, 0:12]
    for row in (0, 19):
        density2[row] = jnp.zeros((24, 128), F32)
    below = Level(density2, keep2, value2, 0)
    below.clear((0, 9))
    for j in (1, 8):
        value2[1, j] = jnp.zeros((24, 128), F32)
    below.coefficients(source2, 16.0, 1, 8, 4)
    below.first(1, 8, 8)
    below.half(1, 1, 8, 8)
    below.half(0, 2, 6, 6)
    below.half(1, 2, 6, 6)
    red, black = below.residual(16.0, 3, 4)
    plane[0:4, 0:24] = red + black
    rows = density2[6:14].reshape(4, 2, 24, 128)
    plane[4:8, 0:24] = rows[:, 0] + rows[:, 1]
    rows = []
    for row in range(4):
        for part in (row, 4 + row):
            rows.append(plane[part, pl.ds(8, 4, stride=2)] + plane[part, pl.ds(9, 4, stride=2)])
    pooled = dot(jnp.concatenate(rows, axis=0), halving(0, 0.125, 32))
    for row in range(4):
        total = pooled[8 * row : 8 * row + 1]
        for i in range(1, 8):
            total = total + pltpu.roll(pooled[8 * row + i : 8 * row + i + 1], 16 * i, 1)
        chunk_ref[0, row : row + 1] = total
    black = jnp.zeros((8, 128), F32)
    for j in range(4):
        total = black
        for k, ref in enumerate((source2, density2, source2, density2)):
            total = total + pltpu.roll(ref[6 + 2 * j + k // 2, 8:16], 32 * k, 1)
        halo_ref[8 * j : 8 * j + 8] = total
    for j in range(4):
        black = black + pltpu.roll(value2[1, 3 + j, 8:16], 32 * j, 1)
    halo_ref[32:40] = black
    chunk_ref[0, 4:8] = jnp.zeros((4, 128), F32)
    for peer in range(1, chunk_ref.shape[0]):
        chunk_ref[peer] = chunk_ref[0]


def coarsest(place_ref, gathered_ref, source, density, keep, value, wide, besides):
    planes = wide.shape[0] - 8
    lane = iota((8, 128), 1)
    for row in (0, 1, planes + 2, planes + 3):
        density[row] = jnp.zeros((8, 128), F32)

    def spread(g):
        tiles = [gathered_ref[g, 8 * h : 8 * h + 8] for h in range(gathered_ref.shape[1] // 8)]
        tiles += [jnp.zeros((8, 128), F32)] * (8 - len(tiles))
        for step in (1, 2, 4):
            upper = (lane // 16) % (2 * step) >= step
            for i in range(8):
                if i % (2 * step) < step:
                    a, b = tiles[i], tiles[i + step]
                    tiles[i] = jnp.where(upper, pltpu.roll(b, 16 * step, 1), a)
                    tiles[i + step] = jnp.where(upper, b, pltpu.roll(a, 128 - 16 * step, 1))
        for z in range(4):
            source[2 + 4 * g + z] = tiles[z]
            density[2 + 4 * g + z] = tiles[4 + z]

    for g in range(planes // 4):
        spread(g)
    level = Level(density, keep, value, 16, 16, ends=True)
    pairs = planes // 2
    value[...] = jnp.zeros(value.shape, F32)
    level.coefficients(source, 64.0, 1, pairs, 4)

    for turns, beside in besides:

        def sweep(i, carry):
            beside(i)
            level.half(0, 1, pairs, pairs)
            level.half(1, 1, pairs, pairs)
            return carry

        lax.fori_loop(0, turns, sweep, 0)
    wide[0:4] = jnp.zeros((4, 8, 128), F32)
    wide[planes + 4 : planes + 8] = jnp.zeros((4, 8, 128), F32)
    even, odd = level.rows(value[0, 1 : pairs + 1], value[1, 1 : pairs + 1])
    for j in range(pairs):
        wide[4 + 2 * j] = even[j]
        wide[5 + 2 * j] = odd[j]
    return wide[pl.ds(4 * place_ref[0], 12)]


def way_up(devices, place_ref, gathered_ref, halo_ref, kept_ref, below1_ref,
           s_ref, d_ref, rim_before_ref, rim_after_ref, below0_ref, before_ref, after_ref,
           pressure_ref, remain_ref,
           source3, density3, keep3, value3, wide,
           source2, density2, keep2, value2, source1, density1, keep1, value1,
           source0, density0, keep0, value0, plane):
    at_y, at_group = place_ref[1], place_ref[2]
    level1 = Level(density1, keep1, value1, 64, 64)
    finest_window(s_ref, d_ref, rim_before_ref, rim_after_ref, source0, density0)
    level0 = Level(density0, keep0, value0, 128)
    lane = iota((24, 128), 1)
    for rows in (slice(0, 2), slice(20, 22)):
        density2[rows] = jnp.zeros((2, 24, 128), F32)
    for i in range(9):
        group, part = (at_group + i) // 4, (at_group + i) % 4
        block = halo_ref[5 * group + part]
        for k in range(2):
            row = 2 + 2 * i + k
            source2[row] = pltpu.roll(block, 64, 1) if k else block
            density2[row] = jnp.where(lane < 32, pltpu.roll(block, 96 - 64 * k, 1), 0.0)
        black = pltpu.roll(halo_ref[5 * group + 4], (128 - 32 * part) % 128, 1)
        value2[1, 1 + i] = jnp.where(lane < 32, black, 0.0)
    level = Level(density2, keep2, value2, 0)
    level.clear((0, 10))

    def finest(i):
        level0.coefficients(source0, 1.0, 1 + 2 * i, 2, 2)

    def folding(i):
        rows = pl.ds(5 * i, 5)
        folded(kept_ref, rows, source1, density1, rows)
        finest(i)

    near = coarsest(
        place_ref, gathered_ref, source3, density3, keep3, value3, wide,
        (
            (4, folding),
            (3, lambda i: level.coefficients(source2, 16.0, 1 + 3 * i, 3, 3)),
            (4, lambda i: level1.coefficients(source1, 4.0, 1 + 2 * i, 2, 2)),
            (1, lambda i: None),
        ),
    )
    row = iota((8, 128), 0)
    picked = []
    for i in range(9):
        y = at_y + i - 4
        inside = (y >= 0) & (y < devices)
        y = jnp.clip(y, 0, devices - 1)
        rows = jnp.sum(jnp.where(row == y % 8, near, 0.0), axis=1)
        rows = pltpu.roll(rows, (128 - 16 * (y // 8)) % 128, 1)
        picked.append(jnp.where(inside & (iota((12, 128), 1) < 16), rows, 0.0))
        picked.append(jnp.zeros((4, 128), F32))
    spread = dot(jnp.concatenate(picked, axis=0), doubling(16)).reshape(9, 16, 128)
    plane[0:9, pl.ds(0, 12, stride=2)] = spread[:, 0:12]
    plane[0:9, pl.ds(1, 12, stride=2)] = spread[:, 0:12]
    value2[1, 1:10] = value2[1, 1:10] + plane[0:9, 0:24]
    level.half(0, 1, 9, 9)
    level.half(1, 2, 7, 7)
    level.half(0, 2, 7, 7)
    level.half(1, 3, 5, 5)
    even, odd = level.rows(value2[0, 3:8], value2[1, 3:8])

    level = level1
    rows = jnp.stack([even, odd], axis=1).reshape(240, 128)
    spread = dot(rows, doubling(32, 0, 64)).reshape(10, 24, 128)
    plane[0:10, pl.ds(0, 24, stride=2)] = spread
    plane[0:10, pl.ds(1, 24, stride=2)] = spread
    left = iota((10, 24, 128), 2) < 64
    value1[1] = below1_ref[...] + jnp.where(left, plane[0:10, 0:24], plane[0:10, 24:48])
    level.clear_red((0, 9))
    level.half(0, 1, 8, 4)
    level.half(1, 1, 8, 4)
    level.half(0, 2, 6, 6)
    level.half(1, 2, 6, 6)
    even, odd = level.rows(value1[0, 2:8], value1[1, 2:8])
    rows = jnp.stack([even, odd], axis=1).reshape(12, 24, 128)[1:11]

    level = level0
    near = dot(rows[:, 8:24].reshape(160, 128), doubling(64)).reshape(10, 16, 128)
    far = dot(rows[:, 0:16].reshape(160, 128), doubling(64, 64)).reshape(10, 16, 128)
    for start, part in ((0, near), (32, far)):
        plane[0:10, pl.ds(start, 16, stride=2)] = part
        plane[0:10, pl.ds(start + 1, 16, stride=2)] = part
    value0[1] = plane[...]
    value0[1, 0:3, 8:56] = value0[1, 0:3, 8:56] + before_ref[...]
    value0[1, 3:7] = value0[1, 3:7] + below0_ref[...]
    value0[1, 7:10, 8:56] = value0[1, 7:10, 8:56] + after_ref[...]
    level.clear_red((0, 9))
    level.half(0, 1, 8, 4)
    level.half(1, 1, 8, 4)
    level.half(0, 2, 6, 3)
    level.half(1, 2, 6, 3)
    even, odd = level.rows(value0[0, 3:7, 16:48], value0[1, 3:7, 16:48])
    pressure_ref[...] = jnp.swapaxes(jnp.stack([even, odd], axis=1).reshape(8, 32, 128), 0, 1)

    def remaining(j):
        red, black = level.residual(1.0, 3 + j, 2)
        even, odd = level.rows(red, black)
        plane[pl.ds(2 * j, 4)] = jnp.stack([even, odd], axis=1).reshape(4, 64, 128)

    blocks(0, 4, 2, remaining)
    remain_ref[...] = jnp.swapaxes(plane[0:8, 16:48], 0, 1)


def pair(array_up, array_down, axis, group=1):
    groups = lax.axis_size(axis) // group
    up = [(i * group + j, (i + 2) * group - 1 - j) for i in range(groups - 1) for j in range(group)]
    down = [(j, i) for i, j in up]
    return lax.ppermute(array_up, axis, up), lax.ppermute(array_down, axis, down)


def shape(*sizes):
    return jax.ShapeDtypeStruct(sizes, F32)


def vmem(*sizes):
    return pltpu.VMEM(sizes, F32)


def params():
    return pltpu.CompilerParams(vmem_limit_bytes=24 * 1024 * 1024)


def body(right_side, labels):
    gz, xy = lax.axis_size("gz"), lax.axis_size("xy")
    density = jnp.where(labels == 1, gas_density, 1.0).astype(F32)
    before, after = pair(
        jnp.concatenate([right_side[-8:], density[-9:]], axis=0),
        jnp.concatenate([right_side[:8], density[:9]], axis=0),
        "gz",
    )
    wide_source, wide_density, low_rim, high_rim = pl.pallas_call(
        finest_rims,
        out_shape=[shape(8, 64, 128)] * 2 + [shape(10, 48, 128)] * 2,
        scratch_shapes=[vmem(64, 8, 128)] * 2,
        compiler_params=params(),
    )(right_side, labels, before, after)
    before, after = pair(high_rim, low_rim, "xy")
    finest = (wide_source, wide_density, before, after)
    at_group = lax.axis_index("xy") % GROUP
    place = jnp.stack([lax.axis_index("gz"), lax.axis_index("xy"), at_group]).astype(jnp.int32)
    smem, block = pl.BlockSpec(memory_space=pltpu.SMEM), pl.BlockSpec(memory_space=pltpu.VMEM)
    chunks, first_rows, last_rows, below0 = pl.pallas_call(
        finest_down,
        out_shape=[shape(GROUP, 64, 128), shape(3, 48, 128), shape(3, 48, 128), shape(4, 64, 128)],
        scratch_shapes=[vmem(20, 64, 128)] * 2 + [vmem(KEPT, 10, 64, 128), vmem(2, 10, 64, 128), vmem(8, 32, 128)],
        compiler_params=params(),
    )(*finest)

    teams = [[GROUP * i + j for j in range(GROUP)] for i in range(xy // GROUP)]
    chunks = lax.all_to_all(chunks, "xy", 0, 0, axis_index_groups=teams, tiled=True)
    window = chunks.reshape(4 * GROUP, 16, 128)
    before, after = pair(window[-13:], window[:13], "xy", GROUP)
    window = jnp.concatenate([before, window, after], axis=0)

    def faces(up):
        parts = []
        for rows, planes in FACES:
            part = window[rows.start : rows.stop, 16 - planes :] if up else window[rows.start : rows.stop, :planes]
            parts.append(part.reshape(-1, 128))
        return jnp.concatenate(parts + [jnp.zeros((8, 128), F32)], axis=0)

    before, after = pair(faces(True), faces(False), "gz")
    rims = pair(last_rows, first_rows, "xy")
    before, after, value_before, value_after = lax.optimization_barrier((before, after, *rims))
    chunks, halo, kept, below1 = pl.pallas_call(
        middle_down,
        out_shape=[shape(xy // GROUP, 8, 128), shape(40, 128), shape(20, 48, 128), shape(10, 24, 128)],
        in_specs=[smem] + [block] * 3,
        scratch_shapes=[vmem(44, 48, 128)]
        + [vmem(44, 24, 128)] * 2
        + [vmem(KEPT, 22, 24, 128), vmem(2, 22, 24, 128), vmem(34, 32, 128)]
        + [vmem(20, 24, 128)] * 2
        + [vmem(KEPT, 10, 24, 128), vmem(2, 10, 24, 128)],
        compiler_params=params(),
    )(place, window, before, after)

    peers = [[GROUP * i + j for i in range(xy // GROUP)] for j in range(GROUP)]
    chunks = lax.all_to_all(chunks, "xy", 0, 0, axis_index_groups=peers, tiled=True)
    before, after = pair(halo, halo, "xy", GROUP)
    halo = jnp.concatenate([before, halo, after], axis=0)
    layer = chunks[:, :4].reshape(1, xy, 128)
    everywhere = lax.all_to_all(jnp.broadcast_to(layer, (gz, xy, 128)), "gz", 0, 0, tiled=True)
    before, after = pair(halo, halo, "gz")
    halo = jnp.concatenate([part.reshape(15, 8, 128) for part in (before, halo, after)], axis=1)
    planes = 4 * gz
    return pl.pallas_call(
        partial(way_up, xy),
        out_shape=[shape(32, 8, 128)] * 2,
        in_specs=[smem] + [block] * 11,
        scratch_shapes=[vmem(planes + 4, 8, 128)] * 2
        + [vmem(KEPT, planes // 2 + 2, 8, 128), vmem(2, planes // 2 + 2, 8, 128), vmem(planes + 8, 8, 128)]
        + [vmem(22, 24, 128)] * 2
        + [vmem(KEPT, 11, 24, 128), vmem(2, 11, 24, 128)]
        + [vmem(20, 24, 128)] * 2
        + [vmem(KEPT, 10, 24, 128), vmem(2, 10, 24, 128)]
        + [vmem(20, 64, 128)] * 2
        + [vmem(KEPT, 10, 64, 128), vmem(2, 10, 64, 128), vmem(10, 64, 128)],
        compiler_params=params(),
    )(place, everywhere, halo, kept, below1, *finest, below0, value_before, value_after)


def solution(mesh):
    return jax.shard_map(
        body,
        mesh=mesh,
        in_specs=(P("gz", "xy", None), P("gz", "xy", None)),
        out_specs=(P("gz", "xy", None), P("gz", "xy", None)),
        check_vma=False,
    )
```
